256 devices in a mesh: head: 64 (over z_hi, x, y, core), mb: 4 (over z_lo).
Axes of the slice: x: 4, y: 4, z: 8 (z_hi: 2, z_lo: 4; z = z_hi * 4 + z_lo), core: 2. Of those that a mesh axis runs over, the one named last changes fastest.
Arguments:
- arrivals: bfloat16 [4, 64, 128, 4096], P('mb', 'head'), may hold values from -6 to 6
- owners: int32 [4], P('mb'), may hold values from 0 to 63
- doc_lengths: int32 [4, 4], P('mb'), may hold values from 1 to 64, 128 in all within a row
- w_in: bfloat16 [4096, 2, 8192], P(None, None, 'head'), may hold values from -0.09375 to 0.09375
- w_bc: bfloat16 [2048, 4096], P('head'), may hold values from -0.09375 to 0.09375
- w_dt: bfloat16 [128, 4096], P('head'), may hold values from -0.09375 to 0.09375
- conv_x: float32 [4, 8192], P(None, 'head'), may hold values from -3 to 3
- conv_bc: float32 [4, 2048], P(None, 'head'), may hold values from -3 to 3
- dt_bias: float32 [128], P('head'), may hold values from -3 to -1
- a_log: float32 [128], P('head'), may hold values from -3.2 to -0.9
- skip_scale: float32 [128], P('head'), may hold values from 0.5 to 2
- norm_gain: float32 [8192], P('head'), may hold values from 0.1 to 1.9
- w_out: bfloat16 [8192, 4096], P('head'), may hold values from -0.0625 to 0.0625
- out_grad: bfloat16 [4, 128, 4096], P('mb', 'head'), may hold values from -6 to 6
Outputs:
- layer_out: bfloat16 [4, 128, 4096], P('mb', 'head')
- in_grad: bfloat16 [4, 128, 4096], P('mb', 'head')
- grad_w_in: bfloat16 [4096, 2, 8192], P('mb', None, 'head')
- grad_w_bc: bfloat16 [4096, 2048], P('mb', 'head')
- grad_w_dt: bfloat16 [4096, 128], P('mb', 'head')
- grad_w_out: bfloat16 [4096, 8192], P('mb', 'head')
The draws below stay inside these ranges and needn't reach their ends.
Inputs may be any that keep to these rules, and one draw needn't show every extreme that they name: `doc_lengths`: each row sums to 128; the longest document of each row has exactly 64 positions. owners[m] is an index along head.
All inputs are finite; a program needn't handle non-finite values.
Results may differ from the reference program's by a relative error of at most 0.014.
Values may be sent and summed in bfloat16 or wider, within the bound.
A program may use at most 64 MiB of HBM per device.

```python
import math
import jax
import jax.numpy as jnp
import numpy as np
from jax import lax

D = 4096
STATE = 128
G = 8
K = 4
L = 128
DOCS = 4
H = 128
DI = 8192
CG = 1024
MICRO = 4
DOC_MOST = 64
N_HEAD = 64


def touch_ends(values, rng, smallest, high):
    shape = values.shape
    index_at = [jax.random.randint(jax.random.fold_in(rng, axis), (), 0, shape[axis]) for axis in range(len(shape))]
    values = values.at[tuple(index_at)].set(smallest)
    longest = shape.index(max(shape))
    index_at[longest] = (index_at[longest] + 1) % shape[longest]
    return values.at[tuple(index_at)].set(high)


def block_levels(rng, dims, pieces, least, high):
    gain, own = 1.0, jax.random.fold_in(rng, 6)
    for axis_at, shards_of in pieces:
        heights = jnp.exp(jax.random.uniform(jax.random.fold_in(own, axis_at), (shards_of,), jnp.float32, least / len(pieces), high / len(pieces)))
        gain = gain * jnp.repeat(heights, dims[axis_at] // shards_of).reshape([-1 if axis == axis_at else 1 for axis in range(len(dims))])
    return gain


def split_up(amount, total, limit, slope):
    portions = [(1 << 20) // math.isqrt(rank ** slope) + 1 for rank in range(2, amount + 1)]
    spare, holding = total - limit - (amount - 1), [1] * (amount - 1)
    while spare > 0:
        free = [i for i in range(amount - 1) if holding[i] < limit]
        whole, left = sum([portions[i] for i in free]), spare
        for i in free:
            addition = min(limit - holding[i], max(1, left * portions[i] // whole), spare)
            holding[i] = holding[i] + addition
            spare = spare - addition
    return np.array([limit] + holding)


def ragged(own_key, number_of, total, limit, skew):
    if number_of == 2:
        one = jax.random.randint(own_key, (), max(1, total - limit), min(limit, total - 1) + 1)
        return jnp.stack([one, total - one])
    sizes = jnp.asarray(split_up(number_of, total, limit, skew), jnp.int32)
    couples = (number_of - 1) // 2
    giver, receiver = sizes[1:1 + 2 * couples:2], sizes[2:2 + 2 * couples:2]
    room = jnp.minimum(giver - 1, limit - receiver)
    passed = jax.random.randint(jax.random.fold_in(own_key, 1), (couples,), 0, 1 << 20) % (room + 1)
    sizes = sizes.at[1:1 + 2 * couples:2].set(giver - passed).at[2:2 + 2 * couples:2].set(receiver + passed)
    return sizes[jax.random.permutation(jax.random.fold_in(own_key, 2), number_of)]


def noise(own_key, shape, scale, most, split=(), held_as=jnp.bfloat16):
    drawn = scale * jax.random.normal(own_key, shape, jnp.float32)
    if split:
        drawn = drawn * block_levels(own_key, shape, split, -0.22, 0.18)
    return jnp.clip(drawn, -most, most).astype(held_as)


def setup_inputs(seed: int = 0) -> dict:
    key_list = jax.random.split(jax.random.key(seed), 15)
    arrivals = noise(key_list[0], (MICRO, N_HEAD, L, D), 1.0, 6.0, ((0, 4), (1, 64)))
    owners = touch_ends(jax.random.randint(key_list[1], (MICRO,), 0, N_HEAD), jax.random.fold_in(key_list[1], 1), 0, N_HEAD - 1).astype(jnp.int32)
    doc_lengths = jax.vmap(lambda own: ragged(own, DOCS, L, DOC_MOST, 1))(jax.random.split(key_list[2], MICRO)).reshape((MICRO, DOCS)).astype(jnp.int32)
    w_in = noise(key_list[3], (D, 2, DI), D ** -0.5, 0.09375, ((2, 64),))
    w_bc = noise(key_list[4], (2 * G * STATE, D), D ** -0.5, 0.09375, ((0, 64),))
    w_dt = noise(key_list[5], (H, D), D ** -0.5, 0.09375, ((0, 64),))
    conv_x = noise(key_list[6], (K, DI), K ** -0.5, 3.0, ((1, 64),), jnp.float32)
    conv_bc = noise(key_list[7], (K, 2 * G * STATE), K ** -0.5, 3.0, ((1, 64),), jnp.float32)
    dt_bias = jnp.clip(-3.0 + 2.0 * jax.random.uniform(key_list[8], (H,), jnp.float32) ** block_levels(key_list[8], (H,), ((0, 64),), -0.2, 0.2), -3.0, -1.0)
    a_log = jnp.clip(-3.2 + 2.3000001 * jax.random.uniform(key_list[9], (H,), jnp.float32) ** block_levels(key_list[9], (H,), ((0, 64),), -0.2, 0.2), -3.2, -0.9)
    skip_scale = jnp.clip(0.5 + 1.5 * jax.random.uniform(key_list[10], (H,), jnp.float32) ** block_levels(key_list[10], (H,), ((0, 64),), -0.2, 0.2), 0.5, 2.0)
    norm_gain = jnp.clip(1.0 + 0.18 * jax.random.normal(key_list[11], (DI,), jnp.float32), 0.1, 1.9)
    w_out = noise(key_list[12], (DI, D), DI ** -0.5, 0.0625, ((0, 64),))
    out_grad = noise(key_list[13], (MICRO, L, D), 1.0, 6.0, ((0, 4), (1, 64)))
    return {"arrivals": arrivals, "owners": owners, "doc_lengths": doc_lengths, "w_in": w_in, "w_bc": w_bc, "w_dt": w_dt, "conv_x": conv_x, "conv_bc": conv_bc, "dt_bias": dt_bias, "a_log": a_log, "skip_scale": skip_scale, "norm_gain": norm_gain, "w_out": w_out, "out_grad": out_grad}


epsilon = 1e-05
highest = lax.Precision.HIGHEST

def doc_index(doc_lengths, length):
    ends = jnp.cumsum(doc_lengths, dtype=jnp.int32)
    places = jnp.arange(length, dtype=jnp.int32)
    return lax.optimization_barrier(jnp.sum((places[:, None] >= ends[None, :]).astype(jnp.int32), axis=1, dtype=jnp.int32))

def conv_reset(values, kernel, doc_ids):
    taps = kernel.shape[0]
    result = values * kernel[taps - 1][None, :]
    for offset in range(1, taps):
        shifted = jnp.concatenate([jnp.zeros((offset, values.shape[1]), values.dtype), values[:-offset]], axis=0)
        same_doc = jnp.concatenate([jnp.zeros((offset,), jnp.bool_), doc_ids[offset:] == doc_ids[:-offset]])
        result = result + jnp.where(same_doc[:, None], shifted, jnp.zeros_like(shifted)) * kernel[taps - 1 - offset][None, :]
    return result

def state_mix(per_head, step_size, rates, b_heads, c_heads, doc_ids):
    length = per_head.shape[0]
    cumulative = jnp.cumsum(step_size * rates[None, :], axis=0)
    places = jnp.arange(length, dtype=jnp.int32)
    visible = (places[:, None] >= places[None, :]) & (doc_ids[:, None] == doc_ids[None, :])
    log_gaps = cumulative.T[:, :, None] - cumulative.T[:, None, :]
    safe_gaps = jnp.where(visible[None], log_gaps, jnp.zeros_like(log_gaps))
    decays = jnp.where(visible[None], jnp.exp(safe_gaps), jnp.zeros_like(log_gaps))
    scores = jnp.einsum('thn,shn->hts', c_heads, b_heads, precision=highest)
    inputs_scaled = per_head * step_size[:, :, None]
    return jnp.einsum('hts,shp->thp', scores * decays, inputs_scaled, precision=highest)

def head_part(projected, b_heads, c_heads, dt_raw, conv_x, dt_bias, a_log, skip_scale, doc_ids):
    length = projected.shape[0]
    channels = projected.shape[1] // 2
    head_count = dt_raw.shape[1]
    conv_out = jax.nn.silu(conv_reset(projected[:, :channels], conv_x, doc_ids))
    step_size = jax.nn.softplus(dt_raw + dt_bias[None, :])
    rates = -jnp.exp(a_log)
    per_head = conv_out.reshape(length, head_count, channels // head_count)
    mixed_state = state_mix(per_head, step_size, rates, b_heads, c_heads, doc_ids) + skip_scale[None, :, None] * per_head
    return mixed_state.reshape(length, channels) * jax.nn.silu(projected[:, channels:])

def rounded(values):
    return lax.optimization_barrier(values.astype(jnp.bfloat16)).astype(jnp.float32)

def reference(arrivals, owners, doc_lengths, w_in, w_bc, w_dt, conv_x, conv_bc, dt_bias, a_log, skip_scale, norm_gain, w_out, out_grad):
    w_flat = w_in.reshape(D, 2 * DI)
    spread = G * STATE
    per_group = H // G
    contract = (((1,), (1,)), ((), ()))
    columns = (((0,), (0,)), ((), ()))
    inputs_all = arrivals[jnp.arange(MICRO), owners]

    def one_batch(totals, batch):
        features, lengths_row, grad_rows = batch
        doc_ids = doc_index(lengths_row, L)
        projected = jnp.dot(features, w_flat, preferred_element_type=jnp.float32)
        state_pre = lax.dot_general(features, w_bc, contract, preferred_element_type=jnp.float32)
        dt_raw = lax.dot_general(features, w_dt, contract, preferred_element_type=jnp.float32)
        state_act = jax.nn.silu(conv_reset(state_pre, conv_bc, doc_ids))
        state_delta = rounded(state_act) - state_act

        def core(proj_in, pre_in, raw_in):
            state_in = jax.nn.silu(conv_reset(pre_in, conv_bc, doc_ids)) + state_delta
            b_heads = jnp.repeat(state_in[:, :spread].reshape(L, G, STATE), per_group, axis=1)
            c_heads = jnp.repeat(state_in[:, spread:].reshape(L, G, STATE), per_group, axis=1)
            gated = head_part(proj_in, b_heads, c_heads, raw_in, conv_x, dt_bias, a_log, skip_scale, doc_ids)
            grouped = gated.reshape(L, G, CG)
            inverse = lax.rsqrt(lax.optimization_barrier(jnp.mean(grouped * grouped, axis=2)) + epsilon)
            return (grouped * inverse[:, :, None]).reshape(L, DI) * norm_gain[None, :]
        normed_full, core_back = jax.vjp(core, projected, state_pre, dt_raw)
        normed = normed_full.astype(jnp.bfloat16)
        layer_out = jnp.dot(normed, w_out, preferred_element_type=jnp.float32).astype(jnp.bfloat16)
        d_normed = lax.dot_general(grad_rows, w_out, contract, preferred_element_type=jnp.float32)
        d_proj, d_pre, d_raw = core_back(d_normed)
        d_proj = d_proj.astype(jnp.bfloat16)
        d_pre = d_pre.astype(jnp.bfloat16)
        d_raw = d_raw.astype(jnp.bfloat16)
        in_grad = lax.dot_general(d_proj, w_flat, contract, preferred_element_type=jnp.float32)
        in_grad = in_grad + jnp.dot(d_pre, w_bc, preferred_element_type=jnp.float32)
        in_grad = (in_grad + jnp.dot(d_raw, w_dt, preferred_element_type=jnp.float32)).astype(jnp.bfloat16)
        grads = (lax.dot_general(features, d_proj, columns, preferred_element_type=jnp.float32), lax.dot_general(features, d_pre, columns, preferred_element_type=jnp.float32), lax.dot_general(features, d_raw, columns, preferred_element_type=jnp.float32), lax.dot_general(grad_rows, normed, columns, preferred_element_type=jnp.float32))
        totals = tuple((total + rounded(grad) for total, grad in zip(totals, grads)))
        return (totals, (layer_out, in_grad))
    initial = (jnp.zeros((D, 2 * DI), jnp.float32), jnp.zeros((D, 2 * spread), jnp.float32), jnp.zeros((D, H), jnp.float32), jnp.zeros((D, DI), jnp.float32))
    totals, outputs = lax.scan(one_batch, initial, (inputs_all, doc_lengths, out_grad))
    layer_out, in_grad = outputs
    return (layer_out, in_grad, totals[0].reshape(D, 2, DI).astype(jnp.bfloat16), totals[1].astype(jnp.bfloat16), totals[2].astype(jnp.bfloat16), totals[3].astype(jnp.bfloat16))
```

```python
import jax
import jax.numpy as jnp
from jax import lax
from jax.experimental import pallas as pl
from jax.experimental.pallas import tpu as pltpu
from jax.sharding import PartitionSpec as P

T = 128
EPS = 1e-05
WIDTH = 1024
HI = lax.Precision.HIGHEST
MESH = pl.DeviceIdType.MESH
BF = jnp.bfloat16
F32 = jnp.float32


def sigmoid(v):
    return 1.0 / (1.0 + jnp.exp(-v))


def hdot(a, b, dims):
    return lax.dot_general(a, b, (dims, ((), ())), precision=HI, preferred_element_type=F32)


def bdot(a, b, dims):
    return lax.dot_general(a, b, (dims, ((), ())), preferred_element_type=F32)


NN = ((1,), (0,))
NT = ((1,), (1,))
TN = ((0,), (0,))


class Ids:
    def __init__(self):
        self.used = 0

    def take(self, count):
        first = self.used
        self.used += count
        return first


def staged(last):
    return dict(
        p=pltpu.VMEM((4, 4, 2, 2, 4, 16, 128), BF),
        r1=pltpu.VMEM((4, 4, 2, 4, 16, 128), BF),
        q=pltpu.VMEM((4, 4, 2, 4, 16, 128), BF),
        r2x=pltpu.VMEM((3, 2, 4, 2, 16, 128), BF),
        r2y=pltpu.VMEM((3, 2, 2, 4, 16, 128), BF),
        qx=pltpu.VMEM((2, 4, 2, 16, 128), BF),
        qy=pltpu.VMEM((2, 2, 4, 16, 128), BF),
        r3x=pltpu.VMEM((3, 2, 2, 16, 128), BF),
        r3y=pltpu.VMEM((3, 2, 2, 16, 128), BF),
        t=pltpu.VMEM((4, 2, 16, 128), BF),
        r4=pltpu.VMEM(last, BF),
    )


def rows_trade():
    return dict(
        v=pltpu.VMEM((64, 128), F32), g=pltpu.VMEM((64, 128), F32), r=pltpu.VMEM((64, 128), F32)
    )


N_SEM = 240

SCRATCH = dict(
    arr=pltpu.VMEM((T, 4096), BF),
    win=pltpu.VMEM((8192, 128), BF),
    wf=pltpu.VMEM((2, 512, 128), F32),
    wxz=pltpu.VMEM((4096, 256), BF),
    w2=pltpu.VMEM((128, 4096), BF),
    wdtf=pltpu.VMEM((16, 4096), F32),
    wout=pltpu.VMEM((128, 4096), BF),
    cbc=pltpu.VMEM((8, 128), F32),
    ax=pltpu.VMEM((7, 4, 2, 2, 4, 16, 128), BF),
    ao=pltpu.VMEM((7, 4, 2, 2, 4, 16, 128), BF),
    x=pltpu.VMEM((T, 4096), BF),
    o=pltpu.VMEM((T, 4096), BF),
    ss=pltpu.VMEM((32, 128), BF),
    bc=pltpu.VMEM((8, 32, 128), BF),
    norm=pltpu.VMEM((8, 8, 128), F32),
    dbcs=pltpu.VMEM((8, 32, 128), F32),
    dbcr=pltpu.VMEM((8, 32, 128), F32),
    dx=pltpu.VMEM((4, 128, 128), BF),
    dz=pltpu.VMEM((4, 128, 128), BF),
    nm=pltpu.VMEM((4, 128, 128), BF),
    d2=pltpu.VMEM((4, 48, 128), BF),
    gf=pltpu.VMEM((2, 256, 128), F32),
    sx=staged((4, 2, 16, 128)),
    slo=staged((4, 16, 128)),
    sig=staged((4, 16, 128)),
    tog=rows_trade(),
    tlo=rows_trade(),
    tig=rows_trade(),
    ssem=pltpu.SemaphoreType.DMA((N_SEM,)),
    rsem=pltpu.SemaphoreType.DMA((N_SEM,)),
    lsem=pltpu.SemaphoreType.DMA((8,)),
)


def mixer_kernel(
    own_ref, doc_ref, dtb_ref, alog_ref, skip_ref, cx_ref, cbc_ref, gain_ref, wdt_ref, og_ref,
    arr_hbm, win_hbm, wbc_hbm, wout_hbm,
    lo_out, ig_out, gin_out, gbc_out, gdt_out, go_out,
    s,
):
    h = lax.axis_index("head")
    m = lax.axis_index("mb")
    zh = h // 32
    x = (h // 8) % 4
    y = (h // 2) % 4
    c = h % 2
    j = h % 8
    g = h // 8
    g_t = (h % 32) // 4
    part = zh * 4 + h % 4
    ssem, rsem, lsem = s["ssem"], s["rsem"], s["lsem"]
    ids = Ids()
    sent = []

    def head_of(zh_, x_, y_, c_):
        return zh_ * 32 + x_ * 8 + y_ * 2 + c_

    def copy(src, dst, i, head, mb, r=None):
        return pltpu.make_async_remote_copy(
            src_ref=src, dst_ref=dst, send_sem=ssem.at[i], recv_sem=rsem.at[i if r is None else r],
            device_id=(head, mb), device_id_type=MESH,
        )

    def start(cp):
        cp.start()
        sent.append(cp)
        return cp

    loc = [
        pltpu.make_async_copy(arr_hbm, s["arr"], lsem.at[0]),
        pltpu.make_async_copy(win_hbm, s["win"], lsem.at[1]),
        pltpu.make_async_copy(wbc_hbm, s["w2"].at[0:32], lsem.at[2]),
        pltpu.make_async_copy(wout_hbm, s["wout"], lsem.at[3]),
    ]
    for cp in loc:
        cp.start()

    barrier = pltpu.get_barrier_semaphore()
    count = 0
    peers = [(head_of(zh, x, y, 1 - c), m), (head_of(1 - zh, x, y, c), m)]
    for d in range(1, 4):
        peers.append((head_of(zh, (x + d) % 4, y, c), m))
        peers.append((h, (m + d) % 4))
    for d in range(1, 8):
        peers.append((8 * g + (j + d) % 8, m))
    for head, mb in peers:
        pl.semaphore_signal(barrier, inc=1, device_id=(head, mb), device_id_type=MESH)
        count += 1
    own_parts = [4 * g + k for k in range(4)] + [32 + 4 * g + k for k in range(4)]
    targets = [8 * g_t + k for k in range(8)]
    for head in own_parts + targets:
        pl.semaphore_signal(barrier, inc=1, device_id=(head, m), device_id_type=MESH)
        count += 1

    s["cbc"][...] = jnp.zeros((8, 128), F32)
    s["cbc"][0:4, 0:32] = cbc_ref[...]
    s["wdtf"][...] = jnp.zeros((16, 4096), F32)
    s["wdtf"][0:2, :] = wdt_ref[...].astype(F32)
    s["w2"][32:48, :] = s["wdtf"][...].astype(BF)
    s["w2"][48:128, :] = jnp.zeros((80, 4096), BF)

    sx = s["sx"]
    loc[0].wait()

    def split_arr(i, _):
        v = s["arr"][:, pl.ds(pl.multiple_of(i * 256, 256), 256)]
        for cc in range(2):
            sx["p"][i // 4, i % 4, cc] = v[:, cc * 128:(cc + 1) * 128].reshape(2, 4, 16, 128)
        return 0

    lax.fori_loop(0, 16, split_arr, 0)
    pl.semaphore_wait(barrier, count)

    owner = own_ref[0]
    o_zh, o_x, o_y, o_c = owner // 32, (owner // 8) % 4, (owner // 2) % 4, owner % 2

    def combine(own, received, picks):
        if picks is None:
            total = own.astype(F32)
            for v in received:
                total = total + v.astype(F32)
            return total
        value = own
        for v, pick in zip(received, picks):
            value = lax.select(pick, v, value)
        return value

    def stage1_copy(b, i):
        return copy(b["p"].at[:, :, 1 - c], b["r1"], i, head_of(zh, x, y, 1 - c), m)

    def stage1_merge(b, picks):
        def one(q, _):
            b["q"][q] = combine(b["p"][q, :, c], [b["r1"][q]], picks and picks["c"]).astype(BF)
            return 0
        lax.fori_loop(0, 4, one, 0)

    def stage2_copies(b, i):
        cps = []
        for d in range(1, 4):
            x2, y2 = (x + d) % 4, (y + d) % 4
            cps.append(copy(b["q"].at[0:2, :, :, x2], b["r2x"].at[d - 1], i + 2 * d - 2, head_of(zh, x2, y, c), m))
            cps.append(copy(b["q"].at[2:4, y2], b["r2y"].at[d - 1], i + 2 * d - 1, head_of(zh, x, y2, c), m))
        return cps

    def stage2_merge(b, picks):
        for q in range(2):
            b["qx"][q] = combine(b["q"][q, :, :, x], [b["r2x"][d, q] for d in range(3)], picks and picks["x"]).astype(BF)
            b["qy"][q] = combine(b["q"][2 + q, y], [b["r2y"][d, q] for d in range(3)], picks and picks["y"]).astype(BF)

    def stage3_copies(b, i):
        cps = []
        for d in range(1, 4):
            x2, y2 = (x + d) % 4, (y + d) % 4
            cps.append(copy(b["qx"].at[:, y2], b["r3x"].at[d - 1], i + 2 * d - 2, head_of(zh, x, y2, c), m))
            cps.append(copy(b["qy"].at[:, :, x2], b["r3y"].at[d - 1], i + 2 * d - 1, head_of(zh, x2, y, c), m))
        return cps

    def stage3_merge(b, picks):
        b["t"][0:2] = combine(b["qx"][:, y], [b["r3x"][d] for d in range(3)], picks and picks["y"]).astype(BF)
        b["t"][2:4] = combine(b["qy"][:, :, x], [b["r3y"][d] for d in range(3)], picks and picks["x"]).astype(BF)

    other_zh = head_of(1 - zh, x, y, c)

    def gather1(a, s1, s2, i):
        cps = []
        for d in range(1, 4):
            x2, y2 = (x + d) % 4, (y + d) % 4
            r1, r2 = a.at[s1, y, c, :, x], a.at[s2, y, c, :, x]
            cps.append(copy(r1, r1, i + 2 * d - 2, head_of(zh, x, y2, c), m))
            cps.append(copy(r2, r2, i + 2 * d - 1, head_of(zh, x2, y, c), m))
        return cps

    def gather2(a, s1, s2, i):
        cps = []
        for d in range(1, 4):
            x2, y2 = (x + d) % 4, (y + d) % 4
            r1, r2 = a.at[s1, :, c, :, x], a.at[s2, y, c]
            cps.append(copy(r1, r1, i + 2 * d - 2, head_of(zh, x2, y, c), m))
            cps.append(copy(r2, r2, i + 2 * d - 1, head_of(zh, x, y2, c), m))
        return cps

    def gather3(a, part_of, i):
        ref = a.at[part_of, :, c]
        return [copy(ref, ref, i, head_of(zh, x, y, 1 - c), m)]

    def go(cps):
        for cp in cps:
            start(cp)
        return cps

    def got(cps):
        for cp in cps:
            cp.wait_recv()

    def trade(b, i):
        cps = []
        for d in range(1, 8):
            k = (j + d) % 8
            src = b["g"].at[pl.ds(pl.multiple_of(k * 8, 8), 8)]
            dst = b["r"].at[pl.ds(pl.multiple_of(j * 8, 8), 8)]
            cps.append(copy(src, dst, i + d - 1, 8 * g + k, m))
        mine = pl.ds(pl.multiple_of(j * 8, 8), 8)
        b["r"][mine, :] = b["g"][mine, :]
        return cps

    lane = lax.broadcasted_iota(jnp.int32, (T, 128), 1)
    row = lax.broadcasted_iota(jnp.int32, (T, 128), 0)

    def unpack_weights(first, last):
        def one(i, _):
            k = i % 2
            s["wf"][k] = s["win"][pl.ds(pl.multiple_of(i * 512, 512), 512), :].astype(F32)
            at = pl.ds(pl.multiple_of(i * 256, 256), 256)
            s["wxz"][at, 0:128] = s["wf"][k, pl.ds(0, 256, stride=2), :].astype(BF)
            s["wxz"][at, 128:256] = s["wf"][k, pl.ds(1, 256, stride=2), :].astype(BF)
            return 0
        lax.fori_loop(first, last, one, 0)

    picks = dict(
        c=[o_c != c],
        x=[o_x == (x + 4 - d) % 4 for d in range(1, 4)],
        y=[o_y == (y + 4 - d) % 4 for d in range(1, 4)],
    )
    a_x, a_o = s["ax"], s["ao"]
    x1 = go([stage1_copy(sx, ids.take(1))])
    tog = s["tog"]
    og = og_ref[...].astype(F32)
    for k in range(8):
        for q in range(4):
            tog["g"][k * 8 + q * 2:k * 8 + q * 2 + 2, :] = og[:, q * 1024 + k * 128:q * 1024 + k * 128 + 128]
    o1 = go(trade(tog, ids.take(7)))
    got(x1)
    stage1_merge(sx, picks)
    x2 = go(stage2_copies(sx, ids.take(6)))
    got(o1)
    for q in range(4):
        for tt in range(2):
            tog["v"][pl.ds(q * 16 + tt, 8, stride=2), :] = tog["r"][pl.ds(q * 2 + tt, 8, stride=8), :]
    a_o[0:4, y, c, zh, x] = tog["v"][...].reshape(4, 16, 128).astype(BF)
    cps = []
    i0 = ids.take(3)
    for d in range(1, 4):
        m2 = (m + d) % 4
        cps.append(copy(a_o.at[m2, y, c, zh, x], a_o.at[7 - d, y, c, zh, x], i0 + d - 1, h, m2))
    oc = go(cps)
    oz_ref = a_o.at[0:4, y, c, zh, x]
    oz = go([copy(oz_ref, oz_ref, ids.take(1), other_zh, m)])
    loc[1].wait()
    unpack_weights(0, 3)
    got(x2)
    stage2_merge(sx, picks)
    x3 = go(stage3_copies(sx, ids.take(6)))
    got(oz)
    q01, q23 = slice(0, 2), slice(2, 4)
    og1 = go(gather1(a_o, q01, q23, ids.take(6)))
    unpack_weights(3, 6)
    got(x3)
    stage3_merge(sx, picks)
    x4 = go([copy(sx["t"], sx["r4"], ids.take(1), other_zh, m)])
    got(oc)
    ocz_ref = a_o.at[4:7, y, c, zh, x]
    ocz = go([copy(ocz_ref, ocz_ref, ids.take(1), other_zh, m)])
    got(og1)
    unpack_weights(6, 9)
    got(x4)
    a_x[0:4, y, c, :, x] = combine(sx["t"][...], [sx["r4"][...]], [o_zh != zh])
    xg1 = go(gather1(a_x, q01, q23, ids.take(6)))
    i0 = ids.take(3)
    cps = []
    for d in range(1, 4):
        m2 = (m + d) % 4
        cps.append(copy(a_x.at[m2, y, c, :, x], a_x.at[7 - d, y, c, :, x], i0 + d - 1, h, m2))
    xc = go(cps)
    og2 = go(gather2(a_o, q01, q23, ids.take(6)))
    unpack_weights(9, 12)
    got(xg1)
    xg2 = go(gather2(a_x, q01, q23, ids.take(6)))
    unpack_weights(12, 16)
    got(og2)
    got(xg2)
    xg3 = go(gather3(a_x, slice(0, 4), ids.take(1)))
    og3 = go(gather3(a_o, slice(0, 4), ids.take(1)))

    def assemble(a, dst, cc):
        def one(i, _):
            at = pl.ds(pl.multiple_of(i * 256 + cc * 128, 128), 128)
            dst[:, at] = a[i // 4, i % 4, cc].reshape(128, 128)
            return 0
        lax.fori_loop(0, 16, one, 0)

    assemble(a_x, s["x"], c)
    loc[2].wait()
    got(xg3)
    assemble(a_x, s["x"], 1 - c)

    e1 = doc_ref[0, 0]
    e2 = e1 + doc_ref[0, 1]
    e3 = e2 + doc_ref[0, 2]
    e4 = e3 + doc_ref[0, 3]

    def doc_of(t):
        return sum((t >= e).astype(jnp.int32) for e in (e1, e2, e3, e4))

    doc_row = doc_of(row)
    same = [None] + [(row >= o) & (doc_of(row - o) == doc_row) for o in range(1, 4)]
    visible = (row >= lane) & (doc_row == doc_of(lane))

    def conv(v, taps):
        result = v * taps[3:4]
        for o in range(1, 4):
            result = result + jnp.where(same[o], pltpu.roll(v, o, 0), 0.0) * taps[3 - o:4 - o]
        return result

    def conv_back(d, taps):
        result = d * taps[3:4]
        for o in range(1, 4):
            result = result + pltpu.roll(jnp.where(same[o], d, 0.0), T - o, 0) * taps[3 - o:4 - o]
        return result

    p2 = bdot(s["x"][...], s["w2"][...], NT)
    taps_bc = s["cbc"][...]
    bc_pre = conv(p2, taps_bc)
    bc_sig = sigmoid(bc_pre)
    s["ss"][...] = jnp.transpose(bc_pre * bc_sig)[0:32].astype(BF)
    i_bc = ids.take(8)
    for k in range(8):
        head = 8 * g_t + k

        @pl.when(head != h)
        def _():
            copy(s["ss"], s["bc"].at[part], i_bc + k, head, m, i_bc + part).start()

        @pl.when(head == h)
        def _():
            pltpu.make_async_copy(s["ss"], s["bc"].at[part], rsem.at[i_bc + part]).start()

    pxz = bdot(s["x"][...], s["wxz"][...], NN)
    z = pxz[:, 128:256]
    taps_x = cx_ref[...]
    x_pre = conv(pxz[:, 0:128], taps_x)
    x_sig = sigmoid(x_pre)
    x_conv = x_pre * x_sig
    z_sig = sigmoid(z)
    z_silu = z * z_sig
    low = lane < 64
    tri = jnp.where(row >= lane, 1.0, 0.0)
    raws, rates, steps = [], [], []
    for e in range(2):
        raw = jnp.broadcast_to(p2[:, 32 + e:33 + e], (T, 128)) + dtb_ref[e]
        raws.append(raw)
        rates.append(-jnp.exp(jnp.full((T, 128), alog_ref[e], F32)))
        steps.append(jnp.maximum(raw, 0.0) + jnp.log1p(jnp.exp(-jnp.abs(raw))))
    step = jnp.where(low, steps[0], steps[1])
    cum = hdot(tri, jnp.where(low, steps[0] * rates[0], steps[1] * rates[1]), NN)
    decays = []
    for e in range(2):
        col = jnp.broadcast_to(cum[:, 64 * e:64 * e + 1], (T, 128))
        gap = col - jnp.transpose(col)
        decays.append(jnp.where(visible, jnp.exp(jnp.where(visible, gap, 0.0)), 0.0))
    scaled = x_conv * step
    skip = jnp.where(low, skip_ref[0], skip_ref[1])

    assemble(a_o, s["o"], c)
    got(og3)
    assemble(a_o, s["o"], 1 - c)
    loc[3].wait()
    weighted = bdot(s["o"][...], s["wout"][...], NT) * gain_ref[...]

    got(xc)
    k1, k2 = slice(4, 5), slice(5, 7)
    cxg1 = go(gather1(a_x, k1, k2, ids.take(6)))
    got(ocz)
    l1, l2 = slice(4, 6), slice(6, 7)
    cog1 = go(gather1(a_o, l1, l2, ids.take(6)))

    for k in range(8):
        copy(s["ss"], s["bc"].at[k], i_bc + k, other_zh, m).wait_recv()
    b_t = s["bc"][0:4].reshape(128, 128)
    c_t = s["bc"][4:8].reshape(128, 128)
    scores = bdot(c_t, b_t, TN)
    mixes = [scores * decays[0], scores * decays[1]]
    zero = jnp.zeros((T, 128), F32)
    scaled2 = jnp.concatenate([jnp.where(low, scaled, zero), jnp.where(low, zero, scaled)], axis=0)
    state = hdot(jnp.concatenate(mixes, axis=1), scaled2, NN) + skip * x_conv
    gated = state * z_silu
    squares = jnp.sum(gated * gated, axis=1, keepdims=True)
    inners = jnp.sum(weighted * gated, axis=1, keepdims=True)
    nmat = jnp.where(lane == 0, squares, jnp.where(lane == 1, inners, 0.0))
    s["norm"][j] = jnp.transpose(nmat)[0:8]
    i_n = ids.take(7)
    ncp = []
    for d in range(1, 8):
        ncp.append(copy(s["norm"].at[j], s["norm"].at[j], i_n + d - 1, 8 * g + (j + d) % 8, m))
    go(ncp)
    got(cxg1)
    cxg2 = go(gather2(a_x, k1, k2, ids.take(6)))
    got(cog1)
    cog2 = go(gather2(a_o, l1, l2, ids.take(6)))
    got(ncp)
    total = jnp.sum(s["norm"][...], axis=0)
    tcol = jnp.transpose(jnp.concatenate([total, jnp.zeros((120, 128), F32)], axis=0))
    inverse = jnp.broadcast_to(lax.rsqrt(tcol[:, 0:1] * (1.0 / WIDTH) + EPS), (T, 128))
    inner = jnp.broadcast_to(tcol[:, 1:2] * (1.0 / WIDTH), (T, 128))
    normed = (gated * inverse * gain_ref[...]).astype(BF)
    s["nm"][0] = normed
    d_gated = inverse * weighted - gated * (inverse * inverse * inverse * inner)

    d_state = d_gated * z_silu
    d_z = d_gated * state * (z_sig * (1.0 + z * (1.0 - z_sig)))
    s["dz"][0] = d_z.astype(BF)
    dy0, dy1 = jnp.where(low, d_state, zero), jnp.where(low, zero, d_state)
    d_mix = [hdot(dy0, scaled, NT), hdot(dy1, scaled, NT)]
    d_scores = d_mix[0] * decays[0] + d_mix[1] * decays[1]
    s["dbcs"][0:4] = hdot(c_t.astype(F32), d_scores, NN).reshape(4, 32, 128)
    s["dbcs"][4:8] = hdot(b_t.astype(F32), d_scores, NT).reshape(4, 32, 128)
    i_d = ids.take(8)
    for k in range(8):
        head = own_parts[k]

        @pl.when(head != h)
        def _():
            copy(s["dbcs"].at[k], s["dbcr"].at[j], i_d + k, head, m, i_d + j).start()

        @pl.when(head == h)
        def _():
            pltpu.make_async_copy(s["dbcs"].at[k], s["dbcr"].at[j], rsem.at[i_d + j]).start()

    def to_mb(ref, i):
        cps = []
        for d in range(1, 4):
            cps.append(copy(ref.at[0], ref.at[4 - d], i + d - 1, h, (m + d) % 4))
        return go(cps)

    n_mb = to_mb(s["nm"], ids.take(3))
    z_mb = to_mb(s["dz"], ids.take(3))

    slo, sig = s["slo"], s["sig"]

    def lo_half(cc):
        def one(i, _):
            at = pl.ds(pl.multiple_of(i * 256 + cc * 128, 128), 128)
            v = bdot(normed, s["wout"][:, at], NN)
            slo["p"][i // 4, i % 4, cc] = v.astype(BF).reshape(2, 4, 16, 128)
            return 0
        lax.fori_loop(0, 16, one, 0)

    lo_half(1 - c)
    lo1 = go([stage1_copy(slo, ids.take(1))])
    lo_half(c)

    d_scaled = hdot(
        jnp.concatenate(mixes, axis=0), jnp.concatenate([dy0, dy1], axis=0), TN
    )
    d_xconv = skip * d_state + d_scaled * step
    d_x = conv_back(d_xconv * (x_sig * (1.0 + x_pre * (1.0 - x_sig))), taps_x)
    s["dx"][0] = d_x.astype(BF)
    x_mb = to_mb(s["dx"], ids.take(3))
    through = d_scaled * x_conv
    d_raws = []
    for e in range(2):
        mine = low if e == 0 else lane >= 64
        gap_grad = d_mix[e] * mixes[e]
        d_cum = jnp.sum(gap_grad - jnp.transpose(gap_grad), axis=1, keepdims=True)
        back = hdot(tri, jnp.broadcast_to(d_cum, (T, 128)), TN)
        d_step = jnp.sum(jnp.where(mine, through, 0.0), axis=1, keepdims=True) + rates[e] * back
        d_raws.append(d_step * sigmoid(raws[e]))

    got(cxg2)
    cxg3 = go(gather3(a_x, slice(4, 7), ids.take(1)))
    got(cog2)
    cog3 = go(gather3(a_o, slice(4, 7), ids.take(1)))

    for k in range(8):
        copy(s["dbcs"].at[k], s["dbcr"].at[k], i_d + k, other_zh, m).wait_recv()
    d_act = jnp.transpose(
        jnp.concatenate([jnp.sum(s["dbcr"][...], axis=0), jnp.zeros((96, 128), F32)], axis=0)
    )
    d_bc = conv_back(d_act * (bc_sig * (1.0 + bc_pre * (1.0 - bc_sig))), taps_bc)
    d2 = jnp.where(lane == 32, d_raws[0], jnp.where(lane == 33, d_raws[1], d_bc))
    d2_b = d2.astype(BF)
    s["d2"][0] = jnp.transpose(d2)[0:48].astype(BF)
    d2_mb = to_mb(s["d2"], ids.take(3))

    d_proj = jnp.concatenate([s["dx"][0], s["dz"][0]], axis=1)

    def ig_half(cc):
        def one(i, _):
            at = pl.ds(pl.multiple_of(i * 256 + cc * 128, 128), 128)
            v = bdot(d_proj, s["wxz"][at, :], NT) + bdot(d2_b, s["w2"][:, at], NN)
            sig["p"][i // 4, i % 4, cc] = v.astype(BF).reshape(2, 4, 16, 128)
            return 0
        lax.fori_loop(0, 16, one, 0)

    ig_half(1 - c)
    ig1 = go([stage1_copy(sig, ids.take(1))])
    ig_half(c)
    got(lo1)
    stage1_merge(slo, None)
    got(ig1)
    stage1_merge(sig, None)
    ig2 = go(stage2_copies(sig, ids.take(6)))
    lo2 = go(stage2_copies(slo, ids.take(6)))

    got(n_mb)
    got(cog3)
    nm_all = s["nm"][...].reshape(512, 128)

    def grad_out(i, _):
        yy, cc = i // 2, i % 2
        lhs = jnp.concatenate(
            [a_o[m, yy, cc].reshape(128, 128)] + [a_o[k, yy, cc].reshape(128, 128) for k in range(4, 7)], axis=0
        )
        go_out[pl.ds(pl.multiple_of(i * 128, 128), 128), :] = bdot(lhs, nm_all, TN).astype(BF)
        return 0

    lax.fori_loop(0, 8, grad_out, 0)

    def stage4(b, i):
        return go([copy(b["t"].at[:, 1 - zh], b["r4"], i, other_zh, m)])

    def stage5(b, t, i):
        t["v"][...] = (b["t"][:, zh].astype(F32) + b["r4"][...].astype(F32)).reshape(64, 128)
        for q in range(4):
            for tt in range(2):
                t["g"][pl.ds(q * 2 + tt, 8, stride=8), :] = t["v"][pl.ds(q * 16 + tt, 8, stride=2), :]
        return go(trade(t, i))

    def finish(t, out):
        for k in range(8):
            for q in range(4):
                at = q * 1024 + k * 128
                out[:, at:at + 128] = t["r"][k * 8 + q * 2:k * 8 + q * 2 + 2, :].astype(BF)

    got(ig2)
    stage2_merge(sig, None)
    ig3 = go(stage3_copies(sig, ids.take(6)))
    got(lo2)
    stage2_merge(slo, None)
    lo3 = go(stage3_copies(slo, ids.take(6)))
    got(x_mb)
    got(z_mb)
    got(d2_mb)
    got(cxg3)
    d_all = jnp.concatenate(
        [s["dx"][...].reshape(512, 128), s["dz"][...].reshape(512, 128)], axis=1
    )
    d2_all = jnp.concatenate([s["d2"][k] for k in range(4)], axis=1)

    def grad_in(i, _):
        yy, cc, k = i // 2, i % 2, i % 2
        lhs = jnp.concatenate(
            [a_x[m, yy, cc].reshape(128, 128)] + [a_x[k_, yy, cc].reshape(128, 128) for k_ in range(4, 7)], axis=0
        )
        r = bdot(lhs, d_all, TN)
        s["gf"][k, pl.ds(0, 128, stride=2), :] = r[:, 0:128]
        s["gf"][k, pl.ds(1, 128, stride=2), :] = r[:, 128:256]
        gin_out[pl.ds(pl.multiple_of(i * 256, 256), 256), :] = s["gf"][k].astype(BF)
        small = bdot(d2_all, lhs, NN)
        at = pl.ds(pl.multiple_of(i * 128, 128), 128)
        gbc_out[:, at] = small[0:32].astype(BF)
        gdt_out[:, at] = small[32:34].astype(BF)
        return 0

    lax.fori_loop(0, 4, grad_in, 0)
    got(ig3)
    stage3_merge(sig, None)
    ig4 = stage4(sig, ids.take(1))
    got(lo3)
    stage3_merge(slo, None)
    lo4 = stage4(slo, ids.take(1))
    lax.fori_loop(4, 8, grad_in, 0)
    got(ig4)
    ig5 = stage5(sig, s["tig"], ids.take(7))
    got(lo4)
    lo5 = stage5(slo, s["tlo"], ids.take(7))
    got(ig5)
    finish(s["tig"], ig_out)
    got(lo5)
    finish(s["tlo"], lo_out)

    for cp in sent:
        cp.wait_send()
    for k in range(8):
        @pl.when(8 * g_t + k != h)
        def _():
            copy(s["ss"], s["bc"].at[part], i_bc + k, 8 * g_t + k, m).wait_send()

        @pl.when(own_parts[k] != h)
        def _():
            copy(s["dbcs"].at[k], s["dbcr"].at[j], i_d + k, own_parts[k], m).wait_send()

    assert ids.used <= N_SEM


def per_device(
    arrivals, owners, doc_lengths, w_in, w_bc, w_dt, conv_x, conv_bc, dt_bias, a_log, skip_scale,
    norm_gain, w_out, out_grad,
):
    smem = pl.BlockSpec(memory_space=pltpu.SMEM)
    vmem = pl.BlockSpec(memory_space=pltpu.VMEM)
    hbm = pl.BlockSpec(memory_space=pl.ANY)
    sds = jax.ShapeDtypeStruct
    lo, ig, gin, gbc, gdt, gout = pl.pallas_call(
        mixer_kernel,
        out_shape=(
            sds((2, 4096), BF), sds((2, 4096), BF), sds((2048, 128), BF), sds((32, 1024), BF),
            sds((2, 1024), BF), sds((1024, 128), BF),
        ),
        in_specs=[smem] * 5 + [vmem] * 5 + [hbm] * 4,
        out_specs=(vmem,) * 6,
        scratch_shapes=[SCRATCH],
        compiler_params=pltpu.CompilerParams(
            collective_id=0, has_side_effects=True, vmem_limit_bytes=56 * 1024 * 1024
        ),
    )(
        owners, doc_lengths, dt_bias, a_log, skip_scale, conv_x, conv_bc,
        norm_gain.reshape(1, 128), w_dt, out_grad.reshape(2, 4096),
        arrivals.reshape(T, 4096), w_in.reshape(8192, 128), w_bc, w_out,
    )
    return (
        lo[None], ig[None], gin.reshape(1024, 2, 128), gbc.T, gdt.T, gout,
    )


def solution(mesh):
    return jax.shard_map(
        per_device,
        mesh=mesh,
        in_specs=(
            P("mb", "head", None, None),
            P("mb"),
            P("mb", None),
            P(None, None, "head"),
            P("head", None),
            P("head", None),
            P(None, "head"),
            P(None, "head"),
            P("head"),
            P("head"),
            P("head"),
            P("head"),
            P("head", None),
            P("mb", "head", None),
        ),
        out_specs=(
            P("mb", "head", None),
            P("mb", "head", None),
            P("mb", None, "head"),
            P("mb", "head"),
            P("mb", "head"),
            P("mb", "head"),
        ),
        check_vma=False,
    )
```

```python
import jax
import jax.numpy as jnp
from jax import lax
from jax.experimental import pallas as pl
from jax.experimental.pallas import tpu as pltpu
from jax.sharding import PartitionSpec as P

T = 128
EPS = 1e-05
WIDTH = 1024
HI = lax.Precision.HIGHEST
MESH = pl.DeviceIdType.MESH
BF = jnp.bfloat16
F32 = jnp.float32


def sigmoid(v):
    return 1.0 / (1.0 + jnp.exp(-v))


def hdot(a, b, dims):
    return lax.dot_general(a, b, (dims, ((), ())), precision=HI, preferred_element_type=F32)


def bdot(a, b, dims):
    return lax.dot_general(a, b, (dims, ((), ())), preferred_element_type=F32)


NN = ((1,), (0,))
NT = ((1,), (1,))
TN = ((0,), (0,))


class Ids:
    def __init__(self):
        self.used = 0

    def take(self, count):
        first = self.used
        self.used += count
        return first


def staged(last):
    return dict(
        p=pltpu.VMEM((4, 4, 2, 2, 4, 16, 128), BF),
        r1=pltpu.VMEM((4, 4, 2, 4, 16, 128), BF),
        q=pltpu.VMEM((4, 4, 2, 4, 16, 128), BF),
        r2x=pltpu.VMEM((3, 2, 4, 2, 16, 128), BF),
        r2y=pltpu.VMEM((3, 2, 2, 4, 16, 128), BF),
        qx=pltpu.VMEM((2, 4, 2, 16, 128), BF),
        qy=pltpu.VMEM((2, 2, 4, 16, 128), BF),
        r3x=pltpu.VMEM((3, 2, 2, 16, 128), BF),
        r3y=pltpu.VMEM((3, 2, 2, 16, 128), BF),
        t=pltpu.VMEM((4, 2, 16, 128), BF),
        r4=pltpu.VMEM(last, BF),
    )


def rows_trade():
    return dict(
        v=pltpu.VMEM((64, 128), F32), g=pltpu.VMEM((64, 128), F32), r=pltpu.VMEM((64, 128), F32)
    )


N_RECV = 52
N_SEND = 66

SCRATCH = dict(
    arr=pltpu.VMEM((T, 4096), BF),
    win=pltpu.VMEM((8192, 128), BF),
    wf=pltpu.VMEM((2, 512, 128), F32),
    wxz=pltpu.VMEM((4096, 256), BF),
    w2=pltpu.VMEM((128, 4096), BF),
    wdtf=pltpu.VMEM((16, 4096), F32),
    wout=pltpu.VMEM((128, 4096), BF),
    cbc=pltpu.VMEM((8, 128), F32),
    ax=pltpu.VMEM((7, 4, 2, 2, 4, 16, 128), BF),
    ao=pltpu.VMEM((7, 4, 2, 2, 4, 16, 128), BF),
    x=pltpu.VMEM((T, 4096), BF),
    o=pltpu.VMEM((T, 4096), BF),
    ss=pltpu.VMEM((32, 128), BF),
    bc=pltpu.VMEM((8, 32, 128), BF),
    norm=pltpu.VMEM((8, 8, 128), F32),
    dbcs=pltpu.VMEM((8, 32, 128), F32),
    dbcr=pltpu.VMEM((8, 32, 128), F32),
    dx=pltpu.VMEM((4, 128, 128), BF),
    dz=pltpu.VMEM((4, 128, 128), BF),
    nm=pltpu.VMEM((4, 128, 128), BF),
    d2=pltpu.VMEM((4, 48, 128), BF),
    gf=pltpu.VMEM((2, 256, 128), F32),
    sx=staged((4, 2, 16, 128)),
    slo=staged((4, 16, 128)),
    sig=staged((4, 16, 128)),
    tog=rows_trade(),
    tlo=rows_trade(),
    tig=rows_trade(),
    ssem=pltpu.SemaphoreType.DMA((N_SEND,)),
    rsem=pltpu.SemaphoreType.DMA((N_RECV,)),
    lsem=pltpu.SemaphoreType.DMA((8,)),
)


def mixer_kernel(
    own_ref, doc_ref, dtb_ref, alog_ref, skip_ref, cx_ref, cbc_ref, gain_ref, wdt_ref, og_ref,
    arr_hbm, win_hbm, wbc_hbm, wout_hbm,
    lo_out, ig_out, gin_out, gbc_out, gdt_out, go_out,
    s,
):
    h = lax.axis_index("head")
    m = lax.axis_index("mb")
    zh = h // 32
    x = (h // 8) % 4
    y = (h // 2) % 4
    c = h % 2
    j = h % 8
    g = h // 8
    g_t = (h % 32) // 4
    part = zh * 4 + h % 4
    ssem, rsem, lsem = s["ssem"], s["rsem"], s["lsem"]
    rids, sids = Ids(), Ids()
    sent = []

    def head_of(zh_, x_, y_, c_):
        return zh_ * 32 + x_ * 8 + y_ * 2 + c_

    def copy(src, dst, i, r, head, mb):
        return pltpu.make_async_remote_copy(
            src_ref=src, dst_ref=dst, send_sem=ssem.at[i], recv_sem=rsem.at[r],
            device_id=(head, mb), device_id_type=MESH,
        )

    def wait_all(ref, sem):
        pltpu.make_async_copy(ref, ref, sem).wait()

    def go(groups):
        waits = []
        for copies, whole in groups:
            i, r = sids.take(1), rids.take(1)
            for src, dst, head, mb in copies:
                copy(src, dst, i, r, head, mb).start()
            waits.append((whole, r))
            sent.append((whole, i))
        return waits

    def got(waits):
        for whole, r in waits:
            wait_all(whole, rsem.at[r])

    loc = [
        pltpu.make_async_copy(arr_hbm, s["arr"], lsem.at[0]),
        pltpu.make_async_copy(win_hbm, s["win"], lsem.at[1]),
        pltpu.make_async_copy(wbc_hbm, s["w2"].at[0:32], lsem.at[2]),
        pltpu.make_async_copy(wout_hbm, s["wout"], lsem.at[3]),
    ]
    for cp in loc:
        cp.start()

    barrier = pltpu.get_barrier_semaphore()
    count = 0
    peers = [(head_of(zh, x, y, 1 - c), m), (head_of(1 - zh, x, y, c), m)]
    for d in range(1, 4):
        peers.append((head_of(zh, (x + d) % 4, y, c), m))
        peers.append((h, (m + d) % 4))
    for d in range(1, 8):
        peers.append((8 * g + (j + d) % 8, m))
    for head, mb in peers:
        pl.semaphore_signal(barrier, inc=1, device_id=(head, mb), device_id_type=MESH)
        count += 1
    own_parts = [4 * g + k for k in range(4)] + [32 + 4 * g + k for k in range(4)]
    targets = [8 * g_t + k for k in range(8)]
    for head in own_parts + targets:
        pl.semaphore_signal(barrier, inc=1, device_id=(head, m), device_id_type=MESH)
        count += 1

    s["cbc"][...] = jnp.zeros((8, 128), F32)
    s["cbc"][0:4, 0:32] = cbc_ref[...]
    s["wdtf"][...] = jnp.zeros((16, 4096), F32)
    s["wdtf"][0:2, :] = wdt_ref[...].astype(F32)
    s["w2"][32:48, :] = s["wdtf"][...].astype(BF)
    s["w2"][48:128, :] = jnp.zeros((80, 4096), BF)

    sx = s["sx"]
    loc[0].wait()

    def split_arr(i, _):
        v = s["arr"][:, pl.ds(pl.multiple_of(i * 256, 256), 256)]
        for cc in range(2):
            sx["p"][i // 4, i % 4, cc] = v[:, cc * 128:(cc + 1) * 128].reshape(2, 4, 16, 128)
        return 0

    lax.fori_loop(0, 16, split_arr, 0, unroll=4)
    pl.semaphore_wait(barrier, count)

    owner = own_ref[0]
    o_zh, o_x, o_y, o_c = owner // 32, (owner // 8) % 4, (owner // 2) % 4, owner % 2

    def combine(own, received, picks):
        if picks is None:
            total = own.astype(F32)
            for v in received:
                total = total + v.astype(F32)
            return total
        value = own
        for v, pick in zip(received, picks):
            value = lax.select(pick, v, value)
        return value

    def stage1_copies(b):
        return [([(b["p"].at[:, :, 1 - c], b["r1"], head_of(zh, x, y, 1 - c), m)], b["r1"])]

    def stage1_merge(b, picks):
        def one(q, _):
            b["q"][q] = combine(b["p"][q, :, c], [b["r1"][q]], picks and picks["c"]).astype(BF)
            return 0
        lax.fori_loop(0, 4, one, 0)

    def stage2_copies(b):
        along_x, along_y = [], []
        for d in range(1, 4):
            x2, y2 = (x + d) % 4, (y + d) % 4
            along_x.append((b["q"].at[0:2, :, :, x2], b["r2x"].at[d - 1], head_of(zh, x2, y, c), m))
            along_y.append((b["q"].at[2:4, y2], b["r2y"].at[d - 1], head_of(zh, x, y2, c), m))
        return [(along_x, b["r2x"]), (along_y, b["r2y"])]

    def stage2_merge(b, picks):
        for q in range(2):
            b["qx"][q] = combine(b["q"][q, :, :, x], [b["r2x"][d, q] for d in range(3)], picks and picks["x"]).astype(BF)
            b["qy"][q] = combine(b["q"][2 + q, y], [b["r2y"][d, q] for d in range(3)], picks and picks["y"]).astype(BF)

    def stage3_copies(b):
        along_x, along_y = [], []
        for d in range(1, 4):
            x2, y2 = (x + d) % 4, (y + d) % 4
            along_y.append((b["qx"].at[:, y2], b["r3x"].at[d - 1], head_of(zh, x, y2, c), m))
            along_x.append((b["qy"].at[:, :, x2], b["r3y"].at[d - 1], head_of(zh, x2, y, c), m))
        return [(along_y, b["r3x"]), (along_x, b["r3y"])]

    def stage3_merge(b, picks):
        b["t"][0:2] = combine(b["qx"][:, y], [b["r3x"][d] for d in range(3)], picks and picks["y"]).astype(BF)
        b["t"][2:4] = combine(b["qy"][:, :, x], [b["r3y"][d] for d in range(3)], picks and picks["x"]).astype(BF)

    other_zh = head_of(1 - zh, x, y, c)

    def gather1(a, s1, s2):
        along_x, along_y = [], []
        r1, r2 = a.at[s1, y, c, :, x], a.at[s2, y, c, :, x]
        for d in range(1, 4):
            x2, y2 = (x + d) % 4, (y + d) % 4
            along_y.append((r1, r1, head_of(zh, x, y2, c), m))
            along_x.append((r2, r2, head_of(zh, x2, y, c), m))
        return [(along_y, a.at[s1, 0:3, c, :, x]), (along_x, a.at[s2, y, c, :, 0:3])]

    def gather2(a, s1, s2):
        along_x, along_y = [], []
        r1, r2 = a.at[s1, :, c, :, x], a.at[s2, y, c]
        for d in range(1, 4):
            x2, y2 = (x + d) % 4, (y + d) % 4
            along_x.append((r1, r1, head_of(zh, x2, y, c), m))
            along_y.append((r2, r2, head_of(zh, x, y2, c), m))
        return [(along_x, a.at[s1, :, c, :, 0:3]), (along_y, a.at[s2, 0:3, c])]

    def gather3(a, part_of):
        ref = a.at[part_of, :, c]
        return [([(ref, ref, head_of(zh, x, y, 1 - c), m)], ref)]

    def trade(b):
        cps = []
        for d in range(1, 8):
            k = (j + d) % 8
            src = b["g"].at[pl.ds(pl.multiple_of(k * 8, 8), 8)]
            dst = b["r"].at[pl.ds(pl.multiple_of(j * 8, 8), 8)]
            cps.append((src, dst, 8 * g + k, m))
        mine = pl.ds(pl.multiple_of(j * 8, 8), 8)
        b["r"][mine, :] = b["g"][mine, :]
        return [(cps, b["r"].at[0:56])]

    lane = lax.broadcasted_iota(jnp.int32, (T, 128), 1)
    row = lax.broadcasted_iota(jnp.int32, (T, 128), 0)

    def unpack_weights(first, last):
        def one(i, _):
            k = i % 2
            s["wf"][k] = s["win"][pl.ds(pl.multiple_of(i * 512, 512), 512), :].astype(F32)
            at = pl.ds(pl.multiple_of(i * 256, 256), 256)
            s["wxz"][at, 0:128] = s["wf"][k, pl.ds(0, 256, stride=2), :].astype(BF)
            s["wxz"][at, 128:256] = s["wf"][k, pl.ds(1, 256, stride=2), :].astype(BF)
            return 0
        lax.fori_loop(first, last, one, 0)

    picks = dict(
        c=[o_c != c],
        x=[o_x == (x + 4 - d) % 4 for d in range(1, 4)],
        y=[o_y == (y + 4 - d) % 4 for d in range(1, 4)],
    )
    a_x, a_o = s["ax"], s["ao"]
    x1 = go(stage1_copies(sx))
    tog = s["tog"]
    og = og_ref[...].astype(F32)
    for k in range(8):
        for q in range(4):
            tog["g"][k * 8 + q * 2:k * 8 + q * 2 + 2, :] = og[:, q * 1024 + k * 128:q * 1024 + k * 128 + 128]
    o1 = go(trade(tog))
    got(x1)
    stage1_merge(sx, picks)
    x2 = go(stage2_copies(sx))
    got(o1)
    for q in range(4):
        for tt in range(2):
            tog["v"][pl.ds(q * 16 + tt, 8, stride=2), :] = tog["r"][pl.ds(q * 2 + tt, 8, stride=8), :]
    a_o[0:4, y, c, zh, x] = tog["v"][...].reshape(4, 16, 128).astype(BF)
    cps = []
    for d in range(1, 4):
        m2 = (m + d) % 4
        cps.append((a_o.at[m2, y, c, zh, x], a_o.at[7 - d, y, c, zh, x], h, m2))
    oc = go([(cps, a_o.at[4:7, y, c, zh, x])])
    oz_ref = a_o.at[0:4, y, c, zh, x]
    oz = go([([(oz_ref, oz_ref, other_zh, m)], oz_ref)])
    loc[1].wait()
    unpack_weights(0, 3)
    got(x2)
    stage2_merge(sx, picks)
    x3 = go(stage3_copies(sx))
    got(oz)
    q01, q23 = slice(0, 2), slice(2, 4)
    og1 = go(gather1(a_o, q01, q23))
    unpack_weights(3, 6)
    got(x3)
    stage3_merge(sx, picks)
    x4 = go([([(sx["t"], sx["r4"], other_zh, m)], sx["r4"])])
    got(oc)
    ocz_ref = a_o.at[4:7, y, c, zh, x]
    ocz = go([([(ocz_ref, ocz_ref, other_zh, m)], ocz_ref)])
    got(og1)
    unpack_weights(6, 9)
    got(x4)
    a_x[0:4, y, c, :, x] = combine(sx["t"][...], [sx["r4"][...]], [o_zh != zh])
    xg1 = go(gather1(a_x, q01, q23))
    cps = []
    for d in range(1, 4):
        m2 = (m + d) % 4
        cps.append((a_x.at[m2, y, c, :, x], a_x.at[7 - d, y, c, :, x], h, m2))
    xc = go([(cps, a_x.at[4:7, y, c, :, x])])
    k1, k2 = slice(4, 5), slice(5, 7)
    l1, l2 = slice(4, 6), slice(6, 7)
    unpack_weights(9, 12)
    got(xg1)
    xg2 = go(gather2(a_x, q01, q23))
    got(ocz)
    cog1 = go(gather1(a_o, l1, l2))
    got(xc)
    cxg1 = go(gather1(a_x, k1, k2))
    unpack_weights(12, 16)
    got(xg2)
    xg3 = go(gather3(a_x, slice(0, 4)))
    og2 = go(gather2(a_o, q01, q23))

    def assemble(a, dst, cc):
        def one(i, _):
            at = pl.ds(pl.multiple_of(i * 256 + cc * 128, 128), 128)
            dst[:, at] = a[i // 4, i % 4, cc].reshape(128, 128)
            return 0
        lax.fori_loop(0, 16, one, 0, unroll=8)

    assemble(a_x, s["x"], c)
    loc[2].wait()
    got(xg3)
    assemble(a_x, s["x"], 1 - c)

    e1 = doc_ref[0, 0]
    e2 = e1 + doc_ref[0, 1]
    e3 = e2 + doc_ref[0, 2]
    e4 = e3 + doc_ref[0, 3]

    def doc_of(t):
        return sum((t >= e).astype(jnp.int32) for e in (e1, e2, e3, e4))

    doc_row = doc_of(row)
    same = [None] + [(row >= o) & (doc_of(row - o) == doc_row) for o in range(1, 4)]
    visible = (row >= lane) & (doc_row == doc_of(lane))

    def conv(v, taps):
        result = v * taps[3:4]
        for o in range(1, 4):
            result = result + jnp.where(same[o], pltpu.roll(v, o, 0), 0.0) * taps[3 - o:4 - o]
        return result

    def conv_back(d, taps):
        result = d * taps[3:4]
        for o in range(1, 4):
            result = result + pltpu.roll(jnp.where(same[o], d, 0.0), T - o, 0) * taps[3 - o:4 - o]
        return result

    p2 = bdot(s["x"][...], s["w2"][...], NT)
    taps_bc = s["cbc"][...]
    bc_pre = conv(p2, taps_bc)
    bc_sig = sigmoid(bc_pre)
    s["ss"][...] = jnp.transpose(bc_pre * bc_sig)[0:32].astype(BF)
    i_bc, r_bc = sids.take(8), rids.take(1)
    for k in range(8):
        head = 8 * g_t + k

        @pl.when(head != h)
        def _():
            copy(s["ss"], s["bc"].at[part], i_bc + k, r_bc, head, m).start()

        @pl.when(head == h)
        def _():
            pltpu.make_async_copy(s["ss"], s["bc"].at[part], rsem.at[r_bc]).start()

    got(cxg1)
    cxg2 = go(gather2(a_x, k1, k2))
    got(cog1)
    cog2 = go(gather2(a_o, l1, l2))

    pxz = bdot(s["x"][...], s["wxz"][...], NN)
    got(og2)
    og3 = go(gather3(a_o, slice(0, 4)))
    z = pxz[:, 128:256]
    taps_x = cx_ref[...]
    x_pre = conv(pxz[:, 0:128], taps_x)
    x_sig = sigmoid(x_pre)
    x_conv = x_pre * x_sig
    z_sig = sigmoid(z)
    z_silu = z * z_sig
    low = lane < 64
    tri = jnp.where(row >= lane, 1.0, 0.0)
    raws, rates, steps = [], [], []
    for e in range(2):
        raw = jnp.broadcast_to(p2[:, 32 + e:33 + e], (T, 128)) + dtb_ref[e]
        raws.append(raw)
        rates.append(-jnp.exp(jnp.full((T, 128), alog_ref[e], F32)))
        steps.append(jnp.maximum(raw, 0.0) + jnp.log1p(jnp.exp(-jnp.abs(raw))))
    step = jnp.where(low, steps[0], steps[1])
    cum = hdot(tri, jnp.where(low, steps[0] * rates[0], steps[1] * rates[1]), NN)
    decays = []
    for e in range(2):
        col = jnp.broadcast_to(cum[:, 64 * e:64 * e + 1], (T, 128))
        gap = col - jnp.transpose(col)
        decays.append(jnp.where(visible, jnp.exp(jnp.where(visible, gap, 0.0)), 0.0))
    scaled = x_conv * step
    skip = jnp.where(low, skip_ref[0], skip_ref[1])

    assemble(a_o, s["o"], c)
    got(og3)
    assemble(a_o, s["o"], 1 - c)
    loc[3].wait()
    weighted = bdot(s["o"][...], s["wout"][...], NT) * gain_ref[...]

    wait_all(s["bc"], rsem.at[r_bc])
    b_t = s["bc"][0:4].reshape(128, 128)
    c_t = s["bc"][4:8].reshape(128, 128)
    scores = bdot(c_t, b_t, TN)
    mixes = [scores * decays[0], scores * decays[1]]
    zero = jnp.zeros((T, 128), F32)
    scaled2 = jnp.concatenate([jnp.where(low, scaled, zero), jnp.where(low, zero, scaled)], axis=0)
    state = hdot(jnp.concatenate(mixes, axis=1), scaled2, NN) + skip * x_conv
    gated = state * z_silu
    squares = jnp.sum(gated * gated, axis=1, keepdims=True)
    inners = jnp.sum(weighted * gated, axis=1, keepdims=True)
    nmat = jnp.where(lane == 0, squares, jnp.where(lane == 1, inners, 0.0))
    s["norm"][j] = jnp.transpose(nmat)[0:8]
    cps = [(s["norm"].at[j], s["norm"].at[j], 8 * g + (j + d) % 8, m) for d in range(1, 8)]
    ncp = go([(cps, s["norm"].at[0:7])])
    got(cxg2)
    cxg3 = go(gather3(a_x, slice(4, 7)))
    got(cog2)
    cog3 = go(gather3(a_o, slice(4, 7)))
    got(ncp)
    total = jnp.sum(s["norm"][...], axis=0)
    tcol = jnp.transpose(jnp.concatenate([total, jnp.zeros((120, 128), F32)], axis=0))
    inverse = jnp.broadcast_to(lax.rsqrt(tcol[:, 0:1] * (1.0 / WIDTH) + EPS), (T, 128))
    inner = jnp.broadcast_to(tcol[:, 1:2] * (1.0 / WIDTH), (T, 128))
    normed = (gated * inverse * gain_ref[...]).astype(BF)
    s["nm"][0] = normed
    d_gated = inverse * weighted - gated * (inverse * inverse * inverse * inner)

    d_state = d_gated * z_silu
    d_z = d_gated * state * (z_sig * (1.0 + z * (1.0 - z_sig)))
    s["dz"][0] = d_z.astype(BF)
    dy0, dy1 = jnp.where(low, d_state, zero), jnp.where(low, zero, d_state)
    d_mix = [hdot(dy0, scaled, NT), hdot(dy1, scaled, NT)]
    d_scores = d_mix[0] * decays[0] + d_mix[1] * decays[1]
    s["dbcs"][0:4] = hdot(c_t.astype(F32), d_scores, NN).reshape(4, 32, 128)
    s["dbcs"][4:8] = hdot(b_t.astype(F32), d_scores, NT).reshape(4, 32, 128)
    i_d, r_d = sids.take(8), rids.take(1)
    for k in range(8):
        head = own_parts[k]

        @pl.when(head != h)
        def _():
            copy(s["dbcs"].at[k], s["dbcr"].at[j], i_d + k, r_d, head, m).start()

        @pl.when(head == h)
        def _():
            pltpu.make_async_copy(s["dbcs"].at[k], s["dbcr"].at[j], rsem.at[r_d]).start()

    def to_mb(ref):
        cps = [(ref.at[0], ref.at[4 - d], h, (m + d) % 4) for d in range(1, 4)]
        return go([(cps, ref.at[1:4])])

    n_mb = to_mb(s["nm"])
    z_mb = to_mb(s["dz"])

    slo, sig = s["slo"], s["sig"]

    def lo_half(cc):
        def one(i, _):
            at = pl.ds(pl.multiple_of(i * 256 + cc * 128, 128), 128)
            v = bdot(normed, s["wout"][:, at], NN)
            slo["p"][i // 4, i % 4, cc] = v.astype(BF).reshape(2, 4, 16, 128)
            return 0
        lax.fori_loop(0, 16, one, 0, unroll=8)

    lo_half(1 - c)
    lo1 = go(stage1_copies(slo))
    lo_half(c)

    d_scaled = hdot(
        jnp.concatenate(mixes, axis=0), jnp.concatenate([dy0, dy1], axis=0), TN
    )
    d_xconv = skip * d_state + d_scaled * step
    d_x = conv_back(d_xconv * (x_sig * (1.0 + x_pre * (1.0 - x_sig))), taps_x)
    s["dx"][0] = d_x.astype(BF)
    x_mb = to_mb(s["dx"])
    through = d_scaled * x_conv
    d_raws = []
    for e in range(2):
        mine = low if e == 0 else lane >= 64
        gap_grad = d_mix[e] * mixes[e]
        d_cum = jnp.sum(gap_grad - jnp.transpose(gap_grad), axis=1, keepdims=True)
        back = hdot(tri, jnp.broadcast_to(d_cum, (T, 128)), TN)
        d_step = jnp.sum(jnp.where(mine, through, 0.0), axis=1, keepdims=True) + rates[e] * back
        d_raws.append(d_step * sigmoid(raws[e]))

    got(lo1)
    stage1_merge(slo, None)
    lo2 = go(stage2_copies(slo))

    wait_all(s["dbcr"], rsem.at[r_d])
    d_act = jnp.transpose(
        jnp.concatenate([jnp.sum(s["dbcr"][...], axis=0), jnp.zeros((96, 128), F32)], axis=0)
    )
    d_bc = conv_back(d_act * (bc_sig * (1.0 + bc_pre * (1.0 - bc_sig))), taps_bc)
    d2 = jnp.where(lane == 32, d_raws[0], jnp.where(lane == 33, d_raws[1], d_bc))
    d2_b = d2.astype(BF)
    s["d2"][0] = jnp.transpose(d2)[0:48].astype(BF)
    d2_mb = to_mb(s["d2"])

    d_proj = jnp.concatenate([s["dx"][0], s["dz"][0]], axis=1)

    def ig_half(cc):
        def one(i, _):
            at = pl.ds(pl.multiple_of(i * 256 + cc * 128, 128), 128)
            v = bdot(d_proj, s["wxz"][at, :], NT) + bdot(d2_b, s["w2"][:, at], NN)
            sig["p"][i // 4, i % 4, cc] = v.astype(BF).reshape(2, 4, 16, 128)
            return 0
        lax.fori_loop(0, 16, one, 0, unroll=8)

    ig_half(1 - c)
    ig1 = go(stage1_copies(sig))
    ig_half(c)
    got(lo2)
    stage2_merge(slo, None)
    lo3 = go(stage3_copies(slo))
    got(ig1)
    stage1_merge(sig, None)
    ig2 = go(stage2_copies(sig))

    got(n_mb)
    got(cog3)
    nm_all = s["nm"][...].reshape(512, 128)

    def grad_out(i, _):
        yy, cc = i // 2, i % 2
        lhs = jnp.concatenate(
            [a_o[m, yy, cc].reshape(128, 128)] + [a_o[k, yy, cc].reshape(128, 128) for k in range(4, 7)], axis=0
        )
        go_out[pl.ds(pl.multiple_of(i * 128, 128), 128), :] = bdot(lhs, nm_all, TN).astype(BF)
        return 0

    lax.fori_loop(0, 8, grad_out, 0, unroll=4)

    def stage4(b):
        return go([([(b["t"].at[:, 1 - zh], b["r4"], other_zh, m)], b["r4"])])

    def stage5(b, t):
        t["v"][...] = (b["t"][:, zh].astype(F32) + b["r4"][...].astype(F32)).reshape(64, 128)
        for q in range(4):
            for tt in range(2):
                t["g"][pl.ds(q * 2 + tt, 8, stride=8), :] = t["v"][pl.ds(q * 16 + tt, 8, stride=2), :]
        return go(trade(t))

    def finish(t, out):
        for k in range(8):
            for q in range(4):
                at = q * 1024 + k * 128
                out[:, at:at + 128] = t["r"][k * 8 + q * 2:k * 8 + q * 2 + 2, :].astype(BF)

    got(lo3)
    stage3_merge(slo, None)
    lo4 = stage4(slo)
    got(x_mb)
    got(z_mb)
    got(d2_mb)
    got(cxg3)
    d_all = jnp.concatenate(
        [s["dx"][...].reshape(512, 128), s["dz"][...].reshape(512, 128)], axis=1
    )
    d2_all = jnp.concatenate([s["d2"][k] for k in range(4)], axis=1)

    def grad_in(i, _):
        yy, cc, k = i // 2, i % 2, i % 2
        lhs = jnp.concatenate(
            [a_x[m, yy, cc].reshape(128, 128)] + [a_x[k_, yy, cc].reshape(128, 128) for k_ in range(4, 7)], axis=0
        )
        r = bdot(lhs, d_all, TN)
        s["gf"][k, pl.ds(0, 128, stride=2), :] = r[:, 0:128]
        s["gf"][k, pl.ds(1, 128, stride=2), :] = r[:, 128:256]
        gin_out[pl.ds(pl.multiple_of(i * 256, 256), 256), :] = s["gf"][k].astype(BF)
        small = bdot(d2_all, lhs, NN)
        at = pl.ds(pl.multiple_of(i * 128, 128), 128)
        gbc_out[:, at] = small[0:32].astype(BF)
        gdt_out[:, at] = small[32:34].astype(BF)
        return 0

    lax.fori_loop(0, 3, grad_in, 0)
    got(ig2)
    stage2_merge(sig, None)
    ig3 = go(stage3_copies(sig))
    lax.fori_loop(3, 5, grad_in, 0)
    got(lo4)
    lo5 = stage5(slo, s["tlo"])
    got(ig3)
    stage3_merge(sig, None)
    ig4 = stage4(sig)
    lax.fori_loop(5, 8, grad_in, 0)
    got(lo5)
    finish(s["tlo"], lo_out)
    got(ig4)
    ig5 = stage5(sig, s["tig"])
    got(ig5)
    finish(s["tig"], ig_out)

    for whole, i in sent:
        wait_all(whole, ssem.at[i])
    for k in range(8):
        @pl.when(8 * g_t + k != h)
        def _():
            wait_all(s["ss"], ssem.at[i_bc + k])

        @pl.when(own_parts[k] != h)
        def _():
            wait_all(s["dbcs"].at[k], ssem.at[i_d + k])

    assert rids.used <= N_RECV and sids.used <= N_SEND, (rids.used, sids.used)


def place_kernel(*refs):
    for source, result in zip(refs[:6], refs[6:]):
        result[...] = source[...]


def per_device(
    arrivals, owners, doc_lengths, w_in, w_bc, w_dt, conv_x, conv_bc, dt_bias, a_log, skip_scale,
    norm_gain, w_out, out_grad,
):
    smem = pl.BlockSpec(memory_space=pltpu.SMEM)
    vmem = pl.BlockSpec(memory_space=pltpu.VMEM)
    hbm = pl.BlockSpec(memory_space=pl.ANY)
    sds = jax.ShapeDtypeStruct
    shapes = (
        sds((2, 4096), BF), sds((2, 4096), BF), sds((2048, 128), BF), sds((32, 1024), BF),
        sds((2, 1024), BF), sds((1024, 128), BF),
    )
    made = pl.pallas_call(
        mixer_kernel,
        out_shape=shapes,
        in_specs=[smem] * 5 + [vmem] * 5 + [hbm] * 4,
        out_specs=(vmem,) * 6,
        scratch_shapes=[SCRATCH],
        compiler_params=pltpu.CompilerParams(
            collective_id=0, has_side_effects=True, vmem_limit_bytes=56 * 1024 * 1024
        ),
    )(
        owners, doc_lengths, dt_bias, a_log, skip_scale, conv_x, conv_bc,
        norm_gain.reshape(1, 128), w_dt, out_grad.reshape(2, 4096),
        arrivals.reshape(T, 4096), w_in.reshape(8192, 128), w_bc, w_out,
    )
    lo, ig, gin, gbc, gdt, gout = pl.pallas_call(
        place_kernel,
        out_shape=shapes,
        in_specs=[vmem] * 6,
        out_specs=(vmem,) * 6,
    )(*made)
    return (
        lo[None], ig[None], gin.reshape(1024, 2, 128), gbc.T, gdt.T, gout,
    )


def solution(mesh):
    return jax.shard_map(
        per_device,
        mesh=mesh,
        in_specs=(
            P("mb", "head", None, None),
            P("mb"),
            P("mb", None),
            P(None, None, "head"),
            P("head", None),
            P("head", None),
            P(None, "head"),
            P(None, "head"),
            P("head"),
            P("head"),
            P("head"),
            P("head"),
            P("head", None),
            P("mb", "head", None),
        ),
        out_specs=(
            P("mb", "head", None),
            P("mb", "head", None),
            P("mb", None, "head"),
            P("mb", "head"),
            P("mb", "head"),
            P("mb", "head"),
        ),
        check_vma=False,
    )
```

```python
import jax
import jax.numpy as jnp
from jax import lax
from jax.experimental import pallas as pl
from jax.experimental.pallas import tpu as pltpu
from jax.sharding import PartitionSpec as P

T = 128
EPS = 1e-05
WIDTH = 1024
HI = lax.Precision.HIGHEST
MESH = pl.DeviceIdType.MESH
BF = jnp.bfloat16
F32 = jnp.float32


def sigmoid(v):
    return 1.0 / (1.0 + jnp.exp(-v))


def hdot(a, b, dims):
    return lax.dot_general(a, b, (dims, ((), ())), precision=HI, preferred_element_type=F32)


def bdot(a, b, dims):
    return lax.dot_general(a, b, (dims, ((), ())), preferred_element_type=F32)


NN = ((1,), (0,))
NT = ((1,), (1,))
TN = ((0,), (0,))


class Ids:
    def __init__(self):
        self.used = 0

    def take(self, count):
        first = self.used
        self.used += count
        return first


def staged(last):
    return dict(
        p=pltpu.VMEM((4, 4, 2, 2, 4, 16, 128), BF),
        r1=pltpu.VMEM((4, 4, 2, 4, 16, 128), BF),
        q=pltpu.VMEM((4, 4, 2, 4, 16, 128), BF),
        r2x=pltpu.VMEM((2, 3, 4, 2, 16, 128), BF),
        r2y=pltpu.VMEM((2, 3, 2, 4, 16, 128), BF),
        qx=pltpu.VMEM((2, 4, 2, 16, 128), BF),
        qy=pltpu.VMEM((2, 2, 4, 16, 128), BF),
        r3x=pltpu.VMEM((2, 3, 2, 16, 128), BF),
        r3y=pltpu.VMEM((2, 3, 2, 16, 128), BF),
        t=pltpu.VMEM((4, 2, 16, 128), BF),
        r4=pltpu.VMEM(last, BF),
    )


def rows_trade():
    return dict(
        v=pltpu.VMEM((64, 128), F32), g=pltpu.VMEM((64, 128), F32), r=pltpu.VMEM((64, 128), F32)
    )


N_RECV = 79
N_SEND = 79

SCRATCH = dict(
    arr=pltpu.VMEM((T, 4096), BF),
    win=pltpu.VMEM((8192, 128), BF),
    wf=pltpu.VMEM((2, 512, 128), F32),
    wxz=pltpu.VMEM((4096, 256), BF),
    w2=pltpu.VMEM((128, 4096), BF),
    wdtf=pltpu.VMEM((16, 4096), F32),
    wout=pltpu.VMEM((128, 4096), BF),
    cbc=pltpu.VMEM((8, 128), F32),
    ax=pltpu.VMEM((7, 4, 2, 2, 4, 16, 128), BF),
    ao=pltpu.VMEM((7, 4, 2, 2, 4, 16, 128), BF),
    x=pltpu.VMEM((T, 4096), BF),
    o=pltpu.VMEM((T, 4096), BF),
    ss=pltpu.VMEM((32, 128), BF),
    bc=pltpu.VMEM((8, 32, 128), BF),
    norm=pltpu.VMEM((8, 8, 128), F32),
    dbcs=pltpu.VMEM((8, 32, 128), BF),
    dbcr=pltpu.VMEM((8, 32, 128), BF),
    dsum=pltpu.VMEM((32, 128), F32),
    dgot=pltpu.VMEM((32, 128), F32),
    dx=pltpu.VMEM((4, 128, 128), BF),
    dz=pltpu.VMEM((4, 128, 128), BF),
    nm=pltpu.VMEM((4, 128, 128), BF),
    d2=pltpu.VMEM((4, 48, 128), BF),
    gf=pltpu.VMEM((2, 256, 128), F32),
    sx=staged((4, 2, 16, 128)),
    slo=staged((4, 16, 128)),
    sig=staged((4, 16, 128)),
    tog=rows_trade(),
    tlo=rows_trade(),
    tig=rows_trade(),
    ssem=pltpu.SemaphoreType.DMA((N_SEND,)),
    rsem=pltpu.SemaphoreType.DMA((N_RECV,)),
    lsem=pltpu.SemaphoreType.DMA((8,)),
)


def mixer_kernel(
    own_ref, doc_ref, dtb_ref, alog_ref, skip_ref, cx_ref, cbc_ref, gain_ref, wdt_ref, og_ref,
    arr_hbm, win_hbm, wbc_hbm, wout_hbm,
    lo_out, ig_out, gin_out, gbc_out, gdt_out, go_out,
    s,
):
    h = lax.axis_index("head")
    m = lax.axis_index("mb")
    zh = h // 32
    x = (h // 8) % 4
    y = (h // 2) % 4
    c = h % 2
    j = h % 8
    g = h // 8
    g_t = (h % 32) // 4
    part = zh * 4 + h % 4
    ssem, rsem, lsem = s["ssem"], s["rsem"], s["lsem"]
    rids, sids = Ids(), Ids()
    sent = []

    def head_of(zh_, x_, y_, c_):
        return zh_ * 32 + x_ * 8 + y_ * 2 + c_

    def copy(src, dst, i, r, head, mb):
        return pltpu.make_async_remote_copy(
            src_ref=src, dst_ref=dst, send_sem=ssem.at[i], recv_sem=rsem.at[r],
            device_id=(head, mb), device_id_type=MESH,
        )

    def wait_all(ref, sem):
        pltpu.make_async_copy(ref, ref, sem).wait()

    def go(groups):
        waits = []
        for copies, whole in groups:
            i, r = sids.take(1), rids.take(1)
            for src, dst, head, mb in copies:
                copy(src, dst, i, r, head, mb).start()
            waits.append((whole, r))
            sent.append((whole, i))
        return waits

    def got(waits):
        for whole, r in waits:
            wait_all(whole, rsem.at[r])

    loc = [
        pltpu.make_async_copy(arr_hbm, s["arr"], lsem.at[0]),
        pltpu.make_async_copy(win_hbm, s["win"], lsem.at[1]),
        pltpu.make_async_copy(wbc_hbm, s["w2"].at[0:32], lsem.at[2]),
        pltpu.make_async_copy(wout_hbm, s["wout"], lsem.at[3]),
    ]
    for cp in loc:
        cp.start()

    barrier = pltpu.get_barrier_semaphore()
    count = 0
    peers = [(head_of(zh, x, y, 1 - c), m), (head_of(1 - zh, x, y, c), m)]
    for d in range(1, 4):
        peers.append((head_of(zh, (x + d) % 4, y, c), m))
        peers.append((h, (m + d) % 4))
    for d in range(1, 8):
        peers.append((8 * g + (j + d) % 8, m))
    for head, mb in peers:
        pl.semaphore_signal(barrier, inc=1, device_id=(head, mb), device_id_type=MESH)
        count += 1
    target = 8 * g_t + part
    source = 4 * g + j + 28 * (j // 4)
    for head in (target, source):
        pl.semaphore_signal(barrier, inc=1, device_id=(head, m), device_id_type=MESH)
        count += 1

    s["cbc"][...] = jnp.zeros((8, 128), F32)
    s["cbc"][0:4, 0:32] = cbc_ref[...]
    s["wdtf"][...] = jnp.zeros((16, 4096), F32)
    s["wdtf"][0:2, :] = wdt_ref[...].astype(F32)
    s["w2"][32:48, :] = s["wdtf"][...].astype(BF)
    s["w2"][48:128, :] = jnp.zeros((80, 4096), BF)

    sx = s["sx"]
    loc[0].wait()

    def split_arr(i, _):
        v = s["arr"][:, pl.ds(pl.multiple_of(i * 256, 256), 256)]
        for cc in range(2):
            sx["p"][i // 4, i % 4, cc] = v[:, cc * 128:(cc + 1) * 128].reshape(2, 4, 16, 128)
        return 0

    lax.fori_loop(0, 16, split_arr, 0, unroll=4)
    pl.semaphore_wait(barrier, count)

    owner = own_ref[0]
    o_zh, o_x, o_y, o_c = owner // 32, (owner // 8) % 4, (owner // 2) % 4, owner % 2

    def combine(own, received, picks):
        if picks is None:
            total = own.astype(F32)
            for v in received:
                total = total + v.astype(F32)
            return total
        value = own
        for v, pick in zip(received, picks):
            value = lax.select(pick, v, value)
        return value

    def stage1_copies(b, k):
        head = head_of(zh, x, y, 1 - c)
        return [([(b["p"].at[q, :, 1 - c], b["r1"].at[q], head, m) for q in (k, 2 + k)], b["r1"].at[0:2])]

    def stage1_merge(b, k, picks):
        for q in (k, 2 + k):
            b["q"][q] = combine(b["p"][q, :, c], [b["r1"][q]], picks and picks["c"]).astype(BF)

    def stage2_copies(b, k):
        along_x, along_y = [], []
        for d in range(1, 4):
            x2, y2 = (x + d) % 4, (y + d) % 4
            along_x.append((b["q"].at[k, :, :, x2], b["r2x"].at[k, d - 1], head_of(zh, x2, y, c), m))
            along_y.append((b["q"].at[2 + k, y2], b["r2y"].at[k, d - 1], head_of(zh, x, y2, c), m))
        return [(along_x, b["r2x"].at[k]), (along_y, b["r2y"].at[k])]

    def stage2_merge(b, k, picks):
        b["qx"][k] = combine(b["q"][k, :, :, x], [b["r2x"][k, d] for d in range(3)], picks and picks["x"]).astype(BF)
        b["qy"][k] = combine(b["q"][2 + k, y], [b["r2y"][k, d] for d in range(3)], picks and picks["y"]).astype(BF)

    def stage3_copies(b, k):
        along_x, along_y = [], []
        for d in range(1, 4):
            x2, y2 = (x + d) % 4, (y + d) % 4
            along_y.append((b["qx"].at[k, y2], b["r3x"].at[k, d - 1], head_of(zh, x, y2, c), m))
            along_x.append((b["qy"].at[k, :, x2], b["r3y"].at[k, d - 1], head_of(zh, x2, y, c), m))
        return [(along_y, b["r3x"].at[k]), (along_x, b["r3y"].at[k])]

    def stage3_merge(b, k, picks):
        b["t"][k] = combine(b["qx"][k, y], [b["r3x"][k, d] for d in range(3)], picks and picks["y"]).astype(BF)
        b["t"][2 + k] = combine(b["qy"][k, :, x], [b["r3y"][k, d] for d in range(3)], picks and picks["x"]).astype(BF)

    other_zh = head_of(1 - zh, x, y, c)

    def gather1(a, s1, s2):
        along_x, along_y = [], []
        r1, r2 = a.at[s1, y, c, :, x], a.at[s2, y, c, :, x]
        for d in range(1, 4):
            x2, y2 = (x + d) % 4, (y + d) % 4
            along_y.append((r1, r1, head_of(zh, x, y2, c), m))
            along_x.append((r2, r2, head_of(zh, x2, y, c), m))
        return [(along_y, a.at[s1, 0:3, c, :, x]), (along_x, a.at[s2, y, c, :, 0:3])]

    def gather2(a, s1, s2):
        along_x, along_y = [], []
        r1, r2 = a.at[s1, :, c, :, x], a.at[s2, y, c]
        for d in range(1, 4):
            x2, y2 = (x + d) % 4, (y + d) % 4
            along_x.append((r1, r1, head_of(zh, x2, y, c), m))
            along_y.append((r2, r2, head_of(zh, x, y2, c), m))
        return [(along_x, a.at[s1, :, c, :, 0:3]), (along_y, a.at[s2, 0:3, c])]

    def gather3(a, part_of):
        ref = a.at[part_of, :, c]
        return [([(ref, ref, head_of(zh, x, y, 1 - c), m)], ref)]

    def trade(b):
        cps = []
        for d in range(1, 8):
            k = (j + d) % 8
            src = b["g"].at[pl.ds(pl.multiple_of(k * 8, 8), 8)]
            dst = b["r"].at[pl.ds(pl.multiple_of(j * 8, 8), 8)]
            cps.append((src, dst, 8 * g + k, m))
        mine = pl.ds(pl.multiple_of(j * 8, 8), 8)
        b["r"][mine, :] = b["g"][mine, :]
        return [(cps, b["r"].at[0:56])]

    lane = lax.broadcasted_iota(jnp.int32, (T, 128), 1)
    row = lax.broadcasted_iota(jnp.int32, (T, 128), 0)

    def unpack_weights(first, last):
        def one(i, _):
            k = i % 2
            s["wf"][k] = s["win"][pl.ds(pl.multiple_of(i * 512, 512), 512), :].astype(F32)
            at = pl.ds(pl.multiple_of(i * 256, 256), 256)
            s["wxz"][at, 0:128] = s["wf"][k, pl.ds(0, 256, stride=2), :].astype(BF)
            s["wxz"][at, 128:256] = s["wf"][k, pl.ds(1, 256, stride=2), :].astype(BF)
            return 0
        lax.fori_loop(first, last, one, 0)

    picks = dict(
        c=[o_c != c],
        x=[o_x == (x + 4 - d) % 4 for d in range(1, 4)],
        y=[o_y == (y + 4 - d) % 4 for d in range(1, 4)],
    )
    a_x, a_o = s["ax"], s["ao"]
    x1 = [go(stage1_copies(sx, k)) for k in range(2)]
    tog = s["tog"]
    og = og_ref[...].astype(F32)
    for k in range(8):
        for q in range(4):
            tog["g"][k * 8 + q * 2:k * 8 + q * 2 + 2, :] = og[:, q * 1024 + k * 128:q * 1024 + k * 128 + 128]
    o1 = go(trade(tog))
    x2 = []
    for k in range(2):
        got(x1[k])
        stage1_merge(sx, k, picks)
        x2.append(go(stage2_copies(sx, k)))
    got(o1)
    for q in range(4):
        for tt in range(2):
            tog["v"][pl.ds(q * 16 + tt, 8, stride=2), :] = tog["r"][pl.ds(q * 2 + tt, 8, stride=8), :]
    a_o[0:4, y, c, zh, x] = tog["v"][...].reshape(4, 16, 128).astype(BF)
    cps = []
    for d in range(1, 4):
        m2 = (m + d) % 4
        cps.append((a_o.at[m2, y, c, zh, x], a_o.at[7 - d, y, c, zh, x], h, m2))
    oc = go([(cps, a_o.at[4:7, y, c, zh, x])])
    oz_ref = a_o.at[0:4, y, c, zh, x]
    oz = go([([(oz_ref, oz_ref, other_zh, m)], oz_ref)])
    loc[1].wait()
    unpack_weights(0, 3)
    x3 = []
    for k in range(2):
        got(x2[k])
        stage2_merge(sx, k, picks)
        x3.append(go(stage3_copies(sx, k)))
    got(oz)
    q01, q23 = slice(0, 2), slice(2, 4)
    og1 = go(gather1(a_o, q01, q23))
    unpack_weights(3, 6)
    x4 = []
    for k in range(2):
        got(x3[k])
        stage3_merge(sx, k, picks)
        x4.append(go([([(sx["t"].at[q], sx["r4"].at[q], other_zh, m) for q in (k, 2 + k)], sx["r4"].at[0:2])]))
    got(oc)
    ocz_ref = a_o.at[4:7, y, c, zh, x]
    ocz = go([([(ocz_ref, ocz_ref, other_zh, m)], ocz_ref)])
    got(og1)
    unpack_weights(6, 9)
    xg1, xg2, xg3 = [], [], []
    first = [slice(k, k + 1) for k in range(2)]
    second = [slice(2 + k, 3 + k) for k in range(2)]
    for k in range(2):
        got(x4[k])
        for q in (k, 2 + k):
            a_x[q, y, c, :, x] = combine(sx["t"][q], [sx["r4"][q]], [o_zh != zh])
        xg1.append(go(gather1(a_x, first[k], second[k])))
    cps = []
    for d in range(1, 4):
        m2 = (m + d) % 4
        cps.append((a_x.at[m2, y, c, :, x], a_x.at[7 - d, y, c, :, x], h, m2))
    xc = go([(cps, a_x.at[4:7, y, c, :, x])])
    k1, k2 = slice(4, 5), slice(5, 7)
    l1, l2 = slice(4, 6), slice(6, 7)
    unpack_weights(9, 12)
    for k in range(2):
        got(xg1[k])
        xg2.append(go(gather2(a_x, first[k], second[k])))
    got(ocz)
    cog1 = go(gather1(a_o, l1, l2))
    got(xc)
    cxg1 = go(gather1(a_x, k1, k2))
    unpack_weights(12, 16)
    for k in range(2):
        got(xg2[k])
        xg3.append(go(gather3(a_x, first[k]) + gather3(a_x, second[k])))
    og2 = go(gather2(a_o, q01, q23))

    def assemble(a, dst, cc, q):
        def one(i, _):
            at = pl.ds(pl.multiple_of(q * 1024 + i * 256 + cc * 128, 128), 128)
            dst[:, at] = a[q, i, cc].reshape(128, 128)
            return 0
        lax.fori_loop(0, 4, one, 0, unroll=True)

    for q in range(4):
        assemble(a_x, s["x"], c, q)
    loc[2].wait()
    p2 = jnp.zeros((T, 128), F32)
    for k in range(2):
        got(xg3[k])
        for q in (k, 2 + k):
            assemble(a_x, s["x"], 1 - c, q)
            at = slice(q * 1024, (q + 1) * 1024)
            p2 = p2 + bdot(s["x"][:, at], s["w2"][:, at], NT)

    e1 = doc_ref[0, 0]
    e2 = e1 + doc_ref[0, 1]
    e3 = e2 + doc_ref[0, 2]
    e4 = e3 + doc_ref[0, 3]

    def doc_of(t):
        return sum((t >= e).astype(jnp.int32) for e in (e1, e2, e3, e4))

    doc_row = doc_of(row)
    same = [None] + [(row >= o) & (doc_of(row - o) == doc_row) for o in range(1, 4)]
    visible = (row >= lane) & (doc_row == doc_of(lane))

    def conv(v, taps):
        result = v * taps[3:4]
        for o in range(1, 4):
            result = result + jnp.where(same[o], pltpu.roll(v, o, 0), 0.0) * taps[3 - o:4 - o]
        return result

    def conv_back(d, taps):
        result = d * taps[3:4]
        for o in range(1, 4):
            result = result + pltpu.roll(jnp.where(same[o], d, 0.0), T - o, 0) * taps[3 - o:4 - o]
        return result

    taps_bc = s["cbc"][...]
    bc_pre = conv(p2, taps_bc)
    bc_sig = sigmoid(bc_pre)
    s["ss"][...] = jnp.transpose(bc_pre * bc_sig)[0:32].astype(BF)
    i_bc, r_bc = sids.take(1), rids.take(1)

    @pl.when(target != h)
    def _():
        copy(s["ss"], s["bc"].at[part], i_bc, r_bc, target, m).start()

    @pl.when(target == h)
    def _():
        pltpu.make_async_copy(s["ss"], s["bc"].at[part], rsem.at[r_bc]).start()

    wait_all(s["bc"].at[j], rsem.at[r_bc])
    peers_of = [8 * g + (j + d) % 8 for d in range(1, 8)]
    bcp = go([([(s["bc"].at[j], s["bc"].at[j], head, m) for head in peers_of], s["bc"].at[0:7])])

    got(cxg1)
    cxg2 = go(gather2(a_x, k1, k2))
    got(cog1)
    cog2 = go(gather2(a_o, l1, l2))

    pxz = bdot(s["x"][...], s["wxz"][...], NN)
    got(og2)
    og3 = go(gather3(a_o, slice(0, 4)))
    z = pxz[:, 128:256]
    taps_x = cx_ref[...]
    x_pre = conv(pxz[:, 0:128], taps_x)
    x_sig = sigmoid(x_pre)
    x_conv = x_pre * x_sig
    z_sig = sigmoid(z)
    z_silu = z * z_sig
    low = lane < 64
    tri = jnp.where(row >= lane, 1.0, 0.0)
    raws, rates, steps = [], [], []
    for e in range(2):
        raw = jnp.broadcast_to(p2[:, 32 + e:33 + e], (T, 128)) + dtb_ref[e]
        raws.append(raw)
        rates.append(-jnp.exp(jnp.full((T, 128), alog_ref[e], F32)))
        steps.append(jnp.maximum(raw, 0.0) + jnp.log1p(jnp.exp(-jnp.abs(raw))))
    step = jnp.where(low, steps[0], steps[1])
    cum = hdot(tri, jnp.where(low, steps[0] * rates[0], steps[1] * rates[1]), NN)
    decays = []
    for e in range(2):
        col = jnp.broadcast_to(cum[:, 64 * e:64 * e + 1], (T, 128))
        gap = col - jnp.transpose(col)
        decays.append(jnp.where(visible, jnp.exp(jnp.where(visible, gap, 0.0)), 0.0))
    scaled = x_conv * step
    skip = jnp.where(low, skip_ref[0], skip_ref[1])

    for q in range(4):
        assemble(a_o, s["o"], c, q)
    got(og3)
    for q in range(4):
        assemble(a_o, s["o"], 1 - c, q)
    loc[3].wait()
    weighted = bdot(s["o"][...], s["wout"][...], NT) * gain_ref[...]

    got(bcp)
    b_t = s["bc"][0:4].reshape(128, 128)
    c_t = s["bc"][4:8].reshape(128, 128)
    scores = bdot(c_t, b_t, TN)
    mixes = [scores * decays[0], scores * decays[1]]
    zero = jnp.zeros((T, 128), F32)
    scaled2 = jnp.concatenate([jnp.where(low, scaled, zero), jnp.where(low, zero, scaled)], axis=0)
    state = hdot(jnp.concatenate(mixes, axis=1), scaled2, NN) + skip * x_conv
    gated = state * z_silu
    squares = jnp.sum(gated * gated, axis=1, keepdims=True)
    inners = jnp.sum(weighted * gated, axis=1, keepdims=True)
    nmat = jnp.where(lane == 0, squares, jnp.where(lane == 1, inners, 0.0))
    s["norm"][j] = jnp.transpose(nmat)[0:8]
    cps = [(s["norm"].at[j], s["norm"].at[j], head, m) for head in peers_of]
    ncp = go([(cps, s["norm"].at[0:7])])
    got(cxg2)
    cxg3 = go(gather3(a_x, slice(4, 7)))
    got(cog2)
    cog3 = go(gather3(a_o, slice(4, 7)))
    got(ncp)
    total = jnp.sum(s["norm"][...], axis=0)
    tcol = jnp.transpose(jnp.concatenate([total, jnp.zeros((120, 128), F32)], axis=0))
    inverse = jnp.broadcast_to(lax.rsqrt(tcol[:, 0:1] * (1.0 / WIDTH) + EPS), (T, 128))
    inner = jnp.broadcast_to(tcol[:, 1:2] * (1.0 / WIDTH), (T, 128))
    normed = (gated * inverse * gain_ref[...]).astype(BF)
    s["nm"][0] = normed
    d_gated = inverse * weighted - gated * (inverse * inverse * inverse * inner)

    d_state = d_gated * z_silu
    d_z = d_gated * state * (z_sig * (1.0 + z * (1.0 - z_sig)))
    s["dz"][0] = d_z.astype(BF)
    dy0, dy1 = jnp.where(low, d_state, zero), jnp.where(low, zero, d_state)
    d_mix = [hdot(dy0, scaled, NT), hdot(dy1, scaled, NT)]
    d_scores = d_mix[0] * decays[0] + d_mix[1] * decays[1]
    s["dbcs"][0:4] = hdot(c_t.astype(F32), d_scores, NN).reshape(4, 32, 128).astype(BF)
    s["dbcs"][4:8] = hdot(b_t.astype(F32), d_scores, NT).reshape(4, 32, 128).astype(BF)
    s["dbcr"][j] = s["dbcs"][j]
    cps = [(s["dbcs"].at[(j + d) % 8], s["dbcr"].at[j], 8 * g + (j + d) % 8, m) for d in range(1, 8)]
    dbc = go([(cps, s["dbcr"].at[0:7])])

    def to_mb(ref):
        cps = [(ref.at[0], ref.at[4 - d], h, (m + d) % 4) for d in range(1, 4)]
        return go([(cps, ref.at[1:4])])

    n_mb = to_mb(s["nm"])
    z_mb = to_mb(s["dz"])

    slo, sig = s["slo"], s["sig"]

    def lo_half(cc):
        def one(i, _):
            at = pl.ds(pl.multiple_of(i * 256 + cc * 128, 128), 128)
            v = bdot(normed, s["wout"][:, at], NN)
            slo["p"][i // 4, i % 4, cc] = v.astype(BF).reshape(2, 4, 16, 128)
            return 0
        lax.fori_loop(0, 16, one, 0, unroll=8)

    lo_half(1 - c)
    lo1 = go(stage1_copies(slo, 0) + stage1_copies(slo, 1))
    got(dbc)
    s["dsum"][...] = jnp.sum(s["dbcr"][...].astype(F32), axis=0)
    i_d, r_d = sids.take(1), rids.take(1)

    @pl.when(source != h)
    def _():
        copy(s["dsum"], s["dgot"], i_d, r_d, source, m).start()

    @pl.when(source == h)
    def _():
        pltpu.make_async_copy(s["dsum"], s["dgot"], rsem.at[r_d]).start()

    lo_half(c)

    d_scaled = hdot(
        jnp.concatenate(mixes, axis=0), jnp.concatenate([dy0, dy1], axis=0), TN
    )
    d_xconv = skip * d_state + d_scaled * step
    d_x = conv_back(d_xconv * (x_sig * (1.0 + x_pre * (1.0 - x_sig))), taps_x)
    s["dx"][0] = d_x.astype(BF)
    x_mb = to_mb(s["dx"])
    through = d_scaled * x_conv
    d_raws = []
    for e in range(2):
        mine = low if e == 0 else lane >= 64
        gap_grad = d_mix[e] * mixes[e]
        d_cum = jnp.sum(gap_grad - jnp.transpose(gap_grad), axis=1, keepdims=True)
        back = hdot(tri, jnp.broadcast_to(d_cum, (T, 128)), TN)
        d_step = jnp.sum(jnp.where(mine, through, 0.0), axis=1, keepdims=True) + rates[e] * back
        d_raws.append(d_step * sigmoid(raws[e]))

    got(lo1)
    for k in range(2):
        stage1_merge(slo, k, None)
    lo2 = go(stage2_copies(slo, 0) + stage2_copies(slo, 1))

    wait_all(s["dgot"], rsem.at[r_d])
    d_act = jnp.transpose(
        jnp.concatenate([s["dgot"][...], jnp.zeros((96, 128), F32)], axis=0)
    )
    d_bc = conv_back(d_act * (bc_sig * (1.0 + bc_pre * (1.0 - bc_sig))), taps_bc)
    d2 = jnp.where(lane == 32, d_raws[0], jnp.where(lane == 33, d_raws[1], d_bc))
    d2_b = d2.astype(BF)
    s["d2"][0] = jnp.transpose(d2)[0:48].astype(BF)
    d2_mb = to_mb(s["d2"])

    d_proj = jnp.concatenate([s["dx"][0], s["dz"][0]], axis=1)

    def ig_half(cc, k):
        for q in (k, 2 + k):
            def one(i, _):
                at = pl.ds(pl.multiple_of(q * 1024 + i * 256 + cc * 128, 128), 128)
                v = bdot(d_proj, s["wxz"][at, :], NT) + bdot(d2_b, s["w2"][:, at], NN)
                sig["p"][q, i, cc] = v.astype(BF).reshape(2, 4, 16, 128)
                return 0
            lax.fori_loop(0, 4, one, 0, unroll=True)

    ig1, ig2, ig3, ig4 = [], [], [], []
    for k in range(2):
        ig_half(1 - c, k)
        ig1.append(go(stage1_copies(sig, k)))
    for k in range(2):
        ig_half(c, k)
    for k in range(2):
        got(ig1[k])
        stage1_merge(sig, k, None)
        ig2.append(go(stage2_copies(sig, k)))
    got(lo2)
    for k in range(2):
        stage2_merge(slo, k, None)
    lo3 = go(stage3_copies(slo, 0) + stage3_copies(slo, 1))

    got(n_mb)
    got(cog3)
    nm_all = s["nm"][...].reshape(512, 128)

    def grad_out(i, _):
        yy, cc = i // 2, i % 2
        lhs = jnp.concatenate(
            [a_o[m, yy, cc].reshape(128, 128)] + [a_o[k, yy, cc].reshape(128, 128) for k in range(4, 7)], axis=0
        )
        go_out[pl.ds(pl.multiple_of(i * 128, 128), 128), :] = bdot(lhs, nm_all, TN).astype(BF)
        return 0

    lax.fori_loop(0, 8, grad_out, 0, unroll=4)

    def stage4(b, k):
        return [([(b["t"].at[q, 1 - zh], b["r4"].at[q], other_zh, m) for q in (k, 2 + k)], b["r4"].at[0:2])]

    def stage5(b, t):
        t["v"][...] = (b["t"][:, zh].astype(F32) + b["r4"][...].astype(F32)).reshape(64, 128)
        for q in range(4):
            for tt in range(2):
                t["g"][pl.ds(q * 2 + tt, 8, stride=8), :] = t["v"][pl.ds(q * 16 + tt, 8, stride=2), :]
        return go(trade(t))

    def finish(t, out):
        for k in range(8):
            for q in range(4):
                at = q * 1024 + k * 128
                out[:, at:at + 128] = t["r"][k * 8 + q * 2:k * 8 + q * 2 + 2, :].astype(BF)

    got(lo3)
    for k in range(2):
        stage3_merge(slo, k, None)
    lo4 = go(stage4(slo, 0) + stage4(slo, 1))
    got(x_mb)
    got(z_mb)
    got(d2_mb)
    got(cxg3)
    d_all = jnp.concatenate(
        [s["dx"][...].reshape(512, 128), s["dz"][...].reshape(512, 128)], axis=1
    )
    d2_all = jnp.concatenate([s["d2"][k] for k in range(4)], axis=1)

    def grad_in(i, _):
        yy, cc, k = i // 2, i % 2, i % 2
        lhs = jnp.concatenate(
            [a_x[m, yy, cc].reshape(128, 128)] + [a_x[k_, yy, cc].reshape(128, 128) for k_ in range(4, 7)], axis=0
        )
        r = bdot(lhs, d_all, TN)
        s["gf"][k, pl.ds(0, 128, stride=2), :] = r[:, 0:128]
        s["gf"][k, pl.ds(1, 128, stride=2), :] = r[:, 128:256]
        gin_out[pl.ds(pl.multiple_of(i * 256, 256), 256), :] = s["gf"][k].astype(BF)
        small = bdot(d2_all, lhs, NN)
        at = pl.ds(pl.multiple_of(i * 128, 128), 128)
        gbc_out[:, at] = small[0:32].astype(BF)
        gdt_out[:, at] = small[32:34].astype(BF)
        return 0

    lax.fori_loop(0, 3, grad_in, 0)
    for k in range(2):
        got(ig2[k])
        stage2_merge(sig, k, None)
        ig3.append(go(stage3_copies(sig, k)))
    lax.fori_loop(3, 5, grad_in, 0)
    got(lo4)
    lo5 = stage5(slo, s["tlo"])
    for k in range(2):
        got(ig3[k])
        stage3_merge(sig, k, None)
        ig4.append(go(stage4(sig, k)))
    lax.fori_loop(5, 8, grad_in, 0)
    got(lo5)
    finish(s["tlo"], lo_out)
    for k in range(2):
        got(ig4[k])
    ig5 = stage5(sig, s["tig"])
    got(ig5)
    finish(s["tig"], ig_out)

    for whole, i in sent:
        wait_all(whole, ssem.at[i])
    @pl.when(target != h)
    def _():
        wait_all(s["ss"], ssem.at[i_bc])

    @pl.when(source != h)
    def _():
        wait_all(s["dsum"], ssem.at[i_d])

    assert rids.used <= N_RECV and sids.used <= N_SEND, (rids.used, sids.used)


def place_kernel(*refs):
    for source, result in zip(refs[:6], refs[6:]):
        result[...] = source[...]


def per_device(
    arrivals, owners, doc_lengths, w_in, w_bc, w_dt, conv_x, conv_bc, dt_bias, a_log, skip_scale,
    norm_gain, w_out, out_grad,
):
    smem = pl.BlockSpec(memory_space=pltpu.SMEM)
    vmem = pl.BlockSpec(memory_space=pltpu.VMEM)
    hbm = pl.BlockSpec(memory_space=pl.ANY)
    sds = jax.ShapeDtypeStruct
    shapes = (
        sds((2, 4096), BF), sds((2, 4096), BF), sds((2048, 128), BF), sds((32, 1024), BF),
        sds((2, 1024), BF), sds((1024, 128), BF),
    )
    made = pl.pallas_call(
        mixer_kernel,
        out_shape=shapes,
        in_specs=[smem] * 5 + [vmem] * 5 + [hbm] * 4,
        out_specs=(vmem,) * 6,
        scratch_shapes=[SCRATCH],
        compiler_params=pltpu.CompilerParams(
            collective_id=0, has_side_effects=True, vmem_limit_bytes=56 * 1024 * 1024
        ),
    )(
        owners, doc_lengths, dt_bias, a_log, skip_scale, conv_x, conv_bc,
        norm_gain.reshape(1, 128), w_dt, out_grad.reshape(2, 4096),
        arrivals.reshape(T, 4096), w_in.reshape(8192, 128), w_bc, w_out,
    )
    lo, ig, gin, gbc, gdt, gout = pl.pallas_call(
        place_kernel,
        out_shape=shapes,
        in_specs=[vmem] * 6,
        out_specs=(vmem,) * 6,
    )(*made)
    return (
        lo[None], ig[None], gin.reshape(1024, 2, 128), gbc.T, gdt.T, gout,
    )


def solution(mesh):
    return jax.shard_map(
        per_device,
        mesh=mesh,
        in_specs=(
            P("mb", "head", None, None),
            P("mb"),
            P("mb", None),
            P(None, None, "head"),
            P("head", None),
            P("head", None),
            P(None, "head"),
            P(None, "head"),
            P("head"),
            P("head"),
            P("head"),
            P("head"),
            P("head", None),
            P("mb", "head", None),
        ),
        out_specs=(
            P("mb", "head", None),
            P("mb", "head", None),
            P("mb", None, "head"),
            P("mb", "head"),
            P("mb", "head"),
            P("mb", "head"),
        ),
        check_vma=False,
    )
```

```python
import jax
import jax.numpy as jnp
from jax import lax
from jax.experimental import pallas as pl
from jax.experimental.pallas import tpu as pltpu
from jax.sharding import PartitionSpec as P

T = 128
EPS = 1e-05
WIDTH = 1024
HI = lax.Precision.HIGHEST
MESH = pl.DeviceIdType.MESH
BF = jnp.bfloat16
F32 = jnp.float32


def sigmoid(v):
    return 1.0 / (1.0 + jnp.exp(-v))


def hdot(a, b, dims):
    return lax.dot_general(a, b, (dims, ((), ())), precision=HI, preferred_element_type=F32)


def bdot(a, b, dims):
    return lax.dot_general(a, b, (dims, ((), ())), preferred_element_type=F32)


NN = ((1,), (0,))
NT = ((1,), (1,))
TN = ((0,), (0,))


class Ids:
    def __init__(self):
        self.used = 0

    def take(self, count):
        first = self.used
        self.used += count
        return first


def staged(last):
    return dict(
        p=pltpu.VMEM((4, 4, 2, 2, 4, 16, 128), BF),
        r1=pltpu.VMEM((4, 4, 2, 4, 16, 128), BF),
        q=pltpu.VMEM((4, 4, 2, 4, 16, 128), BF),
        r2x=pltpu.VMEM((2, 3, 4, 2, 16, 128), BF),
        r2y=pltpu.VMEM((2, 3, 2, 4, 16, 128), BF),
        qx=pltpu.VMEM((2, 4, 2, 16, 128), BF),
        qy=pltpu.VMEM((2, 2, 4, 16, 128), BF),
        r3x=pltpu.VMEM((2, 3, 2, 16, 128), BF),
        r3y=pltpu.VMEM((2, 3, 2, 16, 128), BF),
        t=pltpu.VMEM((4, 2, 16, 128), BF),
        r4=pltpu.VMEM(last, BF),
    )


def rows_trade():
    return dict(
        v=pltpu.VMEM((64, 128), F32), g=pltpu.VMEM((64, 128), F32), r=pltpu.VMEM((64, 128), F32)
    )


N_RECV = 79
N_SEND = 79

SCRATCH = dict(
    arr=pltpu.VMEM((T, 4096), BF),
    win=pltpu.VMEM((8192, 128), BF),
    wf=pltpu.VMEM((2, 512, 128), F32),
    wxz=pltpu.VMEM((4096, 256), BF),
    w2=pltpu.VMEM((128, 4096), BF),
    wdtf=pltpu.VMEM((16, 4096), F32),
    wout=pltpu.VMEM((128, 4096), BF),
    cbc=pltpu.VMEM((8, 128), F32),
    ax=pltpu.VMEM((7, 4, 2, 2, 4, 16, 128), BF),
    ao=pltpu.VMEM((7, 4, 2, 2, 4, 16, 128), BF),
    x=pltpu.VMEM((T, 4096), BF),
    o=pltpu.VMEM((T, 4096), BF),
    ss=pltpu.VMEM((32, 128), BF),
    bc=pltpu.VMEM((8, 32, 128), BF),
    norm=pltpu.VMEM((8, 8, 128), F32),
    dbcs=pltpu.VMEM((8, 32, 128), BF),
    dbcr=pltpu.VMEM((8, 32, 128), BF),
    dsum=pltpu.VMEM((32, 128), F32),
    dgot=pltpu.VMEM((32, 128), F32),
    dx=pltpu.VMEM((4, 128, 128), BF),
    dz=pltpu.VMEM((4, 128, 128), BF),
    nm=pltpu.VMEM((4, 128, 128), BF),
    d2=pltpu.VMEM((4, 48, 128), BF),
    gf=pltpu.VMEM((2, 256, 128), F32),
    sx=staged((4, 2, 16, 128)),
    slo=staged((4, 16, 128)),
    sig=staged((4, 16, 128)),
    tog=rows_trade(),
    tlo=rows_trade(),
    tig=rows_trade(),
    ssem=pltpu.SemaphoreType.DMA((N_SEND,)),
    rsem=pltpu.SemaphoreType.DMA((N_RECV,)),
    lsem=pltpu.SemaphoreType.DMA((8,)),
)


def mixer_kernel(
    own_ref, doc_ref, dtb_ref, alog_ref, skip_ref, cx_ref, cbc_ref, gain_ref, wdt_ref, og_ref,
    arr_hbm, win_hbm, wbc_hbm, wout_hbm,
    lo_out, ig_out, gin_out, gbc_out, gdt_out, go_out,
    s,
):
    h = lax.axis_index("head")
    m = lax.axis_index("mb")
    zh = h // 32
    x = (h // 8) % 4
    y = (h // 2) % 4
    c = h % 2
    j = h % 8
    g = h // 8
    g_t = (h % 32) // 4
    part = zh * 4 + h % 4
    ssem, rsem, lsem = s["ssem"], s["rsem"], s["lsem"]
    rids, sids = Ids(), Ids()
    sent = []

    def head_of(zh_, x_, y_, c_):
        return zh_ * 32 + x_ * 8 + y_ * 2 + c_

    def copy(src, dst, i, r, head, mb):
        return pltpu.make_async_remote_copy(
            src_ref=src, dst_ref=dst, send_sem=ssem.at[i], recv_sem=rsem.at[r],
            device_id=(head, mb), device_id_type=MESH,
        )

    def wait_all(ref, sem):
        pltpu.make_async_copy(ref, ref, sem).wait()

    def go(groups):
        waits = []
        for copies, whole in groups:
            i, r = sids.take(1), rids.take(1)
            for src, dst, head, mb in copies:
                copy(src, dst, i, r, head, mb).start()
            waits.append((whole, r))
            sent.append((whole, i))
        return waits

    def got(waits):
        for whole, r in waits:
            wait_all(whole, rsem.at[r])

    loc = [
        pltpu.make_async_copy(arr_hbm, s["arr"], lsem.at[0]),
        pltpu.make_async_copy(win_hbm, s["win"], lsem.at[1]),
        pltpu.make_async_copy(wbc_hbm, s["w2"].at[0:32], lsem.at[2]),
        pltpu.make_async_copy(wout_hbm, s["wout"], lsem.at[3]),
    ]
    for cp in loc:
        cp.start()

    barrier = pltpu.get_barrier_semaphore()
    count = 0
    peers = [(head_of(zh, x, y, 1 - c), m), (head_of(1 - zh, x, y, c), m)]
    for d in range(1, 4):
        peers.append((head_of(zh, (x + d) % 4, y, c), m))
        peers.append((h, (m + d) % 4))
    for d in range(1, 8):
        peers.append((8 * g + (j + d) % 8, m))
    for head, mb in peers:
        pl.semaphore_signal(barrier, inc=1, device_id=(head, mb), device_id_type=MESH)
        count += 1
    target = 8 * g_t + part
    source = 4 * g + j + 28 * (j // 4)
    for head in (target, source):
        pl.semaphore_signal(barrier, inc=1, device_id=(head, m), device_id_type=MESH)
        count += 1

    s["cbc"][...] = jnp.zeros((8, 128), F32)
    s["cbc"][0:4, 0:32] = cbc_ref[...]
    s["wdtf"][...] = jnp.zeros((16, 4096), F32)
    s["wdtf"][0:2, :] = wdt_ref[...].astype(F32)
    s["w2"][32:48, :] = s["wdtf"][...].astype(BF)
    s["w2"][48:128, :] = jnp.zeros((80, 4096), BF)

    sx = s["sx"]
    loc[0].wait()

    def split_arr(i, _):
        v = s["arr"][:, pl.ds(pl.multiple_of(i * 256, 256), 256)]
        for cc in range(2):
            sx["p"][i // 4, i % 4, cc] = v[:, cc * 128:(cc + 1) * 128].reshape(2, 4, 16, 128)
        return 0

    lax.fori_loop(0, 16, split_arr, 0, unroll=4)
    pl.semaphore_wait(barrier, count)

    owner = own_ref[0]
    o_zh, o_x, o_y, o_c = owner // 32, (owner // 8) % 4, (owner // 2) % 4, owner % 2

    def combine(own, received, picks):
        if picks is None:
            total = own.astype(F32)
            for v in received:
                total = total + v.astype(F32)
            return total
        value = own
        for v, pick in zip(received, picks):
            value = lax.select(pick, v, value)
        return value

    def stage1_copies(b, k):
        head = head_of(zh, x, y, 1 - c)
        return [([(b["p"].at[q, :, 1 - c], b["r1"].at[q], head, m) for q in (k, 2 + k)], b["r1"].at[0:2])]

    def stage1_merge(b, k, picks):
        for q in (k, 2 + k):
            b["q"][q] = combine(b["p"][q, :, c], [b["r1"][q]], picks and picks["c"]).astype(BF)

    def stage2_copies(b, k):
        along_x, along_y = [], []
        for d in range(1, 4):
            x2, y2 = (x + d) % 4, (y + d) % 4
            along_x.append((b["q"].at[k, :, :, x2], b["r2x"].at[k, d - 1], head_of(zh, x2, y, c), m))
            along_y.append((b["q"].at[2 + k, y2], b["r2y"].at[k, d - 1], head_of(zh, x, y2, c), m))
        return [(along_x, b["r2x"].at[k]), (along_y, b["r2y"].at[k])]

    def stage2_merge(b, k, picks):
        b["qx"][k] = combine(b["q"][k, :, :, x], [b["r2x"][k, d] for d in range(3)], picks and picks["x"]).astype(BF)
        b["qy"][k] = combine(b["q"][2 + k, y], [b["r2y"][k, d] for d in range(3)], picks and picks["y"]).astype(BF)

    def stage3_copies(b, k):
        along_x, along_y = [], []
        for d in range(1, 4):
            x2, y2 = (x + d) % 4, (y + d) % 4
            along_y.append((b["qx"].at[k, y2], b["r3x"].at[k, d - 1], head_of(zh, x, y2, c), m))
            along_x.append((b["qy"].at[k, :, x2], b["r3y"].at[k, d - 1], head_of(zh, x2, y, c), m))
        return [(along_y, b["r3x"].at[k]), (along_x, b["r3y"].at[k])]

    def stage3_merge(b, k, picks):
        b["t"][k] = combine(b["qx"][k, y], [b["r3x"][k, d] for d in range(3)], picks and picks["y"]).astype(BF)
        b["t"][2 + k] = combine(b["qy"][k, :, x], [b["r3y"][k, d] for d in range(3)], picks and picks["x"]).astype(BF)

    other_zh = head_of(1 - zh, x, y, c)

    def gather1(a, s1, s2):
        along_x, along_y = [], []
        r1, r2 = a.at[s1, y, c, :, x], a.at[s2, y, c, :, x]
        for d in range(1, 4):
            x2, y2 = (x + d) % 4, (y + d) % 4
            along_y.append((r1, r1, head_of(zh, x, y2, c), m))
            along_x.append((r2, r2, head_of(zh, x2, y, c), m))
        return [(along_y, a.at[s1, 0:3, c, :, x]), (along_x, a.at[s2, y, c, :, 0:3])]

    def gather2(a, s1, s2):
        along_x, along_y = [], []
        r1, r2 = a.at[s1, :, c, :, x], a.at[s2, y, c]
        for d in range(1, 4):
            x2, y2 = (x + d) % 4, (y + d) % 4
            along_x.append((r1, r1, head_of(zh, x2, y, c), m))
            along_y.append((r2, r2, head_of(zh, x, y2, c), m))
        return [(along_x, a.at[s1, :, c, :, 0:3]), (along_y, a.at[s2, 0:3, c])]

    def gather3(a, part_of):
        ref = a.at[part_of, :, c]
        return [([(ref, ref, head_of(zh, x, y, 1 - c), m)], ref)]

    def trade(b):
        cps = []
        for d in range(1, 8):
            k = (j + d) % 8
            src = b["g"].at[pl.ds(pl.multiple_of(k * 8, 8), 8)]
            dst = b["r"].at[pl.ds(pl.multiple_of(j * 8, 8), 8)]
            cps.append((src, dst, 8 * g + k, m))
        mine = pl.ds(pl.multiple_of(j * 8, 8), 8)
        b["r"][mine, :] = b["g"][mine, :]
        return [(cps, b["r"].at[0:56])]

    lane = lax.broadcasted_iota(jnp.int32, (T, 128), 1)
    row = lax.broadcasted_iota(jnp.int32, (T, 128), 0)

    def unpack_weights(first, last):
        def one(i, _):
            k = i % 2
            s["wf"][k] = s["win"][pl.ds(pl.multiple_of(i * 512, 512), 512), :].astype(F32)
            at = pl.ds(pl.multiple_of(i * 256, 256), 256)
            s["wxz"][at, 0:128] = s["wf"][k, pl.ds(0, 256, stride=2), :].astype(BF)
            s["wxz"][at, 128:256] = s["wf"][k, pl.ds(1, 256, stride=2), :].astype(BF)
            return 0
        lax.fori_loop(first, last, one, 0)

    picks = dict(
        c=[o_c != c],
        x=[o_x == (x + 4 - d) % 4 for d in range(1, 4)],
        y=[o_y == (y + 4 - d) % 4 for d in range(1, 4)],
    )
    a_x, a_o = s["ax"], s["ao"]
    x1 = [go(stage1_copies(sx, k)) for k in range(2)]
    tog = s["tog"]
    og = og_ref[...].astype(F32)
    for k in range(8):
        for q in range(4):
            tog["g"][k * 8 + q * 2:k * 8 + q * 2 + 2, :] = og[:, q * 1024 + k * 128:q * 1024 + k * 128 + 128]
    o1 = go(trade(tog))
    x2 = []
    for k in range(2):
        got(x1[k])
        stage1_merge(sx, k, picks)
        x2.append(go(stage2_copies(sx, k)))
    got(o1)
    for q in range(4):
        for tt in range(2):
            tog["v"][pl.ds(q * 16 + tt, 8, stride=2), :] = tog["r"][pl.ds(q * 2 + tt, 8, stride=8), :]
    a_o[0:4, y, c, zh, x] = tog["v"][...].reshape(4, 16, 128).astype(BF)
    cps = []
    for d in range(1, 4):
        m2 = (m + d) % 4
        cps.append((a_o.at[m2, y, c, zh, x], a_o.at[7 - d, y, c, zh, x], h, m2))
    oc = go([(cps, a_o.at[4:7, y, c, zh, x])])
    oz_ref = a_o.at[0:4, y, c, zh, x]
    oz = go([([(oz_ref, oz_ref, other_zh, m)], oz_ref)])
    loc[1].wait()
    unpack_weights(0, 3)
    x3 = []
    for k in range(2):
        got(x2[k])
        stage2_merge(sx, k, picks)
        x3.append(go(stage3_copies(sx, k)))
    got(oz)
    q01, q23 = slice(0, 2), slice(2, 4)
    og1 = go(gather1(a_o, q01, q23))
    unpack_weights(3, 6)
    x4 = []
    for k in range(2):
        got(x3[k])
        stage3_merge(sx, k, picks)
        x4.append(go([([(sx["t"].at[q], sx["r4"].at[q], other_zh, m) for q in (k, 2 + k)], sx["r4"].at[0:2])]))
    got(oc)
    ocz_ref = a_o.at[4:7, y, c, zh, x]
    ocz = go([([(ocz_ref, ocz_ref, other_zh, m)], ocz_ref)])
    got(og1)
    unpack_weights(6, 9)
    xg1, xg2, xg3 = [], [], []
    first = [slice(k, k + 1) for k in range(2)]
    second = [slice(2 + k, 3 + k) for k in range(2)]
    for k in range(2):
        got(x4[k])
        for q in (k, 2 + k):
            a_x[q, y, c, :, x] = combine(sx["t"][q], [sx["r4"][q]], [o_zh != zh])
        xg1.append(go(gather1(a_x, first[k], second[k])))
    cps = []
    for d in range(1, 4):
        m2 = (m + d) % 4
        cps.append((a_x.at[m2, y, c, :, x], a_x.at[7 - d, y, c, :, x], h, m2))
    xc = go([(cps, a_x.at[4:7, y, c, :, x])])
    k1, k2 = slice(4, 5), slice(5, 7)
    l1, l2 = slice(4, 6), slice(6, 7)
    unpack_weights(9, 12)
    for k in range(2):
        got(xg1[k])
        xg2.append(go(gather2(a_x, first[k], second[k])))
    got(ocz)
    cog1 = go(gather1(a_o, l1, l2))
    got(xc)
    cxg1 = go(gather1(a_x, k1, k2))
    unpack_weights(12, 16)
    for k in range(2):
        got(xg2[k])
        xg3.append(go(gather3(a_x, first[k]) + gather3(a_x, second[k])))
    og2 = go(gather2(a_o, q01, q23))

    def assemble(a, dst, cc, q):
        def one(i, _):
            at = pl.ds(pl.multiple_of(q * 1024 + i * 256 + cc * 128, 128), 128)
            dst[:, at] = a[q, i, cc].reshape(128, 128)
            return 0
        lax.fori_loop(0, 4, one, 0, unroll=True)

    for q in range(4):
        assemble(a_x, s["x"], c, q)
    loc[2].wait()
    p2 = jnp.zeros((T, 128), F32)
    for k in range(2):
        got(xg3[k])
        for q in (k, 2 + k):
            assemble(a_x, s["x"], 1 - c, q)
            at = slice(q * 1024, (q + 1) * 1024)
            p2 = p2 + bdot(s["x"][:, at], s["w2"][:, at], NT)

    e1 = doc_ref[0, 0]
    e2 = e1 + doc_ref[0, 1]
    e3 = e2 + doc_ref[0, 2]
    e4 = e3 + doc_ref[0, 3]

    def doc_of(t):
        return sum((t >= e).astype(jnp.int32) for e in (e1, e2, e3, e4))

    doc_row = doc_of(row)
    same = [None] + [(row >= o) & (doc_of(row - o) == doc_row) for o in range(1, 4)]
    visible = (row >= lane) & (doc_row == doc_of(lane))

    def conv(v, taps):
        result = v * taps[3:4]
        for o in range(1, 4):
            result = result + jnp.where(same[o], pltpu.roll(v, o, 0), 0.0) * taps[3 - o:4 - o]
        return result

    def conv_back(d, taps):
        result = d * taps[3:4]
        for o in range(1, 4):
            result = result + pltpu.roll(jnp.where(same[o], d, 0.0), T - o, 0) * taps[3 - o:4 - o]
        return result

    taps_bc = s["cbc"][...]
    bc_pre = conv(p2, taps_bc)
    bc_sig = sigmoid(bc_pre)
    s["ss"][...] = jnp.transpose(bc_pre * bc_sig)[0:32].astype(BF)
    i_bc, r_bc = sids.take(1), rids.take(1)

    @pl.when(target != h)
    def _():
        copy(s["ss"], s["bc"].at[part], i_bc, r_bc, target, m).start()

    @pl.when(target == h)
    def _():
        pltpu.make_async_copy(s["ss"], s["bc"].at[part], rsem.at[r_bc]).start()

    wait_all(s["bc"].at[j], rsem.at[r_bc])
    peers_of = [8 * g + (j + d) % 8 for d in range(1, 8)]
    bcp = go([([(s["bc"].at[j], s["bc"].at[j], head, m) for head in peers_of], s["bc"].at[0:7])])

    got(cxg1)
    cxg2 = go(gather2(a_x, k1, k2))

    pxz = bdot(s["x"][...], s["wxz"][...], NN)
    got(og2)
    og3 = go(gather3(a_o, slice(0, 4)))
    z = pxz[:, 128:256]
    taps_x = cx_ref[...]
    x_pre = conv(pxz[:, 0:128], taps_x)
    x_sig = sigmoid(x_pre)
    x_conv = x_pre * x_sig
    z_sig = sigmoid(z)
    z_silu = z * z_sig
    low = lane < 64
    tri = jnp.where(row >= lane, 1.0, 0.0)
    raws, rates, steps = [], [], []
    for e in range(2):
        raw = jnp.broadcast_to(p2[:, 32 + e:33 + e], (T, 128)) + dtb_ref[e]
        raws.append(raw)
        rates.append(-jnp.exp(jnp.full((T, 128), alog_ref[e], F32)))
        steps.append(jnp.maximum(raw, 0.0) + jnp.log1p(jnp.exp(-jnp.abs(raw))))
    step = jnp.where(low, steps[0], steps[1])
    cum = hdot(tri, jnp.where(low, steps[0] * rates[0], steps[1] * rates[1]), NN)
    decays = []
    for e in range(2):
        col = jnp.broadcast_to(cum[:, 64 * e:64 * e + 1], (T, 128))
        gap = col - jnp.transpose(col)
        decays.append(jnp.where(visible, jnp.exp(jnp.where(visible, gap, 0.0)), 0.0))
    scaled = x_conv * step
    skip = jnp.where(low, skip_ref[0], skip_ref[1])

    for q in range(4):
        assemble(a_o, s["o"], c, q)
    got(og3)
    for q in range(4):
        assemble(a_o, s["o"], 1 - c, q)
    loc[3].wait()
    weighted = bdot(s["o"][...], s["wout"][...], NT) * gain_ref[...]

    got(bcp)
    b_t = s["bc"][0:4].reshape(128, 128)
    c_t = s["bc"][4:8].reshape(128, 128)
    scores = bdot(c_t, b_t, TN)
    mixes = [scores * decays[0], scores * decays[1]]
    zero = jnp.zeros((T, 128), F32)
    scaled2 = jnp.concatenate([jnp.where(low, scaled, zero), jnp.where(low, zero, scaled)], axis=0)
    state = hdot(jnp.concatenate(mixes, axis=1), scaled2, NN) + skip * x_conv
    gated = state * z_silu
    squares = jnp.sum(gated * gated, axis=1, keepdims=True)
    inners = jnp.sum(weighted * gated, axis=1, keepdims=True)
    nmat = jnp.where(lane == 0, squares, jnp.where(lane == 1, inners, 0.0))
    s["norm"][j] = jnp.transpose(nmat)[0:8]
    cps = [(s["norm"].at[j], s["norm"].at[j], head, m) for head in peers_of]
    ncp = go([(cps, s["norm"].at[0:7])])
    got(cxg2)
    cxg3 = go(gather3(a_x, slice(4, 7)))
    got(ncp)
    total = jnp.sum(s["norm"][...], axis=0)
    tcol = jnp.transpose(jnp.concatenate([total, jnp.zeros((120, 128), F32)], axis=0))
    inverse = jnp.broadcast_to(lax.rsqrt(tcol[:, 0:1] * (1.0 / WIDTH) + EPS), (T, 128))
    inner = jnp.broadcast_to(tcol[:, 1:2] * (1.0 / WIDTH), (T, 128))
    normed = (gated * inverse * gain_ref[...]).astype(BF)
    s["nm"][0] = normed
    d_gated = inverse * weighted - gated * (inverse * inverse * inverse * inner)

    d_state = d_gated * z_silu
    d_z = d_gated * state * (z_sig * (1.0 + z * (1.0 - z_sig)))
    s["dz"][0] = d_z.astype(BF)
    dy0, dy1 = jnp.where(low, d_state, zero), jnp.where(low, zero, d_state)
    d_mix = [hdot(dy0, scaled, NT), hdot(dy1, scaled, NT)]
    d_scores = d_mix[0] * decays[0] + d_mix[1] * decays[1]
    s["dbcs"][0:4] = hdot(c_t.astype(F32), d_scores, NN).reshape(4, 32, 128).astype(BF)
    s["dbcs"][4:8] = hdot(b_t.astype(F32), d_scores, NT).reshape(4, 32, 128).astype(BF)
    s["dbcr"][j] = s["dbcs"][j]
    cps = [(s["dbcs"].at[(j + d) % 8], s["dbcr"].at[j], 8 * g + (j + d) % 8, m) for d in range(1, 8)]
    dbc = go([(cps, s["dbcr"].at[0:7])])
    got(cog1)
    cog2 = go(gather2(a_o, l1, l2))

    def to_mb(ref):
        cps = [(ref.at[0], ref.at[4 - d], h, (m + d) % 4) for d in range(1, 4)]
        return go([(cps, ref.at[1:4])])

    n_mb = to_mb(s["nm"])
    z_mb = to_mb(s["dz"])

    slo, sig = s["slo"], s["sig"]

    def lo_half(cc):
        def one(i, _):
            at = pl.ds(pl.multiple_of(i * 256 + cc * 128, 128), 128)
            v = bdot(normed, s["wout"][:, at], NN)
            slo["p"][i // 4, i % 4, cc] = v.astype(BF).reshape(2, 4, 16, 128)
            return 0
        lax.fori_loop(0, 16, one, 0, unroll=8)

    lo_half(1 - c)
    lo1 = go(stage1_copies(slo, 0) + stage1_copies(slo, 1))
    got(dbc)
    s["dsum"][...] = jnp.sum(s["dbcr"][...].astype(F32), axis=0)
    i_d, r_d = sids.take(1), rids.take(1)

    @pl.when(source != h)
    def _():
        copy(s["dsum"], s["dgot"], i_d, r_d, source, m).start()

    @pl.when(source == h)
    def _():
        pltpu.make_async_copy(s["dsum"], s["dgot"], rsem.at[r_d]).start()

    lo_half(c)

    d_scaled = hdot(
        jnp.concatenate(mixes, axis=0), jnp.concatenate([dy0, dy1], axis=0), TN
    )
    d_xconv = skip * d_state + d_scaled * step
    d_x = conv_back(d_xconv * (x_sig * (1.0 + x_pre * (1.0 - x_sig))), taps_x)
    s["dx"][0] = d_x.astype(BF)
    x_mb = to_mb(s["dx"])
    through = d_scaled * x_conv
    d_raws = []
    for e in range(2):
        mine = low if e == 0 else lane >= 64
        gap_grad = d_mix[e] * mixes[e]
        d_cum = jnp.sum(gap_grad - jnp.transpose(gap_grad), axis=1, keepdims=True)
        back = hdot(tri, jnp.broadcast_to(d_cum, (T, 128)), TN)
        d_step = jnp.sum(jnp.where(mine, through, 0.0), axis=1, keepdims=True) + rates[e] * back
        d_raws.append(d_step * sigmoid(raws[e]))

    got(lo1)
    for k in range(2):
        stage1_merge(slo, k, None)
    lo2 = go(stage2_copies(slo, 0) + stage2_copies(slo, 1))

    wait_all(s["dgot"], rsem.at[r_d])
    got(cog2)
    cog3 = go(gather3(a_o, slice(4, 7)))
    d_act = jnp.transpose(
        jnp.concatenate([s["dgot"][...], jnp.zeros((96, 128), F32)], axis=0)
    )
    d_bc = conv_back(d_act * (bc_sig * (1.0 + bc_pre * (1.0 - bc_sig))), taps_bc)
    d2 = jnp.where(lane == 32, d_raws[0], jnp.where(lane == 33, d_raws[1], d_bc))
    d2_b = d2.astype(BF)
    s["d2"][0] = jnp.transpose(d2)[0:48].astype(BF)
    d2_mb = to_mb(s["d2"])

    d_proj = jnp.concatenate([s["dx"][0], s["dz"][0]], axis=1)

    def ig_half(cc, k):
        for q in (k, 2 + k):
            def one(i, _):
                at = pl.ds(pl.multiple_of(q * 1024 + i * 256 + cc * 128, 128), 128)
                v = bdot(d_proj, s["wxz"][at, :], NT) + bdot(d2_b, s["w2"][:, at], NN)
                sig["p"][q, i, cc] = v.astype(BF).reshape(2, 4, 16, 128)
                return 0
            lax.fori_loop(0, 4, one, 0, unroll=True)

    ig1, ig2, ig3, ig4 = [], [], [], []
    for k in range(2):
        ig_half(1 - c, k)
        ig1.append(go(stage1_copies(sig, k)))
    for k in range(2):
        ig_half(c, k)
    for k in range(2):
        got(ig1[k])
        stage1_merge(sig, k, None)
        ig2.append(go(stage2_copies(sig, k)))
    got(n_mb)
    got(cog3)
    nm_all = s["nm"][...].reshape(512, 128)

    def grad_out(i, _):
        yy, cc = i // 2, i % 2
        lhs = jnp.concatenate(
            [a_o[m, yy, cc].reshape(128, 128)] + [a_o[k, yy, cc].reshape(128, 128) for k in range(4, 7)], axis=0
        )
        go_out[pl.ds(pl.multiple_of(i * 128, 128), 128), :] = bdot(lhs, nm_all, TN).astype(BF)
        return 0

    lax.fori_loop(0, 8, grad_out, 0, unroll=4)

    def stage4(b, k):
        return [([(b["t"].at[q, 1 - zh], b["r4"].at[q], other_zh, m) for q in (k, 2 + k)], b["r4"].at[0:2])]

    def stage5(b, t):
        t["v"][...] = (b["t"][:, zh].astype(F32) + b["r4"][...].astype(F32)).reshape(64, 128)
        for q in range(4):
            for tt in range(2):
                t["g"][pl.ds(q * 2 + tt, 8, stride=8), :] = t["v"][pl.ds(q * 16 + tt, 8, stride=2), :]
        return go(trade(t))

    def finish(t, out):
        for k in range(8):
            for q in range(4):
                at = q * 1024 + k * 128
                out[:, at:at + 128] = t["r"][k * 8 + q * 2:k * 8 + q * 2 + 2, :].astype(BF)

    for k in range(2):
        got(ig2[k])
        stage2_merge(sig, k, None)
        ig3.append(go(stage3_copies(sig, k)))
    got(lo2)
    for k in range(2):
        stage2_merge(slo, k, None)
    lo3 = go(stage3_copies(slo, 0) + stage3_copies(slo, 1))
    got(x_mb)
    got(z_mb)
    got(d2_mb)
    got(cxg3)
    d_all = jnp.concatenate(
        [s["dx"][...].reshape(512, 128), s["dz"][...].reshape(512, 128)], axis=1
    )
    d2_all = jnp.concatenate([s["d2"][k] for k in range(4)], axis=1)

    def grad_in(i, _):
        yy, cc, k = i // 2, i % 2, i % 2
        lhs = jnp.concatenate(
            [a_x[m, yy, cc].reshape(128, 128)] + [a_x[k_, yy, cc].reshape(128, 128) for k_ in range(4, 7)], axis=0
        )
        r = bdot(lhs, d_all, TN)
        s["gf"][k, pl.ds(0, 128, stride=2), :] = r[:, 0:128]
        s["gf"][k, pl.ds(1, 128, stride=2), :] = r[:, 128:256]
        gin_out[pl.ds(pl.multiple_of(i * 256, 256), 256), :] = s["gf"][k].astype(BF)
        small = bdot(d2_all, lhs, NN)
        at = pl.ds(pl.multiple_of(i * 128, 128), 128)
        gbc_out[:, at] = small[0:32].astype(BF)
        gdt_out[:, at] = small[32:34].astype(BF)
        return 0

    lax.fori_loop(0, 4, grad_in, 0)
    for k in range(2):
        got(ig3[k])
        stage3_merge(sig, k, None)
        ig4.append(go(stage4(sig, k)))
    got(lo3)
    for k in range(2):
        stage3_merge(slo, k, None)
    lo4 = go(stage4(slo, 0) + stage4(slo, 1))
    lax.fori_loop(4, 8, grad_in, 0)
    for k in range(2):
        got(ig4[k])
    ig5 = stage5(sig, s["tig"])
    got(lo4)
    lo5 = stage5(slo, s["tlo"])
    got(ig5)
    finish(s["tig"], ig_out)
    got(lo5)
    finish(s["tlo"], lo_out)

    for whole, i in sent:
        wait_all(whole, ssem.at[i])
    @pl.when(target != h)
    def _():
        wait_all(s["ss"], ssem.at[i_bc])

    @pl.when(source != h)
    def _():
        wait_all(s["dsum"], ssem.at[i_d])

    assert rids.used <= N_RECV and sids.used <= N_SEND, (rids.used, sids.used)


def place_kernel(*refs):
    for source, result in zip(refs[:6], refs[6:]):
        result[...] = source[...]


def per_device(
    arrivals, owners, doc_lengths, w_in, w_bc, w_dt, conv_x, conv_bc, dt_bias, a_log, skip_scale,
    norm_gain, w_out, out_grad,
):
    smem = pl.BlockSpec(memory_space=pltpu.SMEM)
    vmem = pl.BlockSpec(memory_space=pltpu.VMEM)
    hbm = pl.BlockSpec(memory_space=pl.ANY)
    sds = jax.ShapeDtypeStruct
    shapes = (
        sds((2, 4096), BF), sds((2, 4096), BF), sds((2048, 128), BF), sds((32, 1024), BF),
        sds((2, 1024), BF), sds((1024, 128), BF),
    )
    made = pl.pallas_call(
        mixer_kernel,
        out_shape=shapes,
        in_specs=[smem] * 5 + [vmem] * 5 + [hbm] * 4,
        out_specs=(vmem,) * 6,
        scratch_shapes=[SCRATCH],
        compiler_params=pltpu.CompilerParams(
            collective_id=0, has_side_effects=True, vmem_limit_bytes=56 * 1024 * 1024
        ),
    )(
        owners, doc_lengths, dt_bias, a_log, skip_scale, conv_x, conv_bc,
        norm_gain.reshape(1, 128), w_dt, out_grad.reshape(2, 4096),
        arrivals.reshape(T, 4096), w_in.reshape(8192, 128), w_bc, w_out,
    )
    lo, ig, gin, gbc, gdt, gout = pl.pallas_call(
        place_kernel,
        out_shape=shapes,
        in_specs=[vmem] * 6,
        out_specs=(vmem,) * 6,
    )(*made)
    return (
        lo[None], ig[None], gin.reshape(1024, 2, 128), gbc.T, gdt.T, gout,
    )


def solution(mesh):
    return jax.shard_map(
        per_device,
        mesh=mesh,
        in_specs=(
            P("mb", "head", None, None),
            P("mb"),
            P("mb", None),
            P(None, None, "head"),
            P("head", None),
            P("head", None),
            P(None, "head"),
            P(None, "head"),
            P("head"),
            P("head"),
            P("head"),
            P("head"),
            P("head", None),
            P("mb", "head", None),
        ),
        out_specs=(
            P("mb", "head", None),
            P("mb", "head", None),
            P("mb", None, "head"),
            P("mb", "head"),
            P("mb", "head"),
            P("mb", "head"),
        ),
        check_vma=False,
    )
```

```python
import jax
import jax.numpy as jnp
from jax import lax
from jax.experimental import pallas as pl
from jax.experimental.pallas import tpu as pltpu
from jax.sharding import PartitionSpec as P

T = 128
EPS = 1e-05
WIDTH = 1024
HI = lax.Precision.HIGHEST
MESH = pl.DeviceIdType.MESH
BF = jnp.bfloat16
F32 = jnp.float32


def sigmoid(v):
    return 1.0 / (1.0 + jnp.exp(-v))


def hdot(a, b, dims):
    return lax.dot_general(a, b, (dims, ((), ())), precision=HI, preferred_element_type=F32)


def bdot(a, b, dims):
    return lax.dot_general(a, b, (dims, ((), ())), preferred_element_type=F32)


NN = ((1,), (0,))
NT = ((1,), (1,))
TN = ((0,), (0,))


class Ids:
    def __init__(self):
        self.used = 0

    def take(self, count):
        first = self.used
        self.used += count
        return first


def staged(last):
    return dict(
        p=pltpu.VMEM((4, 4, 2, 2, 4, 16, 128), BF),
        r1=pltpu.VMEM((4, 4, 2, 4, 16, 128), BF),
        q=pltpu.VMEM((4, 4, 2, 4, 16, 128), BF),
        r2x=pltpu.VMEM((2, 3, 4, 2, 16, 128), BF),
        r2y=pltpu.VMEM((2, 3, 2, 4, 16, 128), BF),
        qx=pltpu.VMEM((2, 4, 2, 16, 128), BF),
        qy=pltpu.VMEM((2, 2, 4, 16, 128), BF),
        r3x=pltpu.VMEM((2, 3, 2, 16, 128), BF),
        r3y=pltpu.VMEM((2, 3, 2, 16, 128), BF),
        t=pltpu.VMEM((4, 2, 16, 128), BF),
        r4=pltpu.VMEM(last, BF),
    )


def rows_trade():
    return dict(
        v=pltpu.VMEM((64, 128), F32), g=pltpu.VMEM((64, 128), F32), r=pltpu.VMEM((64, 128), F32)
    )


N_RECV = 79
N_SEND = 79

SCRATCH = dict(
    arr=pltpu.VMEM((T, 4096), BF),
    win=pltpu.VMEM((8192, 128), BF),
    wf=pltpu.VMEM((2, 512, 128), F32),
    wxz=pltpu.VMEM((4096, 256), BF),
    w2=pltpu.VMEM((128, 4096), BF),
    wdtf=pltpu.VMEM((16, 4096), F32),
    wout=pltpu.VMEM((128, 4096), BF),
    cbc=pltpu.VMEM((8, 128), F32),
    ax=pltpu.VMEM((7, 4, 2, 2, 4, 16, 128), BF),
    ao=pltpu.VMEM((7, 4, 2, 2, 4, 16, 128), BF),
    x=pltpu.VMEM((T, 4096), BF),
    o=pltpu.VMEM((T, 4096), BF),
    ss=pltpu.VMEM((32, 128), BF),
    bc=pltpu.VMEM((8, 32, 128), BF),
    norm=pltpu.VMEM((8, 8, 128), F32),
    dbcs=pltpu.VMEM((8, 32, 128), BF),
    dbcr=pltpu.VMEM((8, 32, 128), BF),
    dsum=pltpu.VMEM((32, 128), F32),
    dgot=pltpu.VMEM((32, 128), F32),
    dx=pltpu.VMEM((4, 128, 128), BF),
    dz=pltpu.VMEM((4, 128, 128), BF),
    nm=pltpu.VMEM((4, 128, 128), BF),
    d2=pltpu.VMEM((4, 48, 128), BF),
    gf=pltpu.VMEM((2, 256, 128), F32),
    sx=staged((4, 2, 16, 128)),
    slo=staged((4, 16, 128)),
    sig=staged((4, 16, 128)),
    tog=rows_trade(),
    tlo=rows_trade(),
    tig=rows_trade(),
    ssem=pltpu.SemaphoreType.DMA((N_SEND,)),
    rsem=pltpu.SemaphoreType.DMA((N_RECV,)),
    lsem=pltpu.SemaphoreType.DMA((8,)),
)


def mixer_kernel(
    own_ref, doc_ref, dtb_ref, alog_ref, skip_ref, cx_ref, cbc_ref, gain_ref, wdt_ref, og_ref,
    arr_hbm, win_hbm, wbc_hbm, wout_hbm,
    lo_out, ig_out, gin_out, gbc_out, gdt_out, go_out,
    s,
):
    h = lax.axis_index("head")
    m = lax.axis_index("mb")
    zh = h // 32
    x = (h // 8) % 4
    y = (h // 2) % 4
    c = h % 2
    j = h % 8
    g = h // 8
    g_t = (h % 32) // 4
    part = zh * 4 + h % 4
    ssem, rsem, lsem = s["ssem"], s["rsem"], s["lsem"]
    rids, sids = Ids(), Ids()
    sent = []

    def head_of(zh_, x_, y_, c_):
        return zh_ * 32 + x_ * 8 + y_ * 2 + c_

    def copy(src, dst, i, r, head, mb):
        return pltpu.make_async_remote_copy(
            src_ref=src, dst_ref=dst, send_sem=ssem.at[i], recv_sem=rsem.at[r],
            device_id=(head, mb), device_id_type=MESH,
        )

    def wait_all(ref, sem):
        pltpu.make_async_copy(ref, ref, sem).wait()

    def go(groups):
        waits = []
        for copies, whole in groups:
            i, r = sids.take(1), rids.take(1)
            for src, dst, head, mb in copies:
                copy(src, dst, i, r, head, mb).start()
            waits.append((whole, r))
            sent.append((whole, i))
        return waits

    def got(waits):
        for whole, r in waits:
            wait_all(whole, rsem.at[r])

    loc = [
        pltpu.make_async_copy(arr_hbm, s["arr"], lsem.at[0]),
        pltpu.make_async_copy(win_hbm, s["win"], lsem.at[1]),
        pltpu.make_async_copy(wbc_hbm, s["w2"].at[0:32], lsem.at[2]),
        pltpu.make_async_copy(wout_hbm, s["wout"], lsem.at[3]),
    ]
    for cp in loc:
        cp.start()

    barrier = pltpu.get_barrier_semaphore()
    count = 0
    peers = [(head_of(zh, x, y, 1 - c), m), (head_of(1 - zh, x, y, c), m)]
    for d in range(1, 4):
        peers.append((head_of(zh, (x + d) % 4, y, c), m))
        peers.append((h, (m + d) % 4))
    for d in range(1, 8):
        peers.append((8 * g + (j + d) % 8, m))
    for head, mb in peers:
        pl.semaphore_signal(barrier, inc=1, device_id=(head, mb), device_id_type=MESH)
        count += 1
    target = 8 * g_t + part
    source = 4 * g + j + 28 * (j // 4)
    for head in (target, source):
        pl.semaphore_signal(barrier, inc=1, device_id=(head, m), device_id_type=MESH)
        count += 1

    s["cbc"][...] = jnp.zeros((8, 128), F32)
    s["cbc"][0:4, 0:32] = cbc_ref[...]
    s["wdtf"][...] = jnp.zeros((16, 4096), F32)
    s["wdtf"][0:2, :] = wdt_ref[...].astype(F32)
    s["w2"][32:48, :] = s["wdtf"][...].astype(BF)
    s["w2"][48:128, :] = jnp.zeros((80, 4096), BF)

    sx = s["sx"]
    loc[0].wait()

    def split_arr(i, _):
        v = s["arr"][:, pl.ds(pl.multiple_of(i * 256, 256), 256)]
        for cc in range(2):
            sx["p"][i // 4, i % 4, cc] = v[:, cc * 128:(cc + 1) * 128].reshape(2, 4, 16, 128)
        return 0

    lax.fori_loop(0, 16, split_arr, 0, unroll=4)
    pl.semaphore_wait(barrier, count)

    owner = own_ref[0]
    o_zh, o_x, o_y, o_c = owner // 32, (owner // 8) % 4, (owner // 2) % 4, owner % 2

    def combine(own, received, picks):
        if picks is None:
            total = own.astype(F32)
            for v in received:
                total = total + v.astype(F32)
            return total
        value = own
        for v, pick in zip(received, picks):
            value = lax.select(pick, v, value)
        return value

    def stage1_copies(b, k):
        head = head_of(zh, x, y, 1 - c)
        return [([(b["p"].at[q, :, 1 - c], b["r1"].at[q], head, m) for q in (k, 2 + k)], b["r1"].at[0:2])]

    def stage1_merge(b, k, picks):
        for q in (k, 2 + k):
            b["q"][q] = combine(b["p"][q, :, c], [b["r1"][q]], picks and picks["c"]).astype(BF)

    def stage2_copies(b, k):
        along_x, along_y = [], []
        for d in range(1, 4):
            x2, y2 = (x + d) % 4, (y + d) % 4
            along_x.append((b["q"].at[k, :, :, x2], b["r2x"].at[k, d - 1], head_of(zh, x2, y, c), m))
            along_y.append((b["q"].at[2 + k, y2], b["r2y"].at[k, d - 1], head_of(zh, x, y2, c), m))
        return [(along_x, b["r2x"].at[k]), (along_y, b["r2y"].at[k])]

    def stage2_merge(b, k, picks):
        b["qx"][k] = combine(b["q"][k, :, :, x], [b["r2x"][k, d] for d in range(3)], picks and picks["x"]).astype(BF)
        b["qy"][k] = combine(b["q"][2 + k, y], [b["r2y"][k, d] for d in range(3)], picks and picks["y"]).astype(BF)

    def stage3_copies(b, k):
        along_x, along_y = [], []
        for d in range(1, 4):
            x2, y2 = (x + d) % 4, (y + d) % 4
            along_y.append((b["qx"].at[k, y2], b["r3x"].at[k, d - 1], head_of(zh, x, y2, c), m))
            along_x.append((b["qy"].at[k, :, x2], b["r3y"].at[k, d - 1], head_of(zh, x2, y, c), m))
        return [(along_y, b["r3x"].at[k]), (along_x, b["r3y"].at[k])]

    def stage3_merge(b, k, picks):
        b["t"][k] = combine(b["qx"][k, y], [b["r3x"][k, d] for d in range(3)], picks and picks["y"]).astype(BF)
        b["t"][2 + k] = combine(b["qy"][k, :, x], [b["r3y"][k, d] for d in range(3)], picks and picks["x"]).astype(BF)

    other_zh = head_of(1 - zh, x, y, c)

    def gather1(a, s1, s2):
        along_x, along_y = [], []
        r1, r2 = a.at[s1, y, c, :, x], a.at[s2, y, c, :, x]
        for d in range(1, 4):
            x2, y2 = (x + d) % 4, (y + d) % 4
            along_y.append((r1, r1, head_of(zh, x, y2, c), m))
            along_x.append((r2, r2, head_of(zh, x2, y, c), m))
        return [(along_y, a.at[s1, 0:3, c, :, x]), (along_x, a.at[s2, y, c, :, 0:3])]

    def gather2(a, s1, s2):
        along_x, along_y = [], []
        r1, r2 = a.at[s1, :, c, :, x], a.at[s2, y, c]
        for d in range(1, 4):
            x2, y2 = (x + d) % 4, (y + d) % 4
            along_x.append((r1, r1, head_of(zh, x2, y, c), m))
            along_y.append((r2, r2, head_of(zh, x, y2, c), m))
        return [(along_x, a.at[s1, :, c, :, 0:3]), (along_y, a.at[s2, 0:3, c])]

    def gather3(a, part_of):
        ref = a.at[part_of, :, c]
        return [([(ref, ref, head_of(zh, x, y, 1 - c), m)], ref)]

    def trade(b):
        cps = []
        for d in range(1, 8):
            k = (j + d) % 8
            src = b["g"].at[pl.ds(pl.multiple_of(k * 8, 8), 8)]
            dst = b["r"].at[pl.ds(pl.multiple_of(j * 8, 8), 8)]
            cps.append((src, dst, 8 * g + k, m))
        mine = pl.ds(pl.multiple_of(j * 8, 8), 8)
        b["r"][mine, :] = b["g"][mine, :]
        return [(cps, b["r"].at[0:56])]

    lane = lax.broadcasted_iota(jnp.int32, (T, 128), 1)
    row = lax.broadcasted_iota(jnp.int32, (T, 128), 0)

    def unpack_weights(first, last):
        def one(i, _):
            k = i % 2
            s["wf"][k] = s["win"][pl.ds(pl.multiple_of(i * 512, 512), 512), :].astype(F32)
            at = pl.ds(pl.multiple_of(i * 256, 256), 256)
            s["wxz"][at, 0:128] = s["wf"][k, pl.ds(0, 256, stride=2), :].astype(BF)
            s["wxz"][at, 128:256] = s["wf"][k, pl.ds(1, 256, stride=2), :].astype(BF)
            return 0
        lax.fori_loop(first, last, one, 0)

    picks = dict(
        c=[o_c != c],
        x=[o_x == (x + 4 - d) % 4 for d in range(1, 4)],
        y=[o_y == (y + 4 - d) % 4 for d in range(1, 4)],
    )
    a_x, a_o = s["ax"], s["ao"]
    x1 = [go(stage1_copies(sx, k)) for k in range(2)]
    tog = s["tog"]
    og = og_ref[...].astype(F32)
    for k in range(8):
        for q in range(4):
            tog["g"][k * 8 + q * 2:k * 8 + q * 2 + 2, :] = og[:, q * 1024 + k * 128:q * 1024 + k * 128 + 128]
    o1 = go(trade(tog))
    x2 = []
    for k in range(2):
        got(x1[k])
        stage1_merge(sx, k, picks)
        x2.append(go(stage2_copies(sx, k)))
    got(o1)
    for q in range(4):
        for tt in range(2):
            tog["v"][pl.ds(q * 16 + tt, 8, stride=2), :] = tog["r"][pl.ds(q * 2 + tt, 8, stride=8), :]
    a_o[0:4, y, c, zh, x] = tog["v"][...].reshape(4, 16, 128).astype(BF)
    cps = []
    for d in range(1, 4):
        m2 = (m + d) % 4
        cps.append((a_o.at[m2, y, c, zh, x], a_o.at[7 - d, y, c, zh, x], h, m2))
    oc = go([(cps, a_o.at[4:7, y, c, zh, x])])
    oz_ref = a_o.at[0:4, y, c, zh, x]
    oz = go([([(oz_ref, oz_ref, other_zh, m)], oz_ref)])
    loc[1].wait()
    unpack_weights(0, 3)
    got(oz)
    q01, q23 = slice(0, 2), slice(2, 4)
    og1 = go(gather1(a_o, q01, q23))
    x3 = []
    for k in range(2):
        got(x2[k])
        stage2_merge(sx, k, picks)
        x3.append(go(stage3_copies(sx, k)))
    unpack_weights(3, 6)
    x4 = []
    for k in range(2):
        got(x3[k])
        stage3_merge(sx, k, picks)
        x4.append(go([([(sx["t"].at[q], sx["r4"].at[q], other_zh, m) for q in (k, 2 + k)], sx["r4"].at[0:2])]))
    got(og1)
    og2 = go(gather2(a_o, q01, q23))
    got(oc)
    ocz_ref = a_o.at[4:7, y, c, zh, x]
    ocz = go([([(ocz_ref, ocz_ref, other_zh, m)], ocz_ref)])
    unpack_weights(6, 9)
    xg1, xg2, xg3 = [], [], []
    first = [slice(k, k + 1) for k in range(2)]
    second = [slice(2 + k, 3 + k) for k in range(2)]
    for k in range(2):
        got(x4[k])
        for q in (k, 2 + k):
            a_x[q, y, c, :, x] = combine(sx["t"][q], [sx["r4"][q]], [o_zh != zh])
        xg1.append(go(gather1(a_x, first[k], second[k])))
    cps = []
    for d in range(1, 4):
        m2 = (m + d) % 4
        cps.append((a_x.at[m2, y, c, :, x], a_x.at[7 - d, y, c, :, x], h, m2))
    xc = go([(cps, a_x.at[4:7, y, c, :, x])])
    k1, k2 = slice(4, 5), slice(5, 7)
    l1, l2 = slice(4, 6), slice(6, 7)
    got(ocz)
    cog1 = go(gather1(a_o, l1, l2))
    unpack_weights(9, 12)
    for k in range(2):
        got(xg1[k])
        xg2.append(go(gather2(a_x, first[k], second[k])))
    got(xc)
    cxg1 = go(gather1(a_x, k1, k2))
    got(og2)
    og3 = go(gather3(a_o, slice(0, 4)))
    unpack_weights(12, 16)
    for k in range(2):
        got(xg2[k])
        xg3.append(go(gather3(a_x, first[k]) + gather3(a_x, second[k])))
    got(cog1)
    cog2 = go(gather2(a_o, l1, l2))

    def assemble(a, dst, cc, q):
        def one(i, _):
            at = pl.ds(pl.multiple_of(q * 1024 + i * 256 + cc * 128, 128), 128)
            dst[:, at] = a[q, i, cc].reshape(128, 128)
            return 0
        lax.fori_loop(0, 4, one, 0, unroll=True)

    for q in range(4):
        assemble(a_x, s["x"], c, q)
    loc[2].wait()
    p2 = jnp.zeros((T, 128), F32)
    for k in range(2):
        got(xg3[k])
        for q in (k, 2 + k):
            assemble(a_x, s["x"], 1 - c, q)
            at = slice(q * 1024, (q + 1) * 1024)
            p2 = p2 + bdot(s["x"][:, at], s["w2"][:, at], NT)

    e1 = doc_ref[0, 0]
    e2 = e1 + doc_ref[0, 1]
    e3 = e2 + doc_ref[0, 2]
    e4 = e3 + doc_ref[0, 3]

    def doc_of(t):
        return sum((t >= e).astype(jnp.int32) for e in (e1, e2, e3, e4))

    doc_row = doc_of(row)
    same = [None] + [(row >= o) & (doc_of(row - o) == doc_row) for o in range(1, 4)]
    visible = (row >= lane) & (doc_row == doc_of(lane))

    def conv(v, taps):
        result = v * taps[3:4]
        for o in range(1, 4):
            result = result + jnp.where(same[o], pltpu.roll(v, o, 0), 0.0) * taps[3 - o:4 - o]
        return result

    def conv_back(d, taps):
        result = d * taps[3:4]
        for o in range(1, 4):
            result = result + pltpu.roll(jnp.where(same[o], d, 0.0), T - o, 0) * taps[3 - o:4 - o]
        return result

    taps_bc = s["cbc"][...]
    bc_pre = conv(p2, taps_bc)
    bc_sig = sigmoid(bc_pre)
    s["ss"][...] = jnp.transpose(bc_pre * bc_sig)[0:32].astype(BF)
    i_bc, r_bc = sids.take(1), rids.take(1)

    @pl.when(target != h)
    def _():
        copy(s["ss"], s["bc"].at[part], i_bc, r_bc, target, m).start()

    @pl.when(target == h)
    def _():
        pltpu.make_async_copy(s["ss"], s["bc"].at[part], rsem.at[r_bc]).start()

    wait_all(s["bc"].at[j], rsem.at[r_bc])
    peers_of = [8 * g + (j + d) % 8 for d in range(1, 8)]
    bcp = go([([(s["bc"].at[j], s["bc"].at[j], head, m) for head in peers_of], s["bc"].at[0:7])])

    got(cxg1)
    cxg2 = go(gather2(a_x, k1, k2))
    got(cog2)
    cog3 = go(gather3(a_o, slice(4, 7)))

    pxz = bdot(s["x"][...], s["wxz"][...], NN)
    z = pxz[:, 128:256]
    taps_x = cx_ref[...]
    x_pre = conv(pxz[:, 0:128], taps_x)
    x_sig = sigmoid(x_pre)
    x_conv = x_pre * x_sig
    z_sig = sigmoid(z)
    z_silu = z * z_sig
    low = lane < 64
    tri = jnp.where(row >= lane, 1.0, 0.0)
    raws, rates, steps = [], [], []
    for e in range(2):
        raw = jnp.broadcast_to(p2[:, 32 + e:33 + e], (T, 128)) + dtb_ref[e]
        raws.append(raw)
        rates.append(-jnp.exp(jnp.full((T, 128), alog_ref[e], F32)))
        steps.append(jnp.maximum(raw, 0.0) + jnp.log1p(jnp.exp(-jnp.abs(raw))))
    step = jnp.where(low, steps[0], steps[1])
    cum = hdot(tri, jnp.where(low, steps[0] * rates[0], steps[1] * rates[1]), NN)
    decays = []
    for e in range(2):
        col = jnp.broadcast_to(cum[:, 64 * e:64 * e + 1], (T, 128))
        gap = col - jnp.transpose(col)
        decays.append(jnp.where(visible, jnp.exp(jnp.where(visible, gap, 0.0)), 0.0))
    scaled = x_conv * step
    skip = jnp.where(low, skip_ref[0], skip_ref[1])

    for q in range(4):
        assemble(a_o, s["o"], c, q)
    got(og3)
    for q in range(4):
        assemble(a_o, s["o"], 1 - c, q)
    loc[3].wait()
    weighted = bdot(s["o"][...], s["wout"][...], NT) * gain_ref[...]

    got(bcp)
    b_t = s["bc"][0:4].reshape(128, 128)
    c_t = s["bc"][4:8].reshape(128, 128)
    scores = bdot(c_t, b_t, TN)
    mixes = [scores * decays[0], scores * decays[1]]
    zero = jnp.zeros((T, 128), F32)
    scaled2 = jnp.concatenate([jnp.where(low, scaled, zero), jnp.where(low, zero, scaled)], axis=0)
    state = hdot(jnp.concatenate(mixes, axis=1), scaled2, NN) + skip * x_conv
    gated = state * z_silu
    squares = jnp.sum(gated * gated, axis=1, keepdims=True)
    inners = jnp.sum(weighted * gated, axis=1, keepdims=True)
    nmat = jnp.where(lane == 0, squares, jnp.where(lane == 1, inners, 0.0))
    s["norm"][j] = jnp.transpose(nmat)[0:8]
    cps = [(s["norm"].at[j], s["norm"].at[j], head, m) for head in peers_of]
    ncp = go([(cps, s["norm"].at[0:7])])
    got(cxg2)
    cxg3 = go(gather3(a_x, slice(4, 7)))
    got(ncp)
    total = jnp.sum(s["norm"][...], axis=0)
    tcol = jnp.transpose(jnp.concatenate([total, jnp.zeros((120, 128), F32)], axis=0))
    inverse = jnp.broadcast_to(lax.rsqrt(tcol[:, 0:1] * (1.0 / WIDTH) + EPS), (T, 128))
    inner = jnp.broadcast_to(tcol[:, 1:2] * (1.0 / WIDTH), (T, 128))
    normed = (gated * inverse * gain_ref[...]).astype(BF)
    s["nm"][0] = normed
    d_gated = inverse * weighted - gated * (inverse * inverse * inverse * inner)

    d_state = d_gated * z_silu
    d_z = d_gated * state * (z_sig * (1.0 + z * (1.0 - z_sig)))
    s["dz"][0] = d_z.astype(BF)
    dy0, dy1 = jnp.where(low, d_state, zero), jnp.where(low, zero, d_state)
    d_mix = [hdot(dy0, scaled, NT), hdot(dy1, scaled, NT)]
    d_scores = d_mix[0] * decays[0] + d_mix[1] * decays[1]
    s["dbcs"][0:4] = hdot(c_t.astype(F32), d_scores, NN).reshape(4, 32, 128).astype(BF)
    s["dbcs"][4:8] = hdot(b_t.astype(F32), d_scores, NT).reshape(4, 32, 128).astype(BF)
    s["dbcr"][j] = s["dbcs"][j]
    cps = [(s["dbcs"].at[(j + d) % 8], s["dbcr"].at[j], 8 * g + (j + d) % 8, m) for d in range(1, 8)]
    dbc = go([(cps, s["dbcr"].at[0:7])])

    def to_mb(ref):
        cps = [(ref.at[0], ref.at[4 - d], h, (m + d) % 4) for d in range(1, 4)]
        return go([(cps, ref.at[1:4])])

    n_mb = to_mb(s["nm"])
    z_mb = to_mb(s["dz"])

    slo, sig = s["slo"], s["sig"]

    def lo_half(cc):
        def one(i, _):
            at = pl.ds(pl.multiple_of(i * 256 + cc * 128, 128), 128)
            v = bdot(normed, s["wout"][:, at], NN)
            slo["p"][i // 4, i % 4, cc] = v.astype(BF).reshape(2, 4, 16, 128)
            return 0
        lax.fori_loop(0, 16, one, 0, unroll=8)

    lo_half(1 - c)
    lo1 = go(stage1_copies(slo, 0) + stage1_copies(slo, 1))
    got(dbc)
    s["dsum"][...] = jnp.sum(s["dbcr"][...].astype(F32), axis=0)
    i_d, r_d = sids.take(1), rids.take(1)

    @pl.when(source != h)
    def _():
        copy(s["dsum"], s["dgot"], i_d, r_d, source, m).start()

    @pl.when(source == h)
    def _():
        pltpu.make_async_copy(s["dsum"], s["dgot"], rsem.at[r_d]).start()

    lo_half(c)

    d_scaled = hdot(
        jnp.concatenate(mixes, axis=0), jnp.concatenate([dy0, dy1], axis=0), TN
    )
    d_xconv = skip * d_state + d_scaled * step
    d_x = conv_back(d_xconv * (x_sig * (1.0 + x_pre * (1.0 - x_sig))), taps_x)
    s["dx"][0] = d_x.astype(BF)
    x_mb = to_mb(s["dx"])
    through = d_scaled * x_conv
    d_raws = []
    for e in range(2):
        mine = low if e == 0 else lane >= 64
        gap_grad = d_mix[e] * mixes[e]
        d_cum = jnp.sum(gap_grad - jnp.transpose(gap_grad), axis=1, keepdims=True)
        back = hdot(tri, jnp.broadcast_to(d_cum, (T, 128)), TN)
        d_step = jnp.sum(jnp.where(mine, through, 0.0), axis=1, keepdims=True) + rates[e] * back
        d_raws.append(d_step * sigmoid(raws[e]))

    got(lo1)
    for k in range(2):
        stage1_merge(slo, k, None)
    lo2 = go(stage2_copies(slo, 0) + stage2_copies(slo, 1))

    wait_all(s["dgot"], rsem.at[r_d])
    d_act = jnp.transpose(
        jnp.concatenate([s["dgot"][...], jnp.zeros((96, 128), F32)], axis=0)
    )
    d_bc = conv_back(d_act * (bc_sig * (1.0 + bc_pre * (1.0 - bc_sig))), taps_bc)
    d2 = jnp.where(lane == 32, d_raws[0], jnp.where(lane == 33, d_raws[1], d_bc))
    d2_b = d2.astype(BF)
    s["d2"][0] = jnp.transpose(d2)[0:48].astype(BF)
    d2_mb = to_mb(s["d2"])

    d_proj = jnp.concatenate([s["dx"][0], s["dz"][0]], axis=1)

    def ig_half(cc, k):
        for q in (k, 2 + k):
            def one(i, _):
                at = pl.ds(pl.multiple_of(q * 1024 + i * 256 + cc * 128, 128), 128)
                v = bdot(d_proj, s["wxz"][at, :], NT) + bdot(d2_b, s["w2"][:, at], NN)
                sig["p"][q, i, cc] = v.astype(BF).reshape(2, 4, 16, 128)
                return 0
            lax.fori_loop(0, 4, one, 0, unroll=True)

    ig1, ig2, ig3, ig4 = [], [], [], []
    for k in range(2):
        ig_half(1 - c, k)
        ig1.append(go(stage1_copies(sig, k)))
    for k in range(2):
        ig_half(c, k)
    for k in range(2):
        got(ig1[k])
        stage1_merge(sig, k, None)
        ig2.append(go(stage2_copies(sig, k)))
    got(n_mb)
    got(cog3)
    nm_all = s["nm"][...].reshape(512, 128)

    def grad_out(i, _):
        yy, cc = i // 2, i % 2
        lhs = jnp.concatenate(
            [a_o[m, yy, cc].reshape(128, 128)] + [a_o[k, yy, cc].reshape(128, 128) for k in range(4, 7)], axis=0
        )
        go_out[pl.ds(pl.multiple_of(i * 128, 128), 128), :] = bdot(lhs, nm_all, TN).astype(BF)
        return 0

    lax.fori_loop(0, 8, grad_out, 0, unroll=4)

    def stage4(b, k):
        return [([(b["t"].at[q, 1 - zh], b["r4"].at[q], other_zh, m) for q in (k, 2 + k)], b["r4"].at[0:2])]

    def stage5(b, t):
        t["v"][...] = (b["t"][:, zh].astype(F32) + b["r4"][...].astype(F32)).reshape(64, 128)
        for q in range(4):
            for tt in range(2):
                t["g"][pl.ds(q * 2 + tt, 8, stride=8), :] = t["v"][pl.ds(q * 16 + tt, 8, stride=2), :]
        return go(trade(t))

    def finish(t, out):
        for k in range(8):
            for q in range(4):
                at = q * 1024 + k * 128
                out[:, at:at + 128] = t["r"][k * 8 + q * 2:k * 8 + q * 2 + 2, :].astype(BF)

    for k in range(2):
        got(ig2[k])
        stage2_merge(sig, k, None)
        ig3.append(go(stage3_copies(sig, k)))
    got(lo2)
    for k in range(2):
        stage2_merge(slo, k, None)
    lo3 = go(stage3_copies(slo, 0) + stage3_copies(slo, 1))
    got(x_mb)
    got(z_mb)
    got(d2_mb)
    got(cxg3)
    d_all = jnp.concatenate(
        [s["dx"][...].reshape(512, 128), s["dz"][...].reshape(512, 128)], axis=1
    )
    d2_all = jnp.concatenate([s["d2"][k] for k in range(4)], axis=1)

    def grad_in(i, _):
        yy, cc, k = i // 2, i % 2, i % 2
        lhs = jnp.concatenate(
            [a_x[m, yy, cc].reshape(128, 128)] + [a_x[k_, yy, cc].reshape(128, 128) for k_ in range(4, 7)], axis=0
        )
        r = bdot(lhs, d_all, TN)
        s["gf"][k, pl.ds(0, 128, stride=2), :] = r[:, 0:128]
        s["gf"][k, pl.ds(1, 128, stride=2), :] = r[:, 128:256]
        gin_out[pl.ds(pl.multiple_of(i * 256, 256), 256), :] = s["gf"][k].astype(BF)
        small = bdot(d2_all, lhs, NN)
        at = pl.ds(pl.multiple_of(i * 128, 128), 128)
        gbc_out[:, at] = small[0:32].astype(BF)
        gdt_out[:, at] = small[32:34].astype(BF)
        return 0

    lax.fori_loop(0, 4, grad_in, 0)
    for k in range(2):
        got(ig3[k])
        stage3_merge(sig, k, None)
        ig4.append(go(stage4(sig, k)))
    got(lo3)
    for k in range(2):
        stage3_merge(slo, k, None)
    lo4 = go(stage4(slo, 0) + stage4(slo, 1))
    lax.fori_loop(4, 8, grad_in, 0)
    for k in range(2):
        got(ig4[k])
    ig5 = stage5(sig, s["tig"])
    got(lo4)
    lo5 = stage5(slo, s["tlo"])
    got(ig5)
    finish(s["tig"], ig_out)
    got(lo5)
    finish(s["tlo"], lo_out)

    for whole, i in sent:
        wait_all(whole, ssem.at[i])
    @pl.when(target != h)
    def _():
        wait_all(s["ss"], ssem.at[i_bc])

    @pl.when(source != h)
    def _():
        wait_all(s["dsum"], ssem.at[i_d])

    assert rids.used <= N_RECV and sids.used <= N_SEND, (rids.used, sids.used)


def place_kernel(*refs):
    for source, result in zip(refs[:6], refs[6:]):
        result[...] = source[...]


def per_device(
    arrivals, owners, doc_lengths, w_in, w_bc, w_dt, conv_x, conv_bc, dt_bias, a_log, skip_scale,
    norm_gain, w_out, out_grad,
):
    smem = pl.BlockSpec(memory_space=pltpu.SMEM)
    vmem = pl.BlockSpec(memory_space=pltpu.VMEM)
    hbm = pl.BlockSpec(memory_space=pl.ANY)
    sds = jax.ShapeDtypeStruct
    shapes = (
        sds((2, 4096), BF), sds((2, 4096), BF), sds((2048, 128), BF), sds((32, 1024), BF),
        sds((2, 1024), BF), sds((1024, 128), BF),
    )
    made = pl.pallas_call(
        mixer_kernel,
        out_shape=shapes,
        in_specs=[smem] * 5 + [vmem] * 5 + [hbm] * 4,
        out_specs=(vmem,) * 6,
        scratch_shapes=[SCRATCH],
        compiler_params=pltpu.CompilerParams(
            collective_id=0, has_side_effects=True, vmem_limit_bytes=56 * 1024 * 1024
        ),
    )(
        owners, doc_lengths, dt_bias, a_log, skip_scale, conv_x, conv_bc,
        norm_gain.reshape(1, 128), w_dt, out_grad.reshape(2, 4096),
        arrivals.reshape(T, 4096), w_in.reshape(8192, 128), w_bc, w_out,
    )
    lo, ig, gin, gbc, gdt, gout = pl.pallas_call(
        place_kernel,
        out_shape=shapes,
        in_specs=[vmem] * 6,
        out_specs=(vmem,) * 6,
    )(*made)
    return (
        lo[None], ig[None], gin.reshape(1024, 2, 128), gbc.T, gdt.T, gout,
    )


def solution(mesh):
    return jax.shard_map(
        per_device,
        mesh=mesh,
        in_specs=(
            P("mb", "head", None, None),
            P("mb"),
            P("mb", None),
            P(None, None, "head"),
            P("head", None),
            P("head", None),
            P(None, "head"),
            P(None, "head"),
            P("head"),
            P("head"),
            P("head"),
            P("head"),
            P("head", None),
            P("mb", "head", None),
        ),
        out_specs=(
            P("mb", "head", None),
            P("mb", "head", None),
            P("mb", None, "head"),
            P("mb", "head"),
            P("mb", "head"),
            P("mb", "head"),
        ),
        check_vma=False,
    )
```

```python
import jax
import jax.numpy as jnp
from jax import lax
from jax.experimental import pallas as pl
from jax.experimental.pallas import tpu as pltpu
from jax.sharding import PartitionSpec as P

T = 128
EPS = 1e-05
WIDTH = 1024
HI = lax.Precision.HIGHEST
MESH = pl.DeviceIdType.MESH
BF = jnp.bfloat16
F32 = jnp.float32


def sigmoid(v):
    return 1.0 / (1.0 + jnp.exp(-v))


def hdot(a, b, dims):
    return lax.dot_general(a, b, (dims, ((), ())), precision=HI, preferred_element_type=F32)


def bdot(a, b, dims):
    return lax.dot_general(a, b, (dims, ((), ())), preferred_element_type=F32)


NN = ((1,), (0,))
NT = ((1,), (1,))
TN = ((0,), (0,))


class Ids:
    def __init__(self):
        self.used = 0
        self.free = []

    def take(self, count):
        if count == 1 and self.free:
            return self.free.pop()
        first = self.used
        self.used += count
        return first


def staged(last):
    return dict(
        p=pltpu.VMEM((4, 4, 2, 2, 4, 16, 128), BF),
        r1=pltpu.VMEM((4, 4, 2, 4, 16, 128), BF),
        q=pltpu.VMEM((4, 4, 2, 4, 16, 128), BF),
        r2x=pltpu.VMEM((2, 3, 4, 2, 16, 128), BF),
        r2y=pltpu.VMEM((2, 3, 2, 4, 16, 128), BF),
        qx=pltpu.VMEM((2, 4, 2, 16, 128), BF),
        qy=pltpu.VMEM((2, 2, 4, 16, 128), BF),
        r3x=pltpu.VMEM((2, 3, 2, 16, 128), BF),
        r3y=pltpu.VMEM((2, 3, 2, 16, 128), BF),
        t=pltpu.VMEM((4, 2, 16, 128), BF),
        r4=pltpu.VMEM(last, BF),
    )


def rows_trade():
    return dict(
        v=pltpu.VMEM((64, 128), F32), g=pltpu.VMEM((64, 128), F32), r=pltpu.VMEM((64, 128), F32)
    )


N_RECV = 79
N_SEND = 48

SCRATCH = dict(
    arr=pltpu.VMEM((T, 4096), BF),
    win=pltpu.VMEM((8192, 128), BF),
    wf=pltpu.VMEM((2, 512, 128), F32),
    wxz=pltpu.VMEM((4096, 256), BF),
    w2=pltpu.VMEM((128, 4096), BF),
    wdtf=pltpu.VMEM((16, 4096), F32),
    wout=pltpu.VMEM((128, 4096), BF),
    cbc=pltpu.VMEM((8, 128), F32),
    ax=pltpu.VMEM((7, 4, 2, 2, 4, 16, 128), BF),
    ao=pltpu.VMEM((7, 4, 2, 2, 4, 16, 128), BF),
    x=pltpu.VMEM((T, 4096), BF),
    o=pltpu.VMEM((T, 4096), BF),
    ss=pltpu.VMEM((32, 128), BF),
    bc=pltpu.VMEM((8, 32, 128), BF),
    norm=pltpu.VMEM((8, 8, 128), F32),
    dbcs=pltpu.VMEM((8, 32, 128), BF),
    dbcr=pltpu.VMEM((8, 32, 128), BF),
    dsum=pltpu.VMEM((32, 128), F32),
    dgot=pltpu.VMEM((32, 128), F32),
    dx=pltpu.VMEM((4, 128, 128), BF),
    dz=pltpu.VMEM((4, 128, 128), BF),
    nm=pltpu.VMEM((4, 128, 128), BF),
    d2=pltpu.VMEM((4, 48, 128), BF),
    gin=pltpu.VMEM((2048, 128), BF),
    gout=pltpu.VMEM((1024, 128), BF),
    gf=pltpu.VMEM((2, 256, 128), F32),
    sx=staged((4, 2, 16, 128)),
    slo=staged((4, 16, 128)),
    sig=staged((4, 16, 128)),
    tog=rows_trade(),
    tlo=rows_trade(),
    tig=rows_trade(),
    ssem=pltpu.SemaphoreType.DMA((N_SEND,)),
    rsem=pltpu.SemaphoreType.DMA((N_RECV,)),
    lsem=pltpu.SemaphoreType.DMA((8,)),
)


def mixer_kernel(
    own_ref, doc_ref, dtb_ref, alog_ref, skip_ref, cx_ref, cbc_ref, gain_ref, wdt_ref, og_ref,
    arr_hbm, win_hbm, wbc_hbm, wout_hbm,
    lo_out, ig_out, gin_out, gbc_out, gdt_out, go_out,
    s,
):
    h = lax.axis_index("head")
    m = lax.axis_index("mb")
    zh = h // 32
    x = (h // 8) % 4
    y = (h // 2) % 4
    c = h % 2
    j = h % 8
    g = h // 8
    g_t = (h % 32) // 4
    part = zh * 4 + h % 4
    ssem, rsem, lsem = s["ssem"], s["rsem"], s["lsem"]
    rids, sids = Ids(), Ids()
    sent = []

    def head_of(zh_, x_, y_, c_):
        return zh_ * 32 + x_ * 8 + y_ * 2 + c_

    def copy(src, dst, i, r, head, mb):
        return pltpu.make_async_remote_copy(
            src_ref=src, dst_ref=dst, send_sem=ssem.at[i], recv_sem=rsem.at[r],
            device_id=(head, mb), device_id_type=MESH,
        )

    def wait_all(ref, sem):
        pltpu.make_async_copy(ref, ref, sem).wait()

    def go(groups):
        waits = []
        for copies, whole in groups:
            i, r = sids.take(1), rids.take(1)
            for src, dst, head, mb in copies:
                copy(src, dst, i, r, head, mb).start()
            waits.append((whole, r))
            sent.append((whole, i))
        return waits

    def flush(mark):
        for whole, i in [group for group in sent if group[1] < mark]:
            wait_all(whole, ssem.at[i])
            sids.free.append(i)
        sent[:] = [group for group in sent if group[1] >= mark]

    def got(waits):
        for whole, r in waits:
            wait_all(whole, rsem.at[r])

    loc = [
        pltpu.make_async_copy(arr_hbm, s["arr"], lsem.at[0]),
        pltpu.make_async_copy(win_hbm, s["win"], lsem.at[1]),
        pltpu.make_async_copy(wbc_hbm, s["w2"].at[0:32], lsem.at[2]),
        pltpu.make_async_copy(wout_hbm, s["wout"], lsem.at[3]),
    ]
    for cp in loc:
        cp.start()

    barrier = pltpu.get_barrier_semaphore()
    count = 0
    peers = [(head_of(zh, x, y, 1 - c), m), (head_of(1 - zh, x, y, c), m)]
    for d in range(1, 4):
        peers.append((head_of(zh, (x + d) % 4, y, c), m))
        peers.append((h, (m + d) % 4))
    for d in range(1, 8):
        peers.append((8 * g + (j + d) % 8, m))
    for head, mb in peers:
        pl.semaphore_signal(barrier, inc=1, device_id=(head, mb), device_id_type=MESH)
        count += 1
    target = 8 * g_t + part
    source = 4 * g + j + 28 * (j // 4)
    for head in (target, source):
        pl.semaphore_signal(barrier, inc=1, device_id=(head, m), device_id_type=MESH)
        count += 1

    s["cbc"][...] = jnp.zeros((8, 128), F32)
    s["cbc"][0:4, 0:32] = cbc_ref[...]
    s["wdtf"][...] = jnp.zeros((16, 4096), F32)
    s["wdtf"][0:2, :] = wdt_ref[...].astype(F32)
    s["w2"][32:48, :] = s["wdtf"][...].astype(BF)
    s["w2"][48:128, :] = jnp.zeros((80, 4096), BF)

    sx = s["sx"]
    loc[0].wait()

    def split_arr(cc):
        def one(i, _):
            v = s["arr"][:, pl.ds(pl.multiple_of(i * 256 + cc * 128, 128), 128)]
            sx["p"][i // 4, i % 4, cc] = v.reshape(2, 4, 16, 128)
            return 0
        lax.fori_loop(0, 16, one, 0, unroll=4)

    split_arr(1 - c)
    pl.semaphore_wait(barrier, count)

    owner = own_ref[0]
    o_zh, o_x, o_y, o_c = owner // 32, (owner // 8) % 4, (owner // 2) % 4, owner % 2

    def combine(own, received, picks):
        if picks is None:
            total = own.astype(F32)
            for v in received:
                total = total + v.astype(F32)
            return total
        value = own
        for v, pick in zip(received, picks):
            value = lax.select(pick, v, value)
        return value

    def stage1_copies(b, k):
        head = head_of(zh, x, y, 1 - c)
        return [([(b["p"].at[q, :, 1 - c], b["r1"].at[q], head, m) for q in (k, 2 + k)], b["r1"].at[0:2])]

    def stage1_merge(b, k, picks):
        for q in (k, 2 + k):
            b["q"][q] = combine(b["p"][q, :, c], [b["r1"][q]], picks and picks["c"]).astype(BF)

    def stage2_copies(b, k):
        along_x, along_y = [], []
        for d in range(1, 4):
            x2, y2 = (x + d) % 4, (y + d) % 4
            along_x.append((b["q"].at[k, :, :, x2], b["r2x"].at[k, d - 1], head_of(zh, x2, y, c), m))
            along_y.append((b["q"].at[2 + k, y2], b["r2y"].at[k, d - 1], head_of(zh, x, y2, c), m))
        return [(along_x, b["r2x"].at[k]), (along_y, b["r2y"].at[k])]

    def stage2_merge(b, k, picks):
        b["qx"][k] = combine(b["q"][k, :, :, x], [b["r2x"][k, d] for d in range(3)], picks and picks["x"]).astype(BF)
        b["qy"][k] = combine(b["q"][2 + k, y], [b["r2y"][k, d] for d in range(3)], picks and picks["y"]).astype(BF)

    def stage3_copies(b, k):
        along_x, along_y = [], []
        for d in range(1, 4):
            x2, y2 = (x + d) % 4, (y + d) % 4
            along_y.append((b["qx"].at[k, y2], b["r3x"].at[k, d - 1], head_of(zh, x, y2, c), m))
            along_x.append((b["qy"].at[k, :, x2], b["r3y"].at[k, d - 1], head_of(zh, x2, y, c), m))
        return [(along_y, b["r3x"].at[k]), (along_x, b["r3y"].at[k])]

    def stage3_merge(b, k, picks):
        b["t"][k] = combine(b["qx"][k, y], [b["r3x"][k, d] for d in range(3)], picks and picks["y"]).astype(BF)
        b["t"][2 + k] = combine(b["qy"][k, :, x], [b["r3y"][k, d] for d in range(3)], picks and picks["x"]).astype(BF)

    other_zh = head_of(1 - zh, x, y, c)

    def gather1(a, s1, s2):
        along_x, along_y = [], []
        r1, r2 = a.at[s1, y, c, :, x], a.at[s2, y, c, :, x]
        for d in range(1, 4):
            x2, y2 = (x + d) % 4, (y + d) % 4
            along_y.append((r1, r1, head_of(zh, x, y2, c), m))
            along_x.append((r2, r2, head_of(zh, x2, y, c), m))
        return [(along_y, a.at[s1, 0:3, c, :, x]), (along_x, a.at[s2, y, c, :, 0:3])]

    def gather2(a, s1, s2):
        along_x, along_y = [], []
        r1, r2 = a.at[s1, :, c, :, x], a.at[s2, y, c]
        for d in range(1, 4):
            x2, y2 = (x + d) % 4, (y + d) % 4
            along_x.append((r1, r1, head_of(zh, x2, y, c), m))
            along_y.append((r2, r2, head_of(zh, x, y2, c), m))
        return [(along_x, a.at[s1, :, c, :, 0:3]), (along_y, a.at[s2, 0:3, c])]

    def gather3(a, part_of):
        ref = a.at[part_of, :, c]
        return [([(ref, ref, head_of(zh, x, y, 1 - c), m)], ref)]

    def trade(b):
        cps = []
        for d in range(1, 8):
            k = (j + d) % 8
            src = b["g"].at[pl.ds(pl.multiple_of(k * 8, 8), 8)]
            dst = b["r"].at[pl.ds(pl.multiple_of(j * 8, 8), 8)]
            cps.append((src, dst, 8 * g + k, m))
        mine = pl.ds(pl.multiple_of(j * 8, 8), 8)
        b["r"][mine, :] = b["g"][mine, :]
        return [(cps, b["r"].at[0:56])]

    lane = lax.broadcasted_iota(jnp.int32, (T, 128), 1)
    row = lax.broadcasted_iota(jnp.int32, (T, 128), 0)

    def unpack_weights(first, last):
        def one(i, _):
            k = i % 2
            s["wf"][k] = s["win"][pl.ds(pl.multiple_of(i * 512, 512), 512), :].astype(F32)
            at = pl.ds(pl.multiple_of(i * 256, 256), 256)
            s["wxz"][at, 0:128] = s["wf"][k, pl.ds(0, 256, stride=2), :].astype(BF)
            s["wxz"][at, 128:256] = s["wf"][k, pl.ds(1, 256, stride=2), :].astype(BF)
            return 0
        lax.fori_loop(first, last, one, 0)

    picks = dict(
        c=[o_c != c],
        x=[o_x == (x + 4 - d) % 4 for d in range(1, 4)],
        y=[o_y == (y + 4 - d) % 4 for d in range(1, 4)],
    )
    a_x, a_o = s["ax"], s["ao"]
    x1 = [go(stage1_copies(sx, k)) for k in range(2)]
    split_arr(c)
    tog = s["tog"]
    og = og_ref[...].astype(F32)
    for k in range(8):
        for q in range(4):
            tog["g"][k * 8 + q * 2:k * 8 + q * 2 + 2, :] = og[:, q * 1024 + k * 128:q * 1024 + k * 128 + 128]
    o1 = go(trade(tog))
    x2 = []
    for k in range(2):
        got(x1[k])
        stage1_merge(sx, k, picks)
        x2.append(go(stage2_copies(sx, k)))
    got(o1)
    for q in range(4):
        for tt in range(2):
            tog["v"][pl.ds(q * 16 + tt, 8, stride=2), :] = tog["r"][pl.ds(q * 2 + tt, 8, stride=8), :]
    a_o[0:4, y, c, zh, x] = tog["v"][...].reshape(4, 16, 128).astype(BF)
    cps = []
    for d in range(1, 4):
        m2 = (m + d) % 4
        cps.append((a_o.at[m2, y, c, zh, x], a_o.at[7 - d, y, c, zh, x], h, m2))
    oc = go([(cps, a_o.at[4:7, y, c, zh, x])])
    oz_ref = a_o.at[0:4, y, c, zh, x]
    oz = go([([(oz_ref, oz_ref, other_zh, m)], oz_ref)])
    loc[1].wait()
    unpack_weights(0, 3)
    x3 = []
    for k in range(2):
        got(x2[k])
        stage2_merge(sx, k, picks)
        x3.append(go(stage3_copies(sx, k)))
    got(oz)
    q01, q23 = slice(0, 2), slice(2, 4)
    og1 = go(gather1(a_o, q01, q23))
    unpack_weights(3, 6)
    x4 = []
    for k in range(2):
        got(x3[k])
        stage3_merge(sx, k, picks)
        x4.append(go([([(sx["t"].at[q], sx["r4"].at[q], other_zh, m) for q in (k, 2 + k)], sx["r4"].at[0:2])]))
    got(oc)
    ocz_ref = a_o.at[4:7, y, c, zh, x]
    ocz = go([([(ocz_ref, ocz_ref, other_zh, m)], ocz_ref)])
    got(og1)
    unpack_weights(6, 9)
    xg1, xg2, xg3 = [], [], []
    first = [slice(k, k + 1) for k in range(2)]
    second = [slice(2 + k, 3 + k) for k in range(2)]
    for k in range(2):
        got(x4[k])
        for q in (k, 2 + k):
            a_x[q, y, c, :, x] = combine(sx["t"][q], [sx["r4"][q]], [o_zh != zh])
        xg1.append(go(gather1(a_x, first[k], second[k])))
    cps = []
    for d in range(1, 4):
        m2 = (m + d) % 4
        cps.append((a_x.at[m2, y, c, :, x], a_x.at[7 - d, y, c, :, x], h, m2))
    xc = go([(cps, a_x.at[4:7, y, c, :, x])])
    k1, k2 = slice(4, 5), slice(5, 7)
    l1, l2 = slice(4, 6), slice(6, 7)
    unpack_weights(9, 12)
    for k in range(2):
        got(xg1[k])
        xg2.append(go(gather2(a_x, first[k], second[k])))
    got(ocz)
    cog1 = go(gather1(a_o, l1, l2))
    got(xc)
    cxg1 = go(gather1(a_x, k1, k2))
    unpack_weights(12, 16)
    mark = sids.used
    for k in range(2):
        got(xg2[k])
        xg3.append(go(gather3(a_x, first[k]) + gather3(a_x, second[k])))
    og2 = go(gather2(a_o, q01, q23))

    def assemble(a, dst, cc, q):
        def one(i, _):
            at = pl.ds(pl.multiple_of(q * 1024 + i * 256 + cc * 128, 128), 128)
            dst[:, at] = a[q, i, cc].reshape(128, 128)
            return 0
        lax.fori_loop(0, 4, one, 0, unroll=True)

    for q in range(4):
        assemble(a_x, s["x"], c, q)
    loc[2].wait()
    p2 = jnp.zeros((T, 128), F32)
    for k in range(2):
        got(xg3[k])
        for q in (k, 2 + k):
            assemble(a_x, s["x"], 1 - c, q)
            at = slice(q * 1024, (q + 1) * 1024)
            p2 = p2 + bdot(s["x"][:, at], s["w2"][:, at], NT)

    e1 = doc_ref[0, 0]
    e2 = e1 + doc_ref[0, 1]
    e3 = e2 + doc_ref[0, 2]
    e4 = e3 + doc_ref[0, 3]

    def doc_of(t):
        return sum((t >= e).astype(jnp.int32) for e in (e1, e2, e3, e4))

    doc_row = doc_of(row)
    same = [None] + [(row >= o) & (doc_of(row - o) == doc_row) for o in range(1, 4)]
    visible = (row >= lane) & (doc_row == doc_of(lane))

    def conv(v, taps):
        result = v * taps[3:4]
        for o in range(1, 4):
            result = result + jnp.where(same[o], pltpu.roll(v, o, 0), 0.0) * taps[3 - o:4 - o]
        return result

    def conv_back(d, taps):
        result = d * taps[3:4]
        for o in range(1, 4):
            result = result + pltpu.roll(jnp.where(same[o], d, 0.0), T - o, 0) * taps[3 - o:4 - o]
        return result

    flush(mark)

    taps_bc = s["cbc"][...]
    bc_pre = conv(p2, taps_bc)
    bc_sig = sigmoid(bc_pre)
    s["ss"][...] = jnp.transpose(bc_pre * bc_sig)[0:32].astype(BF)
    i_bc, r_bc = sids.take(1), rids.take(1)

    @pl.when(target != h)
    def _():
        copy(s["ss"], s["bc"].at[part], i_bc, r_bc, target, m).start()

    @pl.when(target == h)
    def _():
        pltpu.make_async_copy(s["ss"], s["bc"].at[part], rsem.at[r_bc]).start()

    wait_all(s["bc"].at[j], rsem.at[r_bc])
    peers_of = [8 * g + (j + d) % 8 for d in range(1, 8)]
    bcp = go([([(s["bc"].at[j], s["bc"].at[j], head, m) for head in peers_of], s["bc"].at[0:7])])

    got(cxg1)
    cxg2 = go(gather2(a_x, k1, k2))

    pxz = bdot(s["x"][...], s["wxz"][...], NN)
    got(og2)
    og3 = go(gather3(a_o, slice(0, 4)))
    z = pxz[:, 128:256]
    taps_x = cx_ref[...]
    x_pre = conv(pxz[:, 0:128], taps_x)
    x_sig = sigmoid(x_pre)
    x_conv = x_pre * x_sig
    z_sig = sigmoid(z)
    z_silu = z * z_sig
    low = lane < 64
    tri = jnp.where(row >= lane, 1.0, 0.0)
    raws, rates, steps = [], [], []
    for e in range(2):
        raw = jnp.broadcast_to(p2[:, 32 + e:33 + e], (T, 128)) + dtb_ref[e]
        raws.append(raw)
        rates.append(-jnp.exp(jnp.full((T, 128), alog_ref[e], F32)))
        steps.append(jnp.maximum(raw, 0.0) + jnp.log1p(jnp.exp(-jnp.abs(raw))))
    step = jnp.where(low, steps[0], steps[1])
    cum = hdot(tri, jnp.where(low, steps[0] * rates[0], steps[1] * rates[1]), NN)
    decays = []
    for e in range(2):
        col = jnp.broadcast_to(cum[:, 64 * e:64 * e + 1], (T, 128))
        gap = col - jnp.transpose(col)
        decays.append(jnp.where(visible, jnp.exp(jnp.where(visible, gap, 0.0)), 0.0))
    scaled = x_conv * step
    skip = jnp.where(low, skip_ref[0], skip_ref[1])

    for q in range(4):
        assemble(a_o, s["o"], c, q)
    got(og3)
    for q in range(4):
        assemble(a_o, s["o"], 1 - c, q)
    loc[3].wait()
    weighted = bdot(s["o"][...], s["wout"][...], NT) * gain_ref[...]

    got(bcp)
    b_t = s["bc"][0:4].reshape(128, 128)
    c_t = s["bc"][4:8].reshape(128, 128)
    scores = bdot(c_t, b_t, TN)
    mixes = [scores * decays[0], scores * decays[1]]
    zero = jnp.zeros((T, 128), F32)
    scaled2 = jnp.concatenate([jnp.where(low, scaled, zero), jnp.where(low, zero, scaled)], axis=0)
    state = hdot(jnp.concatenate(mixes, axis=1), scaled2, NN) + skip * x_conv
    gated = state * z_silu
    squares = jnp.sum(gated * gated, axis=1, keepdims=True)
    inners = jnp.sum(weighted * gated, axis=1, keepdims=True)
    nmat = jnp.where(lane == 0, squares, jnp.where(lane == 1, inners, 0.0))
    s["norm"][j] = jnp.transpose(nmat)[0:8]
    cps = [(s["norm"].at[j], s["norm"].at[j], head, m) for head in peers_of]
    ncp = go([(cps, s["norm"].at[0:7])])
    got(cxg2)
    cxg3 = go(gather3(a_x, slice(4, 7)))
    got(ncp)
    total = jnp.sum(s["norm"][...], axis=0)
    tcol = jnp.transpose(jnp.concatenate([total, jnp.zeros((120, 128), F32)], axis=0))
    inverse = jnp.broadcast_to(lax.rsqrt(tcol[:, 0:1] * (1.0 / WIDTH) + EPS), (T, 128))
    inner = jnp.broadcast_to(tcol[:, 1:2] * (1.0 / WIDTH), (T, 128))
    normed = (gated * inverse * gain_ref[...]).astype(BF)
    s["nm"][0] = normed
    d_gated = inverse * weighted - gated * (inverse * inverse * inverse * inner)

    d_state = d_gated * z_silu
    d_z = d_gated * state * (z_sig * (1.0 + z * (1.0 - z_sig)))
    s["dz"][0] = d_z.astype(BF)
    dy0, dy1 = jnp.where(low, d_state, zero), jnp.where(low, zero, d_state)
    d_mix = [hdot(dy0, scaled, NT), hdot(dy1, scaled, NT)]
    d_scores = d_mix[0] * decays[0] + d_mix[1] * decays[1]
    s["dbcs"][0:4] = hdot(c_t.astype(F32), d_scores, NN).reshape(4, 32, 128).astype(BF)
    s["dbcs"][4:8] = hdot(b_t.astype(F32), d_scores, NT).reshape(4, 32, 128).astype(BF)
    s["dbcr"][j] = s["dbcs"][j]
    cps = [(s["dbcs"].at[(j + d) % 8], s["dbcr"].at[j], 8 * g + (j + d) % 8, m) for d in range(1, 8)]
    dbc = go([(cps, s["dbcr"].at[0:7])])
    got(cog1)
    cog2 = go(gather2(a_o, l1, l2))

    def to_mb(ref):
        cps = [(ref.at[0], ref.at[4 - d], h, (m + d) % 4) for d in range(1, 4)]
        return go([(cps, ref.at[1:4])])

    n_mb = to_mb(s["nm"])
    z_mb = to_mb(s["dz"])

    slo, sig = s["slo"], s["sig"]

    def lo_half(cc):
        def one(i, _):
            at = pl.ds(pl.multiple_of(i * 256 + cc * 128, 128), 128)
            v = bdot(normed, s["wout"][:, at], NN)
            slo["p"][i // 4, i % 4, cc] = v.astype(BF).reshape(2, 4, 16, 128)
            return 0
        lax.fori_loop(0, 16, one, 0, unroll=8)

    lo_half(1 - c)
    lo1 = go(stage1_copies(slo, 0) + stage1_copies(slo, 1))
    got(dbc)
    s["dsum"][...] = jnp.sum(s["dbcr"][...].astype(F32), axis=0)
    i_d, r_d = sids.take(1), rids.take(1)

    @pl.when(source != h)
    def _():
        copy(s["dsum"], s["dgot"], i_d, r_d, source, m).start()

    @pl.when(source == h)
    def _():
        pltpu.make_async_copy(s["dsum"], s["dgot"], rsem.at[r_d]).start()

    lo_half(c)

    d_scaled = hdot(
        jnp.concatenate(mixes, axis=0), jnp.concatenate([dy0, dy1], axis=0), TN
    )
    d_xconv = skip * d_state + d_scaled * step
    d_x = conv_back(d_xconv * (x_sig * (1.0 + x_pre * (1.0 - x_sig))), taps_x)
    s["dx"][0] = d_x.astype(BF)
    x_mb = to_mb(s["dx"])
    through = d_scaled * x_conv
    d_raws = []
    for e in range(2):
        mine = low if e == 0 else lane >= 64
        gap_grad = d_mix[e] * mixes[e]
        d_cum = jnp.sum(gap_grad - jnp.transpose(gap_grad), axis=1, keepdims=True)
        back = hdot(tri, jnp.broadcast_to(d_cum, (T, 128)), TN)
        d_step = jnp.sum(jnp.where(mine, through, 0.0), axis=1, keepdims=True) + rates[e] * back
        d_raws.append(d_step * sigmoid(raws[e]))

    got(lo1)
    for k in range(2):
        stage1_merge(slo, k, None)
    lo2 = go(stage2_copies(slo, 0) + stage2_copies(slo, 1))

    wait_all(s["dgot"], rsem.at[r_d])
    got(cog2)
    cog3 = go(gather3(a_o, slice(4, 7)))
    d_act = jnp.transpose(
        jnp.concatenate([s["dgot"][...], jnp.zeros((96, 128), F32)], axis=0)
    )
    d_bc = conv_back(d_act * (bc_sig * (1.0 + bc_pre * (1.0 - bc_sig))), taps_bc)
    d2 = jnp.where(lane == 32, d_raws[0], jnp.where(lane == 33, d_raws[1], d_bc))
    d2_b = d2.astype(BF)
    s["d2"][0] = jnp.transpose(d2)[0:48].astype(BF)
    d2_mb = to_mb(s["d2"])

    d_proj = jnp.concatenate([s["dx"][0], s["dz"][0]], axis=1)

    def ig_half(cc, k):
        for q in (k, 2 + k):
            def one(i, _):
                at = pl.ds(pl.multiple_of(q * 1024 + i * 256 + cc * 128, 128), 128)
                v = bdot(d_proj, s["wxz"][at, :], NT) + bdot(d2_b, s["w2"][:, at], NN)
                sig["p"][q, i, cc] = v.astype(BF).reshape(2, 4, 16, 128)
                return 0
            lax.fori_loop(0, 4, one, 0, unroll=True)

    ig1, ig2, ig3, ig4 = [], [], [], []
    for k in range(2):
        ig_half(1 - c, k)
        ig1.append(go(stage1_copies(sig, k)))
    for k in range(2):
        ig_half(c, k)
    for k in range(2):
        got(ig1[k])
        stage1_merge(sig, k, None)
        ig2.append(go(stage2_copies(sig, k)))
    got(n_mb)
    got(cog3)
    nm_all = s["nm"][...].reshape(512, 128)

    def grad_out(i, _):
        yy, cc = i // 2, i % 2
        lhs = jnp.concatenate(
            [a_o[m, yy, cc].reshape(128, 128)] + [a_o[k, yy, cc].reshape(128, 128) for k in range(4, 7)], axis=0
        )
        s["gout"][pl.ds(pl.multiple_of(i * 128, 128), 128), :] = bdot(lhs, nm_all, TN).astype(BF)
        return 0

    lax.fori_loop(0, 8, grad_out, 0, unroll=4)
    leave = [
        pltpu.make_async_copy(s["gout"], go_out, lsem.at[4]),
        pltpu.make_async_copy(s["gin"], gin_out, lsem.at[5]),
    ]
    leave[0].start()

    def stage4(b, k):
        return [([(b["t"].at[q, 1 - zh], b["r4"].at[q], other_zh, m) for q in (k, 2 + k)], b["r4"].at[0:2])]

    def stage5(b, t):
        t["v"][...] = (b["t"][:, zh].astype(F32) + b["r4"][...].astype(F32)).reshape(64, 128)
        for q in range(4):
            for tt in range(2):
                t["g"][pl.ds(q * 2 + tt, 8, stride=8), :] = t["v"][pl.ds(q * 16 + tt, 8, stride=2), :]
        return go(trade(t))

    def finish(t, out):
        for k in range(8):
            for q in range(4):
                at = q * 1024 + k * 128
                out[:, at:at + 128] = t["r"][k * 8 + q * 2:k * 8 + q * 2 + 2, :].astype(BF)

    for k in range(2):
        got(ig2[k])
        stage2_merge(sig, k, None)
        ig3.append(go(stage3_copies(sig, k)))
    got(lo2)
    for k in range(2):
        stage2_merge(slo, k, None)
    lo3 = go(stage3_copies(slo, 0) + stage3_copies(slo, 1))
    got(x_mb)
    got(z_mb)
    got(d2_mb)
    got(cxg3)
    d_all = jnp.concatenate(
        [s["dx"][...].reshape(512, 128), s["dz"][...].reshape(512, 128)], axis=1
    )
    d2_all = jnp.concatenate([s["d2"][k] for k in range(4)], axis=1)

    def grad_in(i, _):
        yy, cc, k = i // 2, i % 2, i % 2
        lhs = jnp.concatenate(
            [a_x[m, yy, cc].reshape(128, 128)] + [a_x[k_, yy, cc].reshape(128, 128) for k_ in range(4, 7)], axis=0
        )
        r = bdot(lhs, d_all, TN)
        s["gf"][k, pl.ds(0, 128, stride=2), :] = r[:, 0:128]
        s["gf"][k, pl.ds(1, 128, stride=2), :] = r[:, 128:256]
        s["gin"][pl.ds(pl.multiple_of(i * 256, 256), 256), :] = s["gf"][k].astype(BF)
        small = bdot(d2_all, lhs, NN)
        at = pl.ds(pl.multiple_of(i * 128, 128), 128)
        gbc_out[:, at] = small[0:32].astype(BF)
        gdt_out[:, at] = small[32:34].astype(BF)
        return 0

    lax.fori_loop(0, 4, grad_in, 0)
    for k in range(2):
        got(ig3[k])
        stage3_merge(sig, k, None)
        ig4.append(go(stage4(sig, k)))
    got(lo3)
    for k in range(2):
        stage3_merge(slo, k, None)
    lo4 = go(stage4(slo, 0) + stage4(slo, 1))
    lax.fori_loop(4, 8, grad_in, 0)
    leave[1].start()
    for k in range(2):
        got(ig4[k])
    ig5 = stage5(sig, s["tig"])
    got(lo4)
    lo5 = stage5(slo, s["tlo"])
    got(ig5)
    finish(s["tig"], ig_out)
    got(lo5)
    finish(s["tlo"], lo_out)

    for cp in leave:
        cp.wait()
    for whole, i in sent:
        wait_all(whole, ssem.at[i])
    @pl.when(target != h)
    def _():
        wait_all(s["ss"], ssem.at[i_bc])

    @pl.when(source != h)
    def _():
        wait_all(s["dsum"], ssem.at[i_d])

    assert rids.used <= N_RECV and sids.used <= N_SEND, (rids.used, sids.used)


def place_kernel(*refs):
    for source, result in zip(refs[:6], refs[6:]):
        result[...] = source[...]


def per_device(
    arrivals, owners, doc_lengths, w_in, w_bc, w_dt, conv_x, conv_bc, dt_bias, a_log, skip_scale,
    norm_gain, w_out, out_grad,
):
    smem = pl.BlockSpec(memory_space=pltpu.SMEM)
    vmem = pl.BlockSpec(memory_space=pltpu.VMEM)
    hbm = pl.BlockSpec(memory_space=pl.ANY)
    sds = jax.ShapeDtypeStruct
    shapes = (
        sds((2, 4096), BF), sds((2, 4096), BF), sds((2048, 128), BF), sds((32, 1024), BF),
        sds((2, 1024), BF), sds((1024, 128), BF),
    )
    made = pl.pallas_call(
        mixer_kernel,
        out_shape=shapes,
        in_specs=[smem] * 5 + [vmem] * 5 + [hbm] * 4,
        out_specs=(vmem, vmem, hbm, vmem, vmem, hbm),
        scratch_shapes=[SCRATCH],
        compiler_params=pltpu.CompilerParams(
            collective_id=0, has_side_effects=True, vmem_limit_bytes=56 * 1024 * 1024
        ),
    )(
        owners, doc_lengths, dt_bias, a_log, skip_scale, conv_x, conv_bc,
        norm_gain.reshape(1, 128), w_dt, out_grad.reshape(2, 4096),
        arrivals.reshape(T, 4096), w_in.reshape(8192, 128), w_bc, w_out,
    )
    lo, ig, gin, gbc, gdt, gout = pl.pallas_call(
        place_kernel,
        out_shape=shapes,
        in_specs=[vmem] * 6,
        out_specs=(vmem,) * 6,
    )(*made)
    return (
        lo[None], ig[None], gin.reshape(1024, 2, 128), gbc.T, gdt.T, gout,
    )


def solution(mesh):
    return jax.shard_map(
        per_device,
        mesh=mesh,
        in_specs=(
            P("mb", "head", None, None),
            P("mb"),
            P("mb", None),
            P(None, None, "head"),
            P("head", None),
            P("head", None),
            P(None, "head"),
            P(None, "head"),
            P("head"),
            P("head"),
            P("head"),
            P("head"),
            P("head", None),
            P("mb", "head", None),
        ),
        out_specs=(
            P("mb", "head", None),
            P("mb", "head", None),
            P("mb", None, "head"),
            P("mb", "head"),
            P("mb", "head"),
            P("mb", "head"),
        ),
        check_vma=False,
    )
```

```python
import jax
import jax.numpy as jnp
from jax import lax
from jax.experimental import pallas as pl
from jax.experimental.pallas import tpu as pltpu
from jax.sharding import PartitionSpec as P

T = 128
EPS = 1e-05
WIDTH = 1024
HI = lax.Precision.HIGHEST
MESH = pl.DeviceIdType.MESH
BF = jnp.bfloat16
F32 = jnp.float32


def sigmoid(v):
    return 1.0 / (1.0 + jnp.exp(-v))


def hdot(a, b, dims):
    return lax.dot_general(a, b, (dims, ((), ())), precision=HI, preferred_element_type=F32)


def bdot(a, b, dims):
    return lax.dot_general(a, b, (dims, ((), ())), preferred_element_type=F32)


NN = ((1,), (0,))
NT = ((1,), (1,))
TN = ((0,), (0,))


class Ids:
    def __init__(self):
        self.used = 0
        self.free = []

    def take(self, count):
        if count == 1 and self.free:
            return self.free.pop()
        first = self.used
        self.used += count
        return first


def staged(last):
    return dict(
        p=pltpu.VMEM((4, 4, 2, 2, 4, 16, 128), BF),
        r1=pltpu.VMEM((4, 4, 2, 4, 16, 128), BF),
        q=pltpu.VMEM((4, 4, 2, 4, 16, 128), BF),
        r2x=pltpu.VMEM((2, 3, 4, 2, 16, 128), BF),
        r2y=pltpu.VMEM((2, 3, 2, 4, 16, 128), BF),
        qx=pltpu.VMEM((2, 4, 2, 16, 128), BF),
        qy=pltpu.VMEM((2, 2, 4, 16, 128), BF),
        r3x=pltpu.VMEM((2, 3, 2, 16, 128), BF),
        r3y=pltpu.VMEM((2, 3, 2, 16, 128), BF),
        t=pltpu.VMEM((4, 2, 16, 128), BF),
        r4=pltpu.VMEM(last, BF),
    )


def rows_trade():
    return dict(
        v=pltpu.VMEM((64, 128), F32), g=pltpu.VMEM((64, 128), F32), r=pltpu.VMEM((64, 128), F32)
    )


N_RECV = 79
N_SEND = 48

SCRATCH = dict(
    arr=pltpu.VMEM((T, 4096), BF),
    win=pltpu.VMEM((8192, 128), BF),
    wf=pltpu.VMEM((2, 512, 128), F32),
    wxz=pltpu.VMEM((4096, 256), BF),
    w2=pltpu.VMEM((128, 4096), BF),
    wdtf=pltpu.VMEM((16, 4096), F32),
    wout=pltpu.VMEM((128, 4096), BF),
    cbc=pltpu.VMEM((8, 128), F32),
    ax=pltpu.VMEM((7, 4, 2, 2, 4, 16, 128), BF),
    ao=pltpu.VMEM((7, 4, 2, 2, 4, 16, 128), BF),
    x=pltpu.VMEM((T, 4096), BF),
    o=pltpu.VMEM((T, 4096), BF),
    ss=pltpu.VMEM((32, 128), BF),
    bc=pltpu.VMEM((8, 32, 128), BF),
    norm=pltpu.VMEM((8, 8, 128), F32),
    dbcs=pltpu.VMEM((8, 32, 128), BF),
    dbcr=pltpu.VMEM((8, 32, 128), BF),
    dsum=pltpu.VMEM((32, 128), F32),
    dgot=pltpu.VMEM((32, 128), F32),
    dx=pltpu.VMEM((4, 128, 128), BF),
    dz=pltpu.VMEM((4, 128, 128), BF),
    nm=pltpu.VMEM((4, 128, 128), BF),
    d2=pltpu.VMEM((4, 48, 128), BF),
    gin=pltpu.VMEM((2048, 128), BF),
    gout=pltpu.VMEM((1024, 128), BF),
    gf=pltpu.VMEM((2, 256, 128), F32),
    sx=staged((4, 2, 16, 128)),
    slo=staged((4, 16, 128)),
    sig=staged((4, 16, 128)),
    tog=rows_trade(),
    tlo=rows_trade(),
    tig=rows_trade(),
    ssem=pltpu.SemaphoreType.DMA((N_SEND,)),
    rsem=pltpu.SemaphoreType.DMA((N_RECV,)),
    lsem=pltpu.SemaphoreType.DMA((8,)),
)


def mixer_kernel(
    own_ref, doc_ref, dtb_ref, alog_ref, skip_ref, cx_ref, cbc_ref, gain_ref, wdt_ref, og_ref,
    arr_hbm, win_hbm, wbc_hbm, wout_hbm,
    lo_out, ig_out, gin_out, gbc_out, gdt_out, go_out,
    s,
):
    h = lax.axis_index("head")
    m = lax.axis_index("mb")
    zh = h // 32
    x = (h // 8) % 4
    y = (h // 2) % 4
    c = h % 2
    j = h % 8
    g = h // 8
    g_t = (h % 32) // 4
    part = zh * 4 + h % 4
    ssem, rsem, lsem = s["ssem"], s["rsem"], s["lsem"]
    rids, sids = Ids(), Ids()
    sent = []

    def head_of(zh_, x_, y_, c_):
        return zh_ * 32 + x_ * 8 + y_ * 2 + c_

    def copy(src, dst, i, r, head, mb):
        return pltpu.make_async_remote_copy(
            src_ref=src, dst_ref=dst, send_sem=ssem.at[i], recv_sem=rsem.at[r],
            device_id=(head, mb), device_id_type=MESH,
        )

    def wait_all(ref, sem):
        pltpu.make_async_copy(ref, ref, sem).wait()

    def go(groups):
        waits = []
        for copies, whole in groups:
            i, r = sids.take(1), rids.take(1)
            for src, dst, head, mb in copies:
                copy(src, dst, i, r, head, mb).start()
            waits.append((whole, r))
            sent.append((whole, i))
        return waits

    def flush(mark):
        for whole, i in [group for group in sent if group[1] < mark]:
            wait_all(whole, ssem.at[i])
            sids.free.append(i)
        sent[:] = [group for group in sent if group[1] >= mark]

    def got(waits):
        for whole, r in waits:
            wait_all(whole, rsem.at[r])

    loc = [
        pltpu.make_async_copy(arr_hbm, s["arr"], lsem.at[0]),
        pltpu.make_async_copy(win_hbm, s["win"], lsem.at[1]),
        pltpu.make_async_copy(wbc_hbm, s["w2"].at[0:32], lsem.at[2]),
        pltpu.make_async_copy(wout_hbm, s["wout"], lsem.at[3]),
    ]
    for cp in loc:
        cp.start()

    barrier = pltpu.get_barrier_semaphore()
    count = 0
    peers = [(head_of(zh, x, y, 1 - c), m), (head_of(1 - zh, x, y, c), m)]
    for d in range(1, 4):
        peers.append((head_of(zh, (x + d) % 4, y, c), m))
        peers.append((h, (m + d) % 4))
    for d in range(1, 8):
        peers.append((8 * g + (j + d) % 8, m))
    for head, mb in peers:
        pl.semaphore_signal(barrier, inc=1, device_id=(head, mb), device_id_type=MESH)
        count += 1
    target = 8 * g_t + part
    source = 4 * g + j + 28 * (j // 4)
    for head in (target, source):
        pl.semaphore_signal(barrier, inc=1, device_id=(head, m), device_id_type=MESH)
        count += 1

    s["cbc"][...] = jnp.zeros((8, 128), F32)
    s["cbc"][0:4, 0:32] = cbc_ref[...]
    s["wdtf"][...] = jnp.zeros((16, 4096), F32)
    s["wdtf"][0:2, :] = wdt_ref[...].astype(F32)
    s["w2"][32:48, :] = s["wdtf"][...].astype(BF)
    s["w2"][48:128, :] = jnp.zeros((80, 4096), BF)

    sx = s["sx"]
    loc[0].wait()

    def split_arr(cc):
        def one(i, _):
            v = s["arr"][:, pl.ds(pl.multiple_of(i * 256 + cc * 128, 128), 128)]
            sx["p"][i // 4, i % 4, cc] = v.reshape(2, 4, 16, 128)
            return 0
        lax.fori_loop(0, 16, one, 0, unroll=4)

    split_arr(1 - c)
    pl.semaphore_wait(barrier, count)

    owner = own_ref[0]
    o_zh, o_x, o_y, o_c = owner // 32, (owner // 8) % 4, (owner // 2) % 4, owner % 2

    def combine(own, received, picks):
        if picks is None:
            total = own.astype(F32)
            for v in received:
                total = total + v.astype(F32)
            return total
        value = own
        for v, pick in zip(received, picks):
            value = lax.select(pick, v, value)
        return value

    def stage1_copies(b, k):
        head = head_of(zh, x, y, 1 - c)
        return [([(b["p"].at[q, :, 1 - c], b["r1"].at[q], head, m) for q in (k, 2 + k)], b["r1"].at[0:2])]

    def stage1_merge(b, k, picks):
        for q in (k, 2 + k):
            b["q"][q] = combine(b["p"][q, :, c], [b["r1"][q]], picks and picks["c"]).astype(BF)

    def stage2_copies(b, k):
        along_x, along_y = [], []
        for d in range(1, 4):
            x2, y2 = (x + d) % 4, (y + d) % 4
            along_x.append((b["q"].at[k, :, :, x2], b["r2x"].at[k, d - 1], head_of(zh, x2, y, c), m))
            along_y.append((b["q"].at[2 + k, y2], b["r2y"].at[k, d - 1], head_of(zh, x, y2, c), m))
        return [(along_x, b["r2x"].at[k]), (along_y, b["r2y"].at[k])]

    def stage2_merge(b, k, picks):
        b["qx"][k] = combine(b["q"][k, :, :, x], [b["r2x"][k, d] for d in range(3)], picks and picks["x"]).astype(BF)
        b["qy"][k] = combine(b["q"][2 + k, y], [b["r2y"][k, d] for d in range(3)], picks and picks["y"]).astype(BF)

    def stage3_copies(b, k):
        along_x, along_y = [], []
        for d in range(1, 4):
            x2, y2 = (x + d) % 4, (y + d) % 4
            along_y.append((b["qx"].at[k, y2], b["r3x"].at[k, d - 1], head_of(zh, x, y2, c), m))
            along_x.append((b["qy"].at[k, :, x2], b["r3y"].at[k, d - 1], head_of(zh, x2, y, c), m))
        return [(along_y, b["r3x"].at[k]), (along_x, b["r3y"].at[k])]

    def stage3_merge(b, k, picks):
        b["t"][k] = combine(b["qx"][k, y], [b["r3x"][k, d] for d in range(3)], picks and picks["y"]).astype(BF)
        b["t"][2 + k] = combine(b["qy"][k, :, x], [b["r3y"][k, d] for d in range(3)], picks and picks["x"]).astype(BF)

    other_zh = head_of(1 - zh, x, y, c)

    def gather1(a, s1, s2):
        along_x, along_y = [], []
        r1, r2 = a.at[s1, y, c, :, x], a.at[s2, y, c, :, x]
        for d in range(1, 4):
            x2, y2 = (x + d) % 4, (y + d) % 4
            along_y.append((r1, r1, head_of(zh, x, y2, c), m))
            along_x.append((r2, r2, head_of(zh, x2, y, c), m))
        return [(along_y, a.at[s1, 0:3, c, :, x]), (along_x, a.at[s2, y, c, :, 0:3])]

    def gather2(a, s1, s2):
        along_x, along_y = [], []
        r1, r2 = a.at[s1, :, c, :, x], a.at[s2, y, c]
        for d in range(1, 4):
            x2, y2 = (x + d) % 4, (y + d) % 4
            along_x.append((r1, r1, head_of(zh, x2, y, c), m))
            along_y.append((r2, r2, head_of(zh, x, y2, c), m))
        return [(along_x, a.at[s1, :, c, :, 0:3]), (along_y, a.at[s2, 0:3, c])]

    def gather3(a, part_of):
        ref = a.at[part_of, :, c]
        return [([(ref, ref, head_of(zh, x, y, 1 - c), m)], ref)]

    def trade(b):
        cps = []
        for d in range(1, 8):
            k = (j + d) % 8
            src = b["g"].at[pl.ds(pl.multiple_of(k * 8, 8), 8)]
            dst = b["r"].at[pl.ds(pl.multiple_of(j * 8, 8), 8)]
            cps.append((src, dst, 8 * g + k, m))
        mine = pl.ds(pl.multiple_of(j * 8, 8), 8)
        b["r"][mine, :] = b["g"][mine, :]
        return [(cps, b["r"].at[0:56])]

    lane = lax.broadcasted_iota(jnp.int32, (T, 128), 1)
    row = lax.broadcasted_iota(jnp.int32, (T, 128), 0)

    def unpack_weights(first, last):
        def one(i, _):
            k = i % 2
            s["wf"][k] = s["win"][pl.ds(pl.multiple_of(i * 512, 512), 512), :].astype(F32)
            at = pl.ds(pl.multiple_of(i * 256, 256), 256)
            s["wxz"][at, 0:128] = s["wf"][k, pl.ds(0, 256, stride=2), :].astype(BF)
            s["wxz"][at, 128:256] = s["wf"][k, pl.ds(1, 256, stride=2), :].astype(BF)
            return 0
        lax.fori_loop(first, last, one, 0)

    picks = dict(
        c=[o_c != c],
        x=[o_x == (x + 4 - d) % 4 for d in range(1, 4)],
        y=[o_y == (y + 4 - d) % 4 for d in range(1, 4)],
    )
    a_x, a_o = s["ax"], s["ao"]
    x1 = [go(stage1_copies(sx, k)) for k in range(2)]
    split_arr(c)
    tog = s["tog"]
    og = og_ref[...].astype(F32)
    for k in range(8):
        for q in range(4):
            tog["g"][k * 8 + q * 2:k * 8 + q * 2 + 2, :] = og[:, q * 1024 + k * 128:q * 1024 + k * 128 + 128]
    o1 = go(trade(tog))
    x2 = []
    for k in range(2):
        got(x1[k])
        stage1_merge(sx, k, picks)
        x2.append(go(stage2_copies(sx, k)))
    got(o1)
    for q in range(4):
        for tt in range(2):
            tog["v"][pl.ds(q * 16 + tt, 8, stride=2), :] = tog["r"][pl.ds(q * 2 + tt, 8, stride=8), :]
    a_o[0:4, y, c, zh, x] = tog["v"][...].reshape(4, 16, 128).astype(BF)
    cps = []
    for d in range(1, 4):
        m2 = (m + d) % 4
        cps.append((a_o.at[m2, y, c, zh, x], a_o.at[7 - d, y, c, zh, x], h, m2))
    oc = go([(cps, a_o.at[4:7, y, c, zh, x])])
    oz_ref = a_o.at[0:4, y, c, zh, x]
    oz = go([([(oz_ref, oz_ref, other_zh, m)], oz_ref)])
    loc[1].wait()
    unpack_weights(0, 3)
    x3 = []
    for k in range(2):
        got(x2[k])
        stage2_merge(sx, k, picks)
        x3.append(go(stage3_copies(sx, k)))
    got(oz)
    q01, q23 = slice(0, 2), slice(2, 4)
    og1 = go(gather1(a_o, q01, q23))
    unpack_weights(3, 6)
    x4 = []
    for k in range(2):
        got(x3[k])
        stage3_merge(sx, k, picks)
        x4.append(go([([(sx["t"].at[q], sx["r4"].at[q], other_zh, m) for q in (k, 2 + k)], sx["r4"].at[0:2])]))
    got(oc)
    ocz_ref = a_o.at[4:7, y, c, zh, x]
    ocz = go([([(ocz_ref, ocz_ref, other_zh, m)], ocz_ref)])
    got(og1)
    unpack_weights(6, 9)
    xg1, xg2, xg3 = [], [], []
    first = [slice(k, k + 1) for k in range(2)]
    second = [slice(2 + k, 3 + k) for k in range(2)]
    for k in range(2):
        got(x4[k])
        for q in (k, 2 + k):
            a_x[q, y, c, :, x] = combine(sx["t"][q], [sx["r4"][q]], [o_zh != zh])
        xg1.append(go(gather1(a_x, first[k], second[k])))
    cps = []
    for d in range(1, 4):
        m2 = (m + d) % 4
        cps.append((a_x.at[m2, y, c, :, x], a_x.at[7 - d, y, c, :, x], h, m2))
    xc = go([(cps, a_x.at[4:7, y, c, :, x])])
    k1, k2 = slice(4, 5), slice(5, 7)
    l1, l2 = slice(4, 6), slice(6, 7)
    unpack_weights(9, 12)
    for k in range(2):
        got(xg1[k])
        xg2.append(go(gather2(a_x, first[k], second[k])))
    got(ocz)
    cog1 = go(gather1(a_o, l1, l2))
    got(xc)
    cxg1 = go(gather1(a_x, k1, k2))
    unpack_weights(12, 16)
    mark = sids.used
    for k in range(2):
        got(xg2[k])
        xg3.append(go(gather3(a_x, first[k]) + gather3(a_x, second[k])))
    og2 = go(gather2(a_o, q01, q23))

    def assemble(a, dst, cc, q):
        def one(i, _):
            at = pl.ds(pl.multiple_of(q * 1024 + i * 256 + cc * 128, 128), 128)
            dst[:, at] = a[q, i, cc].reshape(128, 128)
            return 0
        lax.fori_loop(0, 4, one, 0, unroll=True)

    for q in range(4):
        assemble(a_x, s["x"], c, q)
    loc[2].wait()
    p2 = jnp.zeros((T, 128), F32)
    for k in range(2):
        got(xg3[k])
        for q in (k, 2 + k):
            assemble(a_x, s["x"], 1 - c, q)
            at = slice(q * 1024, (q + 1) * 1024)
            p2 = p2 + bdot(s["x"][:, at], s["w2"][:, at], NT)

    e1 = doc_ref[0, 0]
    e2 = e1 + doc_ref[0, 1]
    e3 = e2 + doc_ref[0, 2]
    e4 = e3 + doc_ref[0, 3]

    def doc_of(t):
        return sum((t >= e).astype(jnp.int32) for e in (e1, e2, e3, e4))

    doc_row = doc_of(row)
    same = [None] + [(row >= o) & (doc_of(row - o) == doc_row) for o in range(1, 4)]
    visible = (row >= lane) & (doc_row == doc_of(lane))

    def conv(v, taps):
        result = v * taps[3:4]
        for o in range(1, 4):
            result = result + jnp.where(same[o], pltpu.roll(v, o, 0), 0.0) * taps[3 - o:4 - o]
        return result

    def conv_back(d, taps):
        result = d * taps[3:4]
        for o in range(1, 4):
            result = result + pltpu.roll(jnp.where(same[o], d, 0.0), T - o, 0) * taps[3 - o:4 - o]
        return result

    flush(mark)

    taps_bc = s["cbc"][...]
    bc_pre = conv(p2, taps_bc)
    bc_sig = sigmoid(bc_pre)
    s["ss"][...] = jnp.transpose(bc_pre * bc_sig)[0:32].astype(BF)
    i_bc, r_bc = sids.take(1), rids.take(1)

    @pl.when(target != h)
    def _():
        copy(s["ss"], s["bc"].at[part], i_bc, r_bc, target, m).start()

    @pl.when(target == h)
    def _():
        pltpu.make_async_copy(s["ss"], s["bc"].at[part], rsem.at[r_bc]).start()

    wait_all(s["bc"].at[j], rsem.at[r_bc])
    peers_of = [8 * g + (j + d) % 8 for d in range(1, 8)]
    bcp = go([([(s["bc"].at[j], s["bc"].at[j], head, m) for head in peers_of], s["bc"].at[0:7])])


    pxz = bdot(s["x"][...], s["wxz"][...], NN)
    got(og2)
    og3 = go(gather3(a_o, slice(0, 4)))
    z = pxz[:, 128:256]
    taps_x = cx_ref[...]
    x_pre = conv(pxz[:, 0:128], taps_x)
    x_sig = sigmoid(x_pre)
    x_conv = x_pre * x_sig
    z_sig = sigmoid(z)
    z_silu = z * z_sig
    low = lane < 64
    tri = jnp.where(row >= lane, 1.0, 0.0)
    raws, rates, steps = [], [], []
    for e in range(2):
        raw = jnp.broadcast_to(p2[:, 32 + e:33 + e], (T, 128)) + dtb_ref[e]
        raws.append(raw)
        rates.append(-jnp.exp(jnp.full((T, 128), alog_ref[e], F32)))
        steps.append(jnp.maximum(raw, 0.0) + jnp.log1p(jnp.exp(-jnp.abs(raw))))
    step = jnp.where(low, steps[0], steps[1])
    cum = hdot(tri, jnp.where(low, steps[0] * rates[0], steps[1] * rates[1]), NN)
    decays = []
    for e in range(2):
        col = jnp.broadcast_to(cum[:, 64 * e:64 * e + 1], (T, 128))
        gap = col - jnp.transpose(col)
        decays.append(jnp.where(visible, jnp.exp(jnp.where(visible, gap, 0.0)), 0.0))
    scaled = x_conv * step
    skip = jnp.where(low, skip_ref[0], skip_ref[1])

    for q in range(4):
        assemble(a_o, s["o"], c, q)
    got(og3)
    for q in range(4):
        assemble(a_o, s["o"], 1 - c, q)
    loc[3].wait()
    weighted = bdot(s["o"][...], s["wout"][...], NT) * gain_ref[...]

    got(bcp)
    b_t = s["bc"][0:4].reshape(128, 128)
    c_t = s["bc"][4:8].reshape(128, 128)
    scores = bdot(c_t, b_t, TN)
    mixes = [scores * decays[0], scores * decays[1]]
    zero = jnp.zeros((T, 128), F32)
    scaled2 = jnp.concatenate([jnp.where(low, scaled, zero), jnp.where(low, zero, scaled)], axis=0)
    state = hdot(jnp.concatenate(mixes, axis=1), scaled2, NN) + skip * x_conv
    gated = state * z_silu
    squares = jnp.sum(gated * gated, axis=1, keepdims=True)
    inners = jnp.sum(weighted * gated, axis=1, keepdims=True)
    nmat = jnp.where(lane == 0, squares, jnp.where(lane == 1, inners, 0.0))
    s["norm"][j] = jnp.transpose(nmat)[0:8]
    cps = [(s["norm"].at[j], s["norm"].at[j], head, m) for head in peers_of]
    ncp = go([(cps, s["norm"].at[0:7])])
    got(cxg1)
    cxg2 = go(gather2(a_x, k1, k2))
    got(ncp)
    total = jnp.sum(s["norm"][...], axis=0)
    tcol = jnp.transpose(jnp.concatenate([total, jnp.zeros((120, 128), F32)], axis=0))
    inverse = jnp.broadcast_to(lax.rsqrt(tcol[:, 0:1] * (1.0 / WIDTH) + EPS), (T, 128))
    inner = jnp.broadcast_to(tcol[:, 1:2] * (1.0 / WIDTH), (T, 128))
    normed = (gated * inverse * gain_ref[...]).astype(BF)
    s["nm"][0] = normed
    d_gated = inverse * weighted - gated * (inverse * inverse * inverse * inner)

    d_state = d_gated * z_silu
    d_z = d_gated * state * (z_sig * (1.0 + z * (1.0 - z_sig)))
    s["dz"][0] = d_z.astype(BF)
    dy0, dy1 = jnp.where(low, d_state, zero), jnp.where(low, zero, d_state)
    d_mix = [hdot(dy0, scaled, NT), hdot(dy1, scaled, NT)]
    d_scores = d_mix[0] * decays[0] + d_mix[1] * decays[1]
    s["dbcs"][0:4] = hdot(c_t.astype(F32), d_scores, NN).reshape(4, 32, 128).astype(BF)
    s["dbcs"][4:8] = hdot(b_t.astype(F32), d_scores, NT).reshape(4, 32, 128).astype(BF)
    s["dbcr"][j] = s["dbcs"][j]
    cps = [(s["dbcs"].at[(j + d) % 8], s["dbcr"].at[j], 8 * g + (j + d) % 8, m) for d in range(1, 8)]
    dbc = go([(cps, s["dbcr"].at[0:7])])
    got(cog1)
    cog2 = go(gather2(a_o, l1, l2))

    def to_mb(ref):
        cps = [(ref.at[0], ref.at[4 - d], h, (m + d) % 4) for d in range(1, 4)]
        return go([(cps, ref.at[1:4])])

    n_mb = to_mb(s["nm"])
    z_mb = to_mb(s["dz"])

    slo, sig = s["slo"], s["sig"]

    def lo_half(cc):
        def one(i, _):
            at = pl.ds(pl.multiple_of(i * 256 + cc * 128, 128), 128)
            v = bdot(normed, s["wout"][:, at], NN)
            slo["p"][i // 4, i % 4, cc] = v.astype(BF).reshape(2, 4, 16, 128)
            return 0
        lax.fori_loop(0, 16, one, 0, unroll=8)

    lo_half(1 - c)
    lo1 = go(stage1_copies(slo, 0) + stage1_copies(slo, 1))
    got(cxg2)
    cxg3 = go(gather3(a_x, slice(4, 7)))
    got(dbc)
    s["dsum"][...] = jnp.sum(s["dbcr"][...].astype(F32), axis=0)
    i_d, r_d = sids.take(1), rids.take(1)

    @pl.when(source != h)
    def _():
        copy(s["dsum"], s["dgot"], i_d, r_d, source, m).start()

    @pl.when(source == h)
    def _():
        pltpu.make_async_copy(s["dsum"], s["dgot"], rsem.at[r_d]).start()

    lo_half(c)

    d_scaled = hdot(
        jnp.concatenate(mixes, axis=0), jnp.concatenate([dy0, dy1], axis=0), TN
    )
    d_xconv = skip * d_state + d_scaled * step
    d_x = conv_back(d_xconv * (x_sig * (1.0 + x_pre * (1.0 - x_sig))), taps_x)
    s["dx"][0] = d_x.astype(BF)
    x_mb = to_mb(s["dx"])
    through = d_scaled * x_conv
    d_raws = []
    for e in range(2):
        mine = low if e == 0 else lane >= 64
        gap_grad = d_mix[e] * mixes[e]
        d_cum = jnp.sum(gap_grad - jnp.transpose(gap_grad), axis=1, keepdims=True)
        back = hdot(tri, jnp.broadcast_to(d_cum, (T, 128)), TN)
        d_step = jnp.sum(jnp.where(mine, through, 0.0), axis=1, keepdims=True) + rates[e] * back
        d_raws.append(d_step * sigmoid(raws[e]))

    got(lo1)
    for k in range(2):
        stage1_merge(slo, k, None)
    lo2 = go(stage2_copies(slo, 0) + stage2_copies(slo, 1))

    wait_all(s["dgot"], rsem.at[r_d])
    got(cog2)
    cog3 = go(gather3(a_o, slice(4, 7)))
    d_act = jnp.transpose(
        jnp.concatenate([s["dgot"][...], jnp.zeros((96, 128), F32)], axis=0)
    )
    d_bc = conv_back(d_act * (bc_sig * (1.0 + bc_pre * (1.0 - bc_sig))), taps_bc)
    d2 = jnp.where(lane == 32, d_raws[0], jnp.where(lane == 33, d_raws[1], d_bc))
    d2_b = d2.astype(BF)
    s["d2"][0] = jnp.transpose(d2)[0:48].astype(BF)
    d2_mb = to_mb(s["d2"])

    d_proj = jnp.concatenate([s["dx"][0], s["dz"][0]], axis=1)

    def ig_half(cc, k):
        for q in (k, 2 + k):
            def one(i, _):
                at = pl.ds(pl.multiple_of(q * 1024 + i * 256 + cc * 128, 128), 128)
                v = bdot(d_proj, s["wxz"][at, :], NT) + bdot(d2_b, s["w2"][:, at], NN)
                sig["p"][q, i, cc] = v.astype(BF).reshape(2, 4, 16, 128)
                return 0
            lax.fori_loop(0, 4, one, 0, unroll=True)

    ig1, ig2, ig3, ig4 = [], [], [], []
    for k in range(2):
        ig_half(1 - c, k)
        ig1.append(go(stage1_copies(sig, k)))
    for k in range(2):
        ig_half(c, k)
    for k in range(2):
        got(ig1[k])
        stage1_merge(sig, k, None)
        ig2.append(go(stage2_copies(sig, k)))
    got(n_mb)
    got(cog3)
    nm_all = s["nm"][...].reshape(512, 128)

    def grad_out(i, _):
        yy, cc = i // 2, i % 2
        lhs = jnp.concatenate(
            [a_o[m, yy, cc].reshape(128, 128)] + [a_o[k, yy, cc].reshape(128, 128) for k in range(4, 7)], axis=0
        )
        s["gout"][pl.ds(pl.multiple_of(i * 128, 128), 128), :] = bdot(lhs, nm_all, TN).astype(BF)
        return 0

    lax.fori_loop(0, 8, grad_out, 0, unroll=4)
    leave = [
        pltpu.make_async_copy(s["gout"], go_out, lsem.at[4]),
        pltpu.make_async_copy(s["gin"], gin_out, lsem.at[5]),
    ]
    leave[0].start()

    def stage4(b, k):
        return [([(b["t"].at[q, 1 - zh], b["r4"].at[q], other_zh, m) for q in (k, 2 + k)], b["r4"].at[0:2])]

    def stage5(b, t):
        t["v"][...] = (b["t"][:, zh].astype(F32) + b["r4"][...].astype(F32)).reshape(64, 128)
        for q in range(4):
            for tt in range(2):
                t["g"][pl.ds(q * 2 + tt, 8, stride=8), :] = t["v"][pl.ds(q * 16 + tt, 8, stride=2), :]
        return go(trade(t))

    def finish(t, out):
        for k in range(8):
            for q in range(4):
                at = q * 1024 + k * 128
                out[:, at:at + 128] = t["r"][k * 8 + q * 2:k * 8 + q * 2 + 2, :].astype(BF)

    for k in range(2):
        got(ig2[k])
        stage2_merge(sig, k, None)
        ig3.append(go(stage3_copies(sig, k)))
    got(lo2)
    for k in range(2):
        stage2_merge(slo, k, None)
    lo3 = go(stage3_copies(slo, 0) + stage3_copies(slo, 1))
    got(x_mb)
    got(z_mb)
    got(d2_mb)
    got(cxg3)
    d_all = jnp.concatenate(
        [s["dx"][...].reshape(512, 128), s["dz"][...].reshape(512, 128)], axis=1
    )
    d2_all = jnp.concatenate([s["d2"][k] for k in range(4)], axis=1)

    def grad_in(i, _):
        yy, cc, k = i // 2, i % 2, i % 2
        lhs = jnp.concatenate(
            [a_x[m, yy, cc].reshape(128, 128)] + [a_x[k_, yy, cc].reshape(128, 128) for k_ in range(4, 7)], axis=0
        )
        r = bdot(lhs, d_all, TN)
        s["gf"][k, pl.ds(0, 128, stride=2), :] = r[:, 0:128]
        s["gf"][k, pl.ds(1, 128, stride=2), :] = r[:, 128:256]
        s["gin"][pl.ds(pl.multiple_of(i * 256, 256), 256), :] = s["gf"][k].astype(BF)
        small = bdot(d2_all, lhs, NN)
        at = pl.ds(pl.multiple_of(i * 128, 128), 128)
        gbc_out[:, at] = small[0:32].astype(BF)
        gdt_out[:, at] = small[32:34].astype(BF)
        return 0

    lax.fori_loop(0, 4, grad_in, 0)
    for k in range(2):
        got(ig3[k])
        stage3_merge(sig, k, None)
        ig4.append(go(stage4(sig, k)))
    got(lo3)
    for k in range(2):
        stage3_merge(slo, k, None)
    lo4 = go(stage4(slo, 0) + stage4(slo, 1))
    lax.fori_loop(4, 8, grad_in, 0)
    leave[1].start()
    for k in range(2):
        got(ig4[k])
    ig5 = stage5(sig, s["tig"])
    got(lo4)
    lo5 = stage5(slo, s["tlo"])
    got(ig5)
    finish(s["tig"], ig_out)
    got(lo5)
    finish(s["tlo"], lo_out)

    for cp in leave:
        cp.wait()
    for whole, i in sent:
        wait_all(whole, ssem.at[i])
    @pl.when(target != h)
    def _():
        wait_all(s["ss"], ssem.at[i_bc])

    @pl.when(source != h)
    def _():
        wait_all(s["dsum"], ssem.at[i_d])

    assert rids.used <= N_RECV and sids.used <= N_SEND, (rids.used, sids.used)


def place_kernel(*refs):
    for source, result in zip(refs[:6], refs[6:]):
        result[...] = source[...]


def per_device(
    arrivals, owners, doc_lengths, w_in, w_bc, w_dt, conv_x, conv_bc, dt_bias, a_log, skip_scale,
    norm_gain, w_out, out_grad,
):
    smem = pl.BlockSpec(memory_space=pltpu.SMEM)
    vmem = pl.BlockSpec(memory_space=pltpu.VMEM)
    hbm = pl.BlockSpec(memory_space=pl.ANY)
    sds = jax.ShapeDtypeStruct
    shapes = (
        sds((2, 4096), BF), sds((2, 4096), BF), sds((2048, 128), BF), sds((32, 1024), BF),
        sds((2, 1024), BF), sds((1024, 128), BF),
    )
    made = pl.pallas_call(
        mixer_kernel,
        out_shape=shapes,
        in_specs=[smem] * 5 + [vmem] * 5 + [hbm] * 4,
        out_specs=(vmem, vmem, hbm, vmem, vmem, hbm),
        scratch_shapes=[SCRATCH],
        compiler_params=pltpu.CompilerParams(
            collective_id=0, has_side_effects=True, vmem_limit_bytes=56 * 1024 * 1024
        ),
    )(
        owners, doc_lengths, dt_bias, a_log, skip_scale, conv_x, conv_bc,
        norm_gain.reshape(1, 128), w_dt, out_grad.reshape(2, 4096),
        arrivals.reshape(T, 4096), w_in.reshape(8192, 128), w_bc, w_out,
    )
    lo, ig, gin, gbc, gdt, gout = pl.pallas_call(
        place_kernel,
        out_shape=shapes,
        in_specs=[vmem] * 6,
        out_specs=(vmem,) * 6,
    )(*made)
    return (
        lo[None], ig[None], gin.reshape(1024, 2, 128), gbc.T, gdt.T, gout,
    )


def solution(mesh):
    return jax.shard_map(
        per_device,
        mesh=mesh,
        in_specs=(
            P("mb", "head", None, None),
            P("mb"),
            P("mb", None),
            P(None, None, "head"),
            P("head", None),
            P("head", None),
            P(None, "head"),
            P(None, "head"),
            P("head"),
            P("head"),
            P("head"),
            P("head"),
            P("head", None),
            P("mb", "head", None),
        ),
        out_specs=(
            P("mb", "head", None),
            P("mb", "head", None),
            P("mb", None, "head"),
            P("mb", "head"),
            P("mb", "head"),
            P("mb", "head"),
        ),
        check_vma=False,
    )
```
